32 devices in a mesh: section: 2 (over core), shard: 4 (over z), replica: 4 (over y, x).
Axes of the slice: x: 2, y: 2, z: 4, core: 2. Of those that a mesh axis runs over, the one named last changes fastest.
Arguments:
- boundary_in: bfloat16 [2, 2, 16, 577, 1024], P('section', None, ('shard', 'replica')), may hold values from -6 to 6
- counts: int32 [4, 2], replicated, may hold values from 2 to 4, as said below
- w_qkv: bfloat16 [2, 1024, 3, 1024], P('section', None, None, 'shard'), may hold values from -0.1875 to 0.1875
- b_qkv: bfloat16 [2, 2, 1024], P('section', None, 'shard'), may hold values from -1.5 to 1.5
- w_out: bfloat16 [2, 1024, 1024], P('section', 'shard'), may hold values from -0.75 to 0.75
- b_out: bfloat16 [2, 1024], P('section'), may hold values from -1.5 to 1.5
- w_up: bfloat16 [2, 1024, 4096], P('section', None, 'shard'), may hold values from -0.1875 to 0.1875
- b_up: bfloat16 [2, 4096], P('section', 'shard'), may hold values from -2.5 to 2.5
- w_down: bfloat16 [2, 4096, 1024], P('section', 'shard'), may hold values from -0.09375 to 0.09375
- b_down: bfloat16 [2, 1024], P('section'), may hold values from -1.5 to 1.5
- norm1_gain: bfloat16 [2, 1024], P('section'), may hold values from 0.5 to 1.5
- norm1_shift: bfloat16 [2, 1024], P('section'), may hold values from -1 to 1
- norm2_gain: bfloat16 [2, 1024], P('section'), may hold values from 0.5 to 1.5
- norm2_shift: bfloat16 [2, 1024], P('section'), may hold values from -1 to 1
Outputs:
- boundary_out: bfloat16 [2, 2, 16, 577, 1024], P('section', None, ('shard', 'replica'))
- grad_qkv: float32 [2, 1024, 3, 1024], P('section', 'replica', None, 'shard')
- grad_qkv_bias: float32 [2, 2, 1024], P('section', None, ('shard', 'replica'))
- grad_out: float32 [2, 1024, 1024], P('section', 'shard', 'replica')
- grad_out_bias: float32 [2, 1024], P('section', ('shard', 'replica'))
- grad_up: float32 [2, 1024, 4096], P('section', 'replica', 'shard')
- grad_up_bias: float32 [2, 4096], P('section', ('shard', 'replica'))
- grad_down: float32 [2, 4096, 1024], P('section', 'shard', 'replica')
- grad_down_bias: float32 [2, 1024], P('section', ('shard', 'replica'))
- grad_norm1_gain: float32 [2, 1024], P('section', ('shard', 'replica'))
- grad_norm1_shift: float32 [2, 1024], P('section', ('shard', 'replica'))
- grad_norm2_gain: float32 [2, 1024], P('section', ('shard', 'replica'))
- grad_norm2_shift: float32 [2, 1024], P('section', ('shard', 'replica'))
The draws below stay inside these ranges and needn't reach their ends.
Inputs may be any that keep to these rules, and one draw needn't show every extreme that they name: counts[r, m] is the number of live image slots, the first ones, of replica r in micro-batch m; the values 4 and 2 each occur.
All inputs are finite; a program needn't handle non-finite values.
Results may differ from the reference program's by a relative error of at most 0.02.
Values may be sent and summed in bfloat16 or wider, within the bound.
No kernel may reach another device: no remote copies, remote signals or barrier semaphores. Data moves between devices by JAX's collectives and lax.ppermute only.
A program may use at most 448 MiB of HBM per device.

```python
import jax
import jax.numpy as jnp
from jax import lax

D = 1024
HEADS = 16
HEAD = 64
FF = 4096
SEQ = 577
MICRO = 2
IMG_SH = 1
REPLICAS = 4
MB_IMG = 4
IMAGES = 16


def draw_counts(key, part):
    key = jax.random.fold_in(key, 11)
    fewest = max(MB_IMG // 2, 1)
    cell_count = REPLICAS * MICRO
    values = jax.random.randint(jax.random.fold_in(key, 1), (cell_count,), fewest, MB_IMG + 1)
    peak_spot = jax.random.randint(jax.random.fold_in(key, 2), (), 0, cell_count)
    values = values.at[peak_spot].set(MB_IMG)
    values = values.at[(peak_spot + 1) % cell_count].set(fewest)
    return values.reshape(REPLICAS, MICRO).astype(jnp.int32)


def steps_of(stream_key, dims, cuts, low, high):
    def one(axis_at, parts):
        heights = jax.random.uniform(jax.random.fold_in(jax.random.fold_in(stream_key, 6), axis_at), (parts,), jnp.float32, low / len(cuts), high / len(cuts))
        return jnp.repeat(jnp.exp(heights), dims[axis_at] // parts).reshape((-1,) + (1,) * (len(dims) - axis_at - 1))

    level = one(*cuts[0])
    for cut in cuts[1:]:
        level = level * one(*cut)
    return level


def scatter_about(stream_key, dims, width, most, shards=(), held_as=jnp.bfloat16):
    values = jax.random.normal(stream_key, dims, jnp.float32) * width
    if len(shards) > 0:
        values = steps_of(stream_key, dims, shards, -0.22, 0.18) * values
    return jnp.clip(values, min=-most, max=most).astype(held_as)


def setup_inputs(seed: int = 0) -> dict:
    splits = jax.random.split(jax.random.key(seed), 15)
    return {
        "boundary_in": scatter_about(splits[0], (2, MICRO, IMAGES, SEQ, D), 1.0, 6.0, ((0, 2), (2, 16))),
        "counts": draw_counts(jax.random.fold_in(splits[14], 71), 0),
        "w_qkv": scatter_about(splits[2], (2, D, 3, D), D ** -0.5, 0.1875, ((0, 2), (3, 4))),
        "b_qkv": scatter_about(splits[3], (2, 2, D), 0.3, 1.5, ((0, 2), (2, 4))),
        "w_out": scatter_about(splits[4], (2, D, D), (D // 16) ** -0.5, 0.75, ((0, 2), (1, 4))),
        "b_out": scatter_about(splits[5], (2, D), 0.3, 1.5, ((0, 2),)),
        "w_up": scatter_about(splits[6], (2, D, FF), D ** -0.5, 0.1875, ((0, 2), (2, 4))),
        "b_up": scatter_about(splits[7], (2, FF), 0.5, 2.5, ((0, 2), (1, 4))),
        "w_down": scatter_about(splits[8], (2, FF, D), FF ** -0.5, 0.09375, ((0, 2), (1, 4))),
        "b_down": scatter_about(splits[9], (2, D), 0.3, 1.5, ((0, 2),)),
        "norm1_gain": jnp.clip(1.0 + 0.1 * jax.random.normal(splits[10], (2, D), jnp.float32), 0.5, 1.5).astype(jnp.bfloat16),
        "norm1_shift": scatter_about(splits[11], (2, D), 0.2, 1.0, ((0, 2),)),
        "norm2_gain": jnp.clip(1.0 + 0.1 * jax.random.normal(splits[12], (2, D), jnp.float32), 0.5, 1.5).astype(jnp.bfloat16),
        "norm2_shift": scatter_about(splits[13], (2, D), 0.2, 1.0, ((0, 2),)),
    }


highest = lax.Precision.HIGHEST

@jax.custom_vjp
def low(v):
    return lax.optimization_barrier(v.astype(jnp.bfloat16)).astype(jnp.float32)

@jax.custom_vjp
def low_back(v):
    return v

def low_keep(v):
    return (low(v), None)

def low_pass(kept, grad):
    return (grad,)

def back_keep(v):
    return (v, None)

def back_low(kept, grad):
    return (low(grad),)
low.defvjp(low_keep, low_pass)
low_back.defvjp(back_keep, back_low)

def layer_norm(values, scales, shifts):
    center = values - lax.optimization_barrier(jnp.mean(values, axis=-1, keepdims=True))
    spread = lax.optimization_barrier(jnp.mean(center * center, axis=-1, keepdims=True))
    return center * lax.rsqrt(spread + 1e-06) * scales + shifts

def attend(triple):
    queries, keys_in, values = triple
    scores = low_back(jnp.einsum('qhe,khe->hqk', queries, keys_in, precision=highest) * HEAD ** (-0.5))
    highest_score = lax.optimization_barrier(jnp.max(scores, axis=-1, keepdims=True))
    weights = jnp.exp(scores - highest_score)
    chances = low(weights / lax.optimization_barrier(jnp.sum(weights, axis=-1, keepdims=True)))
    return jnp.einsum('hqk,khe->qhe', chances, values, precision=highest)

def layer(layer_in, params):
    w_qkv, b_qkv, w_out, b_out, w_up, b_up, w_down, b_down, gain_one, shift_one, gain_two, shift_two = params
    images = layer_in.shape[0]
    normed = low(layer_norm(layer_in, gain_one, shift_one))
    offsets = jnp.stack([b_qkv[0], jnp.zeros_like(b_qkv[0]), b_qkv[1]])
    mixed_rows = low_back(low(jnp.einsum('gsd,dtf->gstf', normed, w_qkv, precision=highest) + offsets))
    split_heads = mixed_rows.reshape(images, SEQ, 3, HEADS, HEAD)
    attended = lax.map(jax.checkpoint(attend), (split_heads[:, :, 0], split_heads[:, :, 1], split_heads[:, :, 2]))
    attended = low_back(low(attended.reshape(images, SEQ, D)))
    branch = low_back(jnp.einsum('gsf,fd->gsd', attended, w_out, precision=highest))
    middle = layer_in + branch + b_out
    normed_two = low(layer_norm(middle, gain_two, shift_two))
    hidden = low_back(jnp.einsum('gsd,df->gsf', normed_two, w_up, precision=highest) + b_up)
    active = low_back(low(jax.nn.gelu(hidden, approximate=False)))
    lowered = low_back(jnp.einsum('gsf,fd->gsd', active, w_down, precision=highest))
    return middle + lowered + b_down

def two_layers(images_in, first_params, second_params):
    handed = low_back(low(layer(images_in, first_params)))
    return layer(handed, second_params)

def reference(boundary_in, counts, w_qkv, b_qkv, w_out, b_out, w_up, b_up, w_down, b_down, norm1_gain, norm1_shift, norm2_gain, norm2_shift):
    params = tuple((tensor.astype(jnp.float32) for tensor in (w_qkv, b_qkv, w_out, b_out, w_up, b_up, w_down, b_down, norm1_gain, norm1_shift, norm2_gain, norm2_shift)))
    first_params = tuple((tensor[0] for tensor in params))
    second_params = tuple((tensor[1] for tensor in params))
    position = jnp.arange(IMAGES, dtype=jnp.int32)
    owner = position // IMG_SH % REPLICAS
    slot_ids = position // (IMG_SH * REPLICAS) * IMG_SH + position % IMG_SH
    live_flags = (slot_ids[None, :] < counts.T[:, owner]).astype(jnp.float32)
    per_block = 4
    block_count = MICRO * IMAGES // per_block
    inputs = boundary_in[0].astype(jnp.float32).reshape(block_count, per_block, SEQ, D)
    tangents = (boundary_in[1].astype(jnp.float32) * live_flags[:, :, None, None]).reshape(block_count, per_block, SEQ, D)
    zero_grads = jax.tree.map(jnp.zeros_like, (first_params, second_params))

    def step_block(carry, pair):
        images_in, tangent = pair
        result, pull = jax.vjp(two_layers, images_in, first_params, second_params)
        back_in, grad_first, grad_second = pull(tangent)
        carry = jax.tree.map(jnp.add, carry, (grad_first, grad_second))
        return (carry, (result, back_in))
    totals, outcome = lax.scan(step_block, zero_grads, (inputs, tangents))
    results = outcome[0].reshape(MICRO, IMAGES, SEQ, D) * live_flags[:, :, None, None]
    back_all = outcome[1].reshape(MICRO, IMAGES, SEQ, D)
    boundary_out = jnp.stack([back_all, results]).astype(jnp.bfloat16)
    grads = tuple((jnp.stack([upper_grad, lower_grad]) for upper_grad, lower_grad in zip(totals[0], totals[1])))
    return (boundary_out, grads[0], grads[1], grads[2], grads[3], grads[4], grads[5], grads[6], grads[7], grads[8], grads[9], grads[10], grads[11])
```

```python
import functools

import jax
import jax.numpy as jnp
from jax import lax
from jax.experimental import pallas as pl
from jax.experimental.pallas import tpu as pltpu
from jax.sharding import PartitionSpec as P

HEAD = 64
SEQ = 577
PAD = 592
CHUNK = 48
LOW = jnp.bfloat16
F32 = jnp.float32
ALL_AXES = ("section", "shard", "replica")
NT = (((1,), (1,)), ((), ()))
NN = (((1,), (0,)), ((), ()))
TN = (((0,), (0,)), ((), ()))


def reverse_bits(value, bits):
    flipped = 0
    for spot in range(bits):
        flipped |= ((value >> spot) & 1) << (bits - 1 - spot)
    return flipped


def product(left, right, dims):
    return lax.dot_general(left, right, dims, preferred_element_type=F32)


def row_loop(body):
    whole = PAD // CHUNK

    def step(index, carry):
        body(pl.multiple_of(index * CHUNK, 16), CHUNK)
        return carry

    lax.fori_loop(0, whole, step, 0)
    if PAD % CHUNK:
        body(whole * CHUNK, PAD % CHUNK)


def params(megabytes=48):
    return pltpu.CompilerParams(vmem_limit_bytes=megabytes * 2**20)


def normalized(values):
    center = values - jnp.mean(values, axis=-1, keepdims=True)
    spread = jnp.mean(center * center, axis=-1, keepdims=True)
    inverse = lax.rsqrt(spread + 1e-06)
    return center * inverse, inverse


class Layout:
    def __init__(self, mesh_shape, width):
        self.shards = mesh_shape["shard"]
        self.replicas = mesh_shape["replica"]
        self.bits = self.replicas.bit_length() - 1
        self.width = width
        self.block = width // self.replicas
        self.flip = [reverse_bits(b, self.bits) for b in range(self.replicas)]
        self.near = self.replicas // 2
        self.slots = 2 * self.shards

    def across_cores(self, value):
        return lax.ppermute(value, "section", [(0, 1), (1, 0)])

    def along_shard(self, value, slot):
        return lax.ppermute(value, "shard", [(i, i ^ slot) for i in range(self.shards)])

    def along_bit(self, value, bit):
        route = []
        for core in range(2):
            physical = bit if core == 0 else self.bits - 1 - bit
            for shard in range(self.shards):
                base = (core * self.shards + shard) * self.replicas
                for replica in range(self.replicas):
                    route.append((base + replica, base + (replica ^ (1 << physical))))
        return lax.ppermute(value, ALL_AXES, route)


def arrange_images(lay, mine, received, blocks, core, live):
    width, block = lay.width, lay.block

    def kernel(scalars, live_ref, mine_ref, other_ref, image_ref, cot_ref):
        here = mine_ref[0]
        there = other_ref[...]
        first = scalars[lay.replicas] == 0
        image = jnp.where(first, here, there)
        cot = jnp.where(first, there, here).astype(F32) * live_ref[0]
        image_ref[...] = jnp.zeros_like(image_ref)
        cot_ref[...] = jnp.zeros_like(cot_ref)
        image_ref[0:SEQ, :] = image
        cot_ref[0:SEQ, :] = cot.astype(LOW)

    scalars = jnp.concatenate([blocks, core[None]]).astype(jnp.int32)
    shape = jax.ShapeDtypeStruct((PAD, width), LOW)
    return pl.pallas_call(
        kernel,
        grid_spec=pltpu.PrefetchScalarGridSpec(
            num_scalar_prefetch=1,
            grid=(lay.replicas,),
            in_specs=[
                pl.BlockSpec(memory_space=pltpu.SMEM),
                pl.BlockSpec((1, SEQ, block), lambda b, s: (s[lay.replicas], 0, s[b])),
                pl.BlockSpec((SEQ, block), lambda b, s: (0, s[b])),
            ],
            out_specs=[pl.BlockSpec((PAD, block), lambda b, s: (0, b))] * 2,
        ),
        out_shape=[shape, shape],
        compiler_params=params(),
        name="arrange_images",
    )(scalars, live, mine, received)


def restore_image(lay, values, blocks, scale):
    def kernel(scalars, scale_ref, in_ref, out_ref):
        out_ref[...] = (in_ref[0:SEQ, :].astype(F32) * scale_ref[0]).astype(LOW)

    return pl.pallas_call(
        kernel,
        grid_spec=pltpu.PrefetchScalarGridSpec(
            num_scalar_prefetch=1,
            grid=(lay.replicas,),
            in_specs=[
                pl.BlockSpec(memory_space=pltpu.SMEM),
                pl.BlockSpec((PAD, lay.block), lambda b, s: (0, b)),
            ],
            out_specs=pl.BlockSpec((SEQ, lay.block), lambda b, s: (0, s[b])),
        ),
        out_shape=jax.ShapeDtypeStruct((SEQ, lay.width), LOW),
        compiler_params=params(),
        name="restore_image",
    )(blocks, scale, values)


def arrange_attention(lay, mine, received, scalars):
    rep, block = lay.replicas, lay.block
    part = mine[0].shape[-1]

    def kernel(s, qkv_mine, qkv_other, out_mine, out_other, first_ref, second_ref):
        first = s[rep + 2] == 0
        for t in range(3):
            here, there = qkv_mine[t, 0], qkv_other[t, 0]
            first_ref[0, 0, :, t * part : (t + 1) * part] = jnp.where(first, here, there)
            second_ref[0, 0, :, t * part : (t + 1) * part] = jnp.where(first, there, here)
        here, there = out_mine[...].T, out_other[...].T
        first_ref[0, 0, :, 3 * part :] = jnp.where(first, here, there)
        second_ref[0, 0, :, 3 * part :] = jnp.where(first, there, here)

    shape = jax.ShapeDtypeStruct((2, rep, block, 4 * part), LOW)
    qkv_spec = pl.BlockSpec((3, 1, block, part), lambda p, b, s: (0, s[rep + p], s[b], 0))
    out_spec = pl.BlockSpec((part, block), lambda p, b, s: (s[rep + p], s[b]))
    return pl.pallas_call(
        kernel,
        grid_spec=pltpu.PrefetchScalarGridSpec(
            num_scalar_prefetch=1,
            grid=(2, rep),
            in_specs=[qkv_spec, qkv_spec, out_spec, out_spec],
            out_specs=[pl.BlockSpec((1, 1, block, 4 * part), lambda p, b, s: (p, b, 0, 0))] * 2,
        ),
        out_shape=[shape, shape],
        compiler_params=params(),
        name="arrange_attention",
    )(scalars, mine[0], received[0], mine[1], received[1])


def arrange_dense(lay, mine, received, scalars):
    rep, block = lay.replicas, lay.block
    part = mine[0].shape[1] // 2

    def kernel(s, up_mine, up_other, down_mine, down_other, up_one, up_two, down_one, down_two):
        first = s[rep + 2] == 0
        here, there = up_mine[...], up_other[...]
        up_one[0, 0] = jnp.where(first, here, there)
        up_two[0, 0] = jnp.where(first, there, here)
        here, there = down_mine[...].T, down_other[...].T
        down_one[0, 0] = jnp.where(first, here, there)
        down_two[0, 0] = jnp.where(first, there, here)

    shape = jax.ShapeDtypeStruct((2, rep, block, part), LOW)
    up_spec = pl.BlockSpec((block, part), lambda p, b, s: (s[b], s[rep + p]))
    down_spec = pl.BlockSpec((part, block), lambda p, b, s: (s[rep + p], s[b]))
    return pl.pallas_call(
        kernel,
        grid_spec=pltpu.PrefetchScalarGridSpec(
            num_scalar_prefetch=1,
            grid=(2, rep),
            in_specs=[up_spec, up_spec, down_spec, down_spec],
            out_specs=[pl.BlockSpec((1, 1, block, part), lambda p, b, s: (p, b, 0, 0))] * 4,
        ),
        out_shape=[shape] * 4,
        compiler_params=params(),
        name="arrange_dense",
    )(scalars, mine[0], received[0], mine[1], received[1])


def gather_weights(lay, own):
    piece = own[0, 0]
    near = jnp.stack([lay.along_shard(piece, k) for k in range(1, lay.shards)])[None]
    for bit in range(lay.bits - 1):
        near = jnp.concatenate([near, lay.along_bit(near, bit)], axis=0)
    far = lay.along_bit(near, lay.bits - 1)
    return (own, near, far, lay.across_cores(near), lay.across_cores(far))


def weight_specs(lay, weights):
    shards, half = lay.shards, lay.near
    rows, columns = weights[0].shape[2:]
    own = pl.BlockSpec((1, lay.replicas, rows, columns), lambda i: (i // shards, 0, 0, 0))
    mine = pl.BlockSpec(
        (half, 1, rows, columns), lambda i: (0, jnp.clip(i - 1, 0, shards - 2), 0, 0)
    )
    other = pl.BlockSpec(
        (half, 1, rows, columns), lambda i: (0, jnp.clip(i - shards - 1, 0, shards - 2), 0, 0)
    )
    return [own, mine, mine, other, other]


def each_case(lay, refs, body):
    own, near, far, near_other, far_other = refs
    shards, half = lay.shards, lay.near
    step = pl.program_id(0)

    def own_block(b):
        return own[0, b]

    def my_block(b):
        return near[b, 0] if b < half else far[b - half, 0]

    def other_block(b):
        b = lay.flip[b]
        return near_other[b, 0] if b < half else far_other[b - half, 0]

    at_own = (step == 0) | (step == shards)
    pl.when(at_own)(lambda: body(own_block))
    pl.when(jnp.logical_not(at_own) & (step < shards))(lambda: body(my_block))
    pl.when(step > shards)(lambda: body(other_block))


def widen(lay, x, weights, columns, mode, vectors=(), extra=()):
    low, high = columns
    size = high - low
    slots, block, width = lay.slots, lay.block, lay.width
    whole = pl.BlockSpec((PAD, width), lambda i: (0, 0))
    row = pl.BlockSpec((1, width), lambda i: (0, 0))
    per_slot = pl.BlockSpec((1, PAD, size), lambda i: (i, 0, 0))
    slot_row = pl.BlockSpec((1, 1, size), lambda i: (i, 0, 0))
    out_slots = jax.ShapeDtypeStruct((slots, PAD, size), LOW)
    out_rows = jax.ShapeDtypeStruct((slots, 1, size), F32)
    scratch = []
    if mode == "qkv":
        ins = [row, row, slot_row]
        outs, out_shape = [whole, per_slot], [jax.ShapeDtypeStruct((PAD, width), LOW), out_slots]
    elif mode == "up":
        ins = [slot_row]
        outs, out_shape = [per_slot, per_slot], [out_slots, out_slots]
    elif mode == "active":
        ins = [per_slot]
        outs = [per_slot, slot_row, row]
        out_shape = [out_slots, out_rows, jax.ShapeDtypeStruct((1, width), F32)]
    else:
        ins = []
        outs, out_shape = [per_slot], [out_slots]

    def kernel(*refs):
        x_ref = refs[0]
        weight_refs = refs[1:6]
        in_refs = refs[6 : 6 + len(ins)]
        out_refs = refs[6 + len(ins) :]
        source = x_ref
        if mode == "qkv":
            source = out_refs[0]

            @pl.when(pl.program_id(0) == 0)
            def _():
                def norm_rows(start, count):
                    values, _ = normalized(x_ref[pl.ds(start, count), :].astype(F32))
                    source[pl.ds(start, count), :] = (
                        values * in_refs[0][...] + in_refs[1][...]
                    ).astype(LOW)

                row_loop(norm_rows)

        if mode == "active":

            @pl.when(pl.program_id(0) == 0)
            def _():
                out_refs[2][...] = jnp.sum(x_ref[...].astype(F32), axis=0, keepdims=True)

        def body(pick):
            total = None
            for b in range(lay.replicas):
                term = product(
                    source[:, b * block : (b + 1) * block], pick(b)[:, low:high], NN
                )
                total = term if total is None else total + term
            if mode == "qkv":
                out_refs[1][0] = (total + in_refs[2][0]).astype(LOW)
            elif mode == "up":
                hidden = total + in_refs[0][0]
                chance = 0.5 + 0.5 * lax.erf(hidden * (0.5**0.5))
                density = jnp.exp(-0.5 * hidden * hidden) * 0.3989422804014327
                out_refs[0][0] = (hidden * chance).astype(LOW)
                out_refs[1][0] = (chance + hidden * density).astype(LOW)
            elif mode == "active":
                grad = total.astype(LOW).astype(F32) * in_refs[0][0].astype(F32)
                grad = grad.astype(LOW)
                out_refs[0][0] = grad
                out_refs[1][0] = jnp.sum(grad.astype(F32), axis=0, keepdims=True)
            else:
                out_refs[0][0] = total.astype(LOW)

        each_case(lay, weight_refs, body)

    return pl.pallas_call(
        kernel,
        grid=(slots,),
        in_specs=[whole] + weight_specs(lay, weights) + ins,
        out_specs=outs,
        out_shape=out_shape,
        scratch_shapes=scratch,
        compiler_params=params(),
        cost_estimate=pl.CostEstimate(
            flops=2 * PAD * width * size * slots,
            bytes_accessed=2 * width * size * slots + 4 * PAD * size * slots,
            transcendentals=0,
        ),
        name="widen_" + mode,
    )(x, *weights, *vectors, *extra)


def narrow(lay, acts, weights, columns, mode, rows_in, vectors):
    low, high = columns
    slots, block, width = lay.slots, lay.block, lay.width
    size = acts.shape[2]
    whole = pl.BlockSpec((PAD, width), lambda i: (0, 0))
    row = pl.BlockSpec((1, width), lambda i: (0, 0))
    full_low = jax.ShapeDtypeStruct((PAD, width), LOW)
    full_wide = jax.ShapeDtypeStruct((PAD, width), F32)
    one_row = jax.ShapeDtypeStruct((1, width), F32)
    if mode == "out":
        out_shape = [full_wide, full_low]
    elif mode == "down":
        out_shape = [full_low]
    elif mode == "back_two":
        out_shape = [full_wide, full_low, one_row, one_row, one_row]
    else:
        out_shape = [full_low, one_row, one_row]
    outs = [row if shape.shape[0] == 1 else whole for shape in out_shape]
    count_rows, count_vectors = len(rows_in), len(vectors)

    def kernel(*refs):
        act_ref = refs[0]
        weight_refs = refs[1:6]
        row_refs = refs[6 : 6 + count_rows]
        vector_refs = refs[6 + count_rows : 6 + count_rows + count_vectors]
        out_refs = refs[6 + count_rows + count_vectors : -1]
        total_ref = refs[-1]
        step = pl.program_id(0)

        @pl.when(step == 0)
        def _():
            total_ref[...] = jnp.zeros_like(total_ref)

        def body(pick):
            for b in range(lay.replicas):
                total_ref[:, b * block : (b + 1) * block] += product(
                    act_ref[0], pick(b)[:, low:high], NT
                )

        each_case(lay, weight_refs, body)

        @pl.when(step == slots - 1)
        def _():
            if mode.startswith("back"):
                for ref in out_refs:
                    if ref.shape[0] == 1:
                        ref[...] = jnp.zeros_like(ref)

            def finish(start, count):
                rows = pl.ds(start, count)
                total = total_ref[rows, :]
                if mode == "out":
                    middle = row_refs[0][rows, :].astype(F32) + total + vector_refs[0][...]
                    out_refs[0][rows, :] = middle
                    values, _ = normalized(middle)
                    out_refs[1][rows, :] = (
                        values * vector_refs[1][...] + vector_refs[2][...]
                    ).astype(LOW)
                elif mode == "down":
                    out_refs[0][rows, :] = (
                        row_refs[0][rows, :] + total + vector_refs[0][...]
                    ).astype(LOW)
                else:
                    values, inverse = normalized(row_refs[0][rows, :].astype(F32))
                    slope = total * vector_refs[0][...]
                    mean = jnp.mean(slope, axis=-1, keepdims=True)
                    along = jnp.mean(slope * values, axis=-1, keepdims=True)
                    grad = row_refs[1][rows, :].astype(F32) + inverse * (
                        slope - mean - values * along
                    )
                    gains = jnp.sum(total * values, axis=0, keepdims=True)
                    shifts = jnp.sum(total, axis=0, keepdims=True)
                    if mode == "back_two":
                        out_refs[0][rows, :] = grad
                        out_refs[1][rows, :] = grad.astype(LOW)
                        out_refs[2][...] += gains
                        out_refs[3][...] += shifts
                        out_refs[4][...] += jnp.sum(grad, axis=0, keepdims=True)
                    else:
                        out_refs[0][rows, :] = grad.astype(LOW)
                        out_refs[1][...] += gains
                        out_refs[2][...] += shifts

            row_loop(finish)

    return pl.pallas_call(
        kernel,
        grid=(slots,),
        in_specs=[pl.BlockSpec((1, PAD, size), lambda i: (i, 0, 0))]
        + weight_specs(lay, weights)
        + [whole] * count_rows
        + [row] * count_vectors,
        out_specs=outs,
        out_shape=out_shape,
        scratch_shapes=[pltpu.VMEM((PAD, width), F32)],
        compiler_params=params(),
        cost_estimate=pl.CostEstimate(
            flops=2 * PAD * width * size * slots,
            bytes_accessed=2 * width * size * slots + 2 * PAD * size * slots,
            transcendentals=0,
        ),
        name="narrow_" + mode,
    )(acts, *weights, *rows_in, *vectors)


def weight_grads(lay, far, pairs):
    half, block, shards, width = lay.near, lay.block, lay.shards, lay.width
    positions = range(half, 2 * half) if far else range(half)
    sizes = [pair[2].shape[2] for pair in pairs]
    total = sum(sizes)
    whole = pl.BlockSpec((PAD, width), lambda k: (0, 0))
    specs, operands, scratch = [], [], []
    for x, x_other, feats, feats_other in pairs:
        feature_spec = pl.BlockSpec((1, PAD, feats.shape[2]), lambda k: (k, 0, 0))
        specs += [whole, whole, feature_spec, feature_spec]
        operands += [x, x_other, feats, feats_other]
        scratch += [pltpu.VMEM((half * block, PAD), LOW)] * 2

    def kernel(*refs):
        out_ref = refs[4 * len(pairs)]
        turned = refs[4 * len(pairs) + 1 :]

        @pl.when(pl.program_id(0) == 0)
        def _():
            for n in range(len(pairs)):
                for spot, b in enumerate(positions):
                    rows = slice(spot * block, (spot + 1) * block)
                    mine = slice(b * block, (b + 1) * block)
                    other = slice(lay.flip[b] * block, (lay.flip[b] + 1) * block)
                    turned[2 * n][rows, :] = refs[4 * n][:, mine].T
                    turned[2 * n + 1][rows, :] = refs[4 * n + 1][:, other].T

        start = 0
        for n, size in enumerate(sizes):
            grads = product(turned[2 * n][...], refs[4 * n + 2][0], NN) + product(
                turned[2 * n + 1][...], refs[4 * n + 3][0], NN
            )
            out_ref[:, 0, :, start : start + size] = grads.reshape(half, block, size).astype(LOW)
            start += size

    return pl.pallas_call(
        kernel,
        grid=(shards,),
        in_specs=specs,
        out_specs=pl.BlockSpec((half, 1, block, total), lambda k: (0, k, 0, 0)),
        out_shape=jax.ShapeDtypeStruct((half, shards, block, total), LOW),
        scratch_shapes=scratch,
        compiler_params=params(),
        cost_estimate=pl.CostEstimate(
            flops=4 * PAD * half * block * total * shards,
            bytes_accessed=2 * (half * block + 2 * PAD) * total * shards,
            transcendentals=0,
        ),
        name="weight_grads",
    )(*operands)


def attention_forward(lay, mixed):
    part = mixed.shape[2] // 3

    def kernel(mixed_ref, out_ref):
        block = mixed_ref[0]
        query, keys, values = block[:, :part], block[:, part : 2 * part], block[:, 2 * part :]
        lanes = lax.broadcasted_iota(jnp.int32, (1, part), 1) // HEAD
        valid = lax.broadcasted_iota(jnp.int32, (1, PAD), 1) < SEQ
        result = None
        for head in range(part // HEAD):
            chosen = query if part == HEAD else jnp.where(lanes == head, query, 0)
            scores = product(chosen * HEAD ** (-0.5), keys, NT)
            scores = jnp.where(valid, scores, -1e30)
            weights = jnp.exp(scores - jnp.max(scores, axis=-1, keepdims=True))
            chances = (weights * (1.0 / jnp.sum(weights, axis=-1, keepdims=True))).astype(LOW)
            term = product(chances, values, NN)
            result = term if result is None else jnp.where(lanes == head, term, result)
        out_ref[0] = result.astype(LOW)

    return pl.pallas_call(
        kernel,
        grid=(lay.slots,),
        in_specs=[pl.BlockSpec((1, PAD, 3 * part), lambda i: (i, 0, 0))],
        out_specs=pl.BlockSpec((1, PAD, part), lambda i: (i, 0, 0)),
        out_shape=jax.ShapeDtypeStruct((lay.slots, PAD, part), LOW),
        compiler_params=params(),
        cost_estimate=pl.CostEstimate(
            flops=4 * PAD * PAD * 256 * lay.slots * part // HEAD,
            bytes_accessed=8 * PAD * part * lay.slots,
            transcendentals=PAD * PAD * lay.slots * part // HEAD,
        ),
        name="attention_forward",
    )(mixed)


def attention_backward(lay, mixed, upstream):
    part = mixed.shape[2] // 3

    def kernel(mixed_ref, up_ref, out_ref, sum_ref):
        block = mixed_ref[0]
        query, keys, values = block[:, :part], block[:, part : 2 * part], block[:, 2 * part :]
        grads = up_ref[0]
        lanes = lax.broadcasted_iota(jnp.int32, (1, part), 1) // HEAD
        valid = lax.broadcasted_iota(jnp.int32, (PAD, 1), 0) < SEQ
        query = query * HEAD ** (-0.5)
        results = None
        for head in range(part // HEAD):
            pick = (lambda v: v) if part == HEAD else (lambda v: jnp.where(lanes == head, v, 0))
            scores = product(keys, pick(query), NT)
            scores = jnp.where(valid, scores, -1e30)
            weights = jnp.exp(scores - jnp.max(scores, axis=0, keepdims=True))
            chances = weights * (1.0 / jnp.sum(weights, axis=0, keepdims=True))
            slopes = product(values, pick(grads), NT)
            inner = jnp.sum(chances * slopes, axis=0, keepdims=True)
            grad_scores = (chances * (slopes - inner)).astype(LOW)
            terms = (
                product(grad_scores, keys, TN) * HEAD ** (-0.5),
                product(grad_scores, query, NN),
                product(chances.astype(LOW), grads, NN),
            )
            if results is None:
                results = terms
            else:
                results = [jnp.where(lanes == head, t, o) for t, o in zip(terms, results)]
        for spot, term in enumerate(results):
            rounded = term.astype(LOW)
            out_ref[0, :, spot * part : (spot + 1) * part] = rounded
            sum_ref[0, :, spot * part : (spot + 1) * part] = jnp.sum(
                rounded.astype(F32), axis=0, keepdims=True
            )

    wide = pl.BlockSpec((1, PAD, 3 * part), lambda i: (i, 0, 0))
    return pl.pallas_call(
        kernel,
        grid=(lay.slots,),
        in_specs=[wide, pl.BlockSpec((1, PAD, part), lambda i: (i, 0, 0))],
        out_specs=[wide, pl.BlockSpec((1, 1, 3 * part), lambda i: (i, 0, 0))],
        out_shape=[
            jax.ShapeDtypeStruct((lay.slots, PAD, 3 * part), LOW),
            jax.ShapeDtypeStruct((lay.slots, 1, 3 * part), F32),
        ],
        compiler_params=params(),
        cost_estimate=pl.CostEstimate(
            flops=10 * PAD * PAD * 256 * lay.slots * part // HEAD,
            bytes_accessed=14 * PAD * part * lay.slots,
            transcendentals=PAD * PAD * lay.slots * part // HEAD,
        ),
        name="attention_backward",
    )(mixed, upstream)


def add_low(one, two):
    return (one.astype(F32) + two.astype(F32)).astype(LOW)


def sum_replicas(lay, far, near):
    near = add_low(near, lay.along_bit(far, lay.bits - 1))
    for bit in range(lay.bits - 2, -1, -1):
        split = near.shape[0] // 2
        near = add_low(near[:split], lay.along_bit(near[split:], bit))
    return near[0]


def sum_shards(lay, terms):
    total = terms[0].astype(F32)
    for slot in range(1, lay.shards):
        total = total + lay.along_shard(terms[slot], slot).astype(F32)
    return total


def shards(
    boundary_in,
    counts,
    w_qkv,
    b_qkv,
    w_out,
    b_out,
    w_up,
    b_up,
    w_down,
    b_down,
    norm1_gain,
    norm1_shift,
    norm2_gain,
    norm2_shift,
):
    width = boundary_in.shape[4]
    sizes = {axis: lax.axis_size(axis) for axis in ALL_AXES}
    lay = Layout(sizes, width)
    core = lax.axis_index("section").astype(jnp.int32)
    shard = lax.axis_index("shard").astype(jnp.int32)
    replica = lax.axis_index("replica").astype(jnp.int32)
    on_first = core == 0
    heads_wide = w_qkv.shape[3]
    part = heads_wide // 2
    ff_part = w_up.shape[2] // 2
    positions = jnp.arange(lay.replicas, dtype=jnp.int32)
    flips = jnp.asarray(lay.flip, jnp.int32)
    blocks = jnp.where(on_first, positions, flips) ^ replica
    inverse_blocks = jnp.where(on_first, positions ^ replica, flips[positions ^ replica])
    halves = jnp.arange(2, dtype=jnp.int32) ^ core
    scalars = jnp.concatenate([blocks, halves, core[None]])

    pictures = boundary_in[0, :, 0]
    received = lay.across_cores(lax.dynamic_index_in_dim(pictures, 1 - core, 0, False))
    live = (shard < counts[replica, core]).astype(F32)[None]
    image, cot = arrange_images(lay, pictures, received, blocks, core, live)

    raw_qkv = w_qkv[0].reshape(width, 3, 2, part).transpose(1, 2, 0, 3)
    own_attention = arrange_attention(
        lay,
        (raw_qkv, w_out[0]),
        (lay.across_cores(raw_qkv), lay.across_cores(w_out[0])),
        scalars,
    )
    up_one, up_two, down_one, down_two = arrange_dense(
        lay,
        (w_up[0], w_down[0]),
        (lay.across_cores(w_up[0]), lay.across_cores(w_down[0])),
        scalars,
    )
    own = ((own_attention[0], up_one, down_one), (own_attention[1], up_two, down_two))

    packed = jnp.concatenate(
        [v[0] for v in (b_out, b_down, norm1_gain, norm1_shift, norm2_gain, norm2_shift)]
        + [b_qkv.reshape(-1), b_up.reshape(-1)]
    )
    packed_other = lay.across_cores(packed)
    both = jnp.stack(
        [jnp.where(on_first, packed, packed_other), jnp.where(on_first, packed_other, packed)]
    )
    wide = both[:, : 6 * width].reshape(2, 6, lay.replicas, lay.block)
    wide = jnp.take(wide, blocks, axis=2).reshape(2, 6, 1, width).astype(F32)
    split = both[:, 6 * width :]
    split = jnp.stack([split] + [lay.along_shard(split, k) for k in range(1, lay.shards)])
    split_qkv = split[:, :, : 4 * part].reshape(lay.shards, 2, 2, 2, part)
    split_qkv = jnp.take(split_qkv, halves, axis=3).transpose(1, 3, 0, 2, 4)
    split_qkv = split_qkv.reshape(2, lay.slots, 2, part)
    bias_qkv = jnp.concatenate(
        [split_qkv[:, :, 0], jnp.zeros_like(split_qkv[:, :, 0]), split_qkv[:, :, 1]], axis=-1
    ).reshape(2, lay.slots, 1, 3 * part).astype(F32)
    bias_up = split[:, :, 4 * part :].reshape(lay.shards, 2, 2, ff_part)
    bias_up = jnp.take(bias_up, halves, axis=2).transpose(1, 2, 0, 3)
    bias_up = bias_up.reshape(2, lay.slots, 1, ff_part).astype(F32)

    weights = [tuple(gather_weights(lay, piece) for piece in layer) for layer in own]
    qkv_columns = (0, 3 * part)
    out_columns = (3 * part, 4 * part)
    ff_columns = (0, ff_part)

    kept = []
    entry = image
    for layer in range(2):
        w_attention, w_wide, w_narrow = weights[layer]
        vec_out, vec_down, gain_one, shift_one, gain_two, shift_two = wide[layer]
        normed, mixed = widen(
            lay,
            entry,
            w_attention,
            qkv_columns,
            "qkv",
            (gain_one, shift_one, bias_qkv[layer]),
        )
        attended = attention_forward(lay, mixed)
        middle, normed_two = narrow(
            lay, attended, w_attention, out_columns, "out", (entry,), (vec_out, gain_two, shift_two)
        )
        active, slope = widen(lay, normed_two, w_wide, ff_columns, "up", (bias_up[layer],))
        (result,) = narrow(lay, active, w_narrow, ff_columns, "down", (middle,), (vec_down,))
        kept.append((entry, normed, mixed, attended, middle, normed_two, active, slope))
        entry = result

    grads = []
    tangent = cot
    for layer in (1, 0):
        w_attention, w_wide, w_narrow = weights[layer]
        vec_out, vec_down, gain_one, shift_one, gain_two, shift_two = wide[layer]
        entry_in, normed, mixed, attended, middle, normed_two, active, slope = kept[layer]

        def pair(x, features):
            return (x, lay.across_cores(x), features, lay.across_cores(features[lay.shards :]))

        def reduced(*pairs):
            far = weight_grads(lay, True, pairs)
            near = weight_grads(lay, False, pairs)
            return sum_shards(lay, sum_replicas(lay, far, near))

        grad_down = reduced(pair(tangent, active))
        grad_hidden, up_sums, down_sums = widen(
            lay, tangent, w_narrow, ff_columns, "active", (), (slope,)
        )
        grad_up = reduced(pair(normed_two, grad_hidden))
        grad_middle, grad_branch, gain_two_sum, shift_two_sum, out_sums = narrow(
            lay, grad_hidden, w_wide, ff_columns, "back_two", (middle, tangent), (gain_two,)
        )
        (grad_attended,) = widen(lay, grad_branch, w_attention, out_columns, "plain")
        grad_mixed, qkv_sums = attention_backward(lay, mixed, grad_attended)
        grad_attention = reduced(pair(normed, grad_mixed), pair(grad_branch, attended))
        grad_entry, gain_one_sum, shift_one_sum = narrow(
            lay, grad_mixed, w_attention, qkv_columns, "back_one", (entry_in, grad_middle), (gain_one,)
        )
        model_sums = jnp.concatenate(
            [out_sums, down_sums, gain_one_sum, shift_one_sum, gain_two_sum, shift_two_sum]
        )
        grads.append((grad_down, grad_up, grad_attention, model_sums, up_sums, qkv_sums))
        tangent = grad_entry
    grads = grads[::-1]

    def to_owner(first, second):
        keep = jnp.where(on_first, first, second)
        other = lay.across_cores(jnp.where(on_first, second, first))
        return jnp.where(on_first, keep, other), jnp.where(on_first, other, keep)

    down_halves = to_owner(grads[0][0], grads[1][0])
    up_halves = to_owner(grads[0][1], grads[1][1])
    attention_halves = to_owner(grads[0][2], grads[1][2])
    grad_w_down = jnp.concatenate(down_halves, axis=1).T[None]
    grad_w_up = jnp.concatenate(up_halves, axis=1)[None]
    grad_w_qkv = jnp.stack(
        [half[:, : 3 * part].reshape(-1, 3, part) for half in attention_halves], axis=2
    ).reshape(1, lay.block, 3, heads_wide)
    grad_w_out = jnp.concatenate([half[:, 3 * part :] for half in attention_halves], axis=1).T[None]

    slot_order = jnp.arange(lay.shards, dtype=jnp.int32) ^ shard
    packs = []
    for _, _, _, model_sums, up_sums, qkv_sums in grads:
        model = jnp.take(model_sums.reshape(6, lay.replicas, lay.block), inverse_blocks, axis=1)
        model = model.reshape(6, lay.shards, lay.replicas, -1).transpose(1, 2, 0, 3)
        ups = jnp.take(up_sums.reshape(2, lay.shards, ff_part), slot_order, axis=1)
        ups = jnp.take(ups, halves, axis=0).transpose(1, 0, 2)
        parts = jnp.take(qkv_sums.reshape(2, lay.shards, 3, part), slot_order, axis=1)
        parts = jnp.take(parts, halves, axis=0)
        parts = jnp.stack([parts[:, :, 0], parts[:, :, 2]]).transpose(2, 0, 1, 3)
        parts = parts.reshape(lay.shards, 2, lay.replicas, -1).transpose(0, 2, 1, 3)
        rows = lay.shards * lay.replicas
        packs.append(
            jnp.concatenate(
                [model.reshape(rows, -1), parts.reshape(rows, -1), ups.reshape(rows, -1)], axis=1
            )
        )
    vector_sums = lax.psum_scatter(
        jnp.stack(packs).reshape(2 * lay.shards * lay.replicas, -1),
        ALL_AXES,
        scatter_dimension=0,
        tiled=True,
    )[0]
    share = width // (lay.shards * lay.replicas)
    vectors = [vector_sums[i * share : (i + 1) * share][None] for i in range(6)]
    grad_b_qkv = vector_sums[6 * share : 8 * share].reshape(1, 2, share)
    grad_b_up = vector_sums[8 * share :][None]

    one = jnp.ones((1,), F32)
    back = restore_image(lay, tangent, blocks, one)
    ahead = restore_image(lay, entry, blocks, live)
    keep = jnp.where(on_first, back, ahead)
    other = lay.across_cores(jnp.where(on_first, ahead, back))
    boundary_out = jnp.stack([jnp.where(on_first, keep, other), jnp.where(on_first, other, keep)])
    boundary_out = boundary_out[None, :, None]
    return (
        boundary_out,
        grad_w_qkv,
        grad_b_qkv,
        grad_w_out,
        vectors[0],
        grad_w_up,
        grad_b_up,
        grad_w_down,
        vectors[1],
        vectors[2],
        vectors[3],
        vectors[4],
        vectors[5],
    )


def solution(mesh):
    spread = P("section", ("shard", "replica"))
    return jax.shard_map(
        shards,
        mesh=mesh,
        in_specs=(
            P("section", None, ("shard", "replica"), None, None),
            P(),
            P("section", None, None, "shard"),
            P("section", None, "shard"),
            P("section", "shard", None),
            P("section", None),
            P("section", None, "shard"),
            P("section", "shard"),
            P("section", "shard", None),
            P("section", None),
            P("section", None),
            P("section", None),
            P("section", None),
            P("section", None),
        ),
        out_specs=(
            P("section", None, ("shard", "replica"), None, None),
            P("section", "replica", None, "shard"),
            P("section", None, ("shard", "replica")),
            P("section", "shard", "replica"),
            spread,
            P("section", "replica", "shard"),
            spread,
            P("section", "shard", "replica"),
            spread,
            spread,
            spread,
            spread,
            spread,
        ),
        check_vma=False,
    )
```

```python
import functools

import jax
import jax.numpy as jnp
from jax import lax
from jax.experimental import pallas as pl
from jax.experimental.pallas import tpu as pltpu
from jax.sharding import PartitionSpec as P

HEAD = 64
SEQ = 577
PAD = 592
CHUNK = 144
LOW = jnp.bfloat16
F32 = jnp.float32
ALL_AXES = ("section", "shard", "replica")
NT = (((1,), (1,)), ((), ()))
NN = (((1,), (0,)), ((), ()))
TN = (((0,), (0,)), ((), ()))


def reverse_bits(value, bits):
    flipped = 0
    for spot in range(bits):
        flipped |= ((value >> spot) & 1) << (bits - 1 - spot)
    return flipped


def product(left, right, dims):
    return lax.dot_general(left, right, dims, preferred_element_type=F32)


def row_loop(body):
    whole = PAD // CHUNK

    def step(index, carry):
        body(pl.multiple_of(index * CHUNK, 16), CHUNK)
        return carry

    lax.fori_loop(0, whole, step, 0)
    if PAD % CHUNK:
        body(whole * CHUNK, PAD % CHUNK)


def params(megabytes=48):
    return pltpu.CompilerParams(vmem_limit_bytes=megabytes * 2**20)


def normalized(values):
    center = values - jnp.mean(values, axis=-1, keepdims=True)
    spread = jnp.mean(center * center, axis=-1, keepdims=True)
    inverse = lax.rsqrt(spread + 1e-06)
    return center * inverse, inverse


class Layout:
    def __init__(self, mesh_shape, width):
        self.shards = mesh_shape["shard"]
        self.replicas = mesh_shape["replica"]
        self.bits = self.replicas.bit_length() - 1
        self.width = width
        self.block = width // self.replicas
        self.flip = [reverse_bits(b, self.bits) for b in range(self.replicas)]
        self.near = self.replicas // 2
        self.slots = 2 * self.shards

    def across_cores(self, value):
        return lax.ppermute(value, "section", [(0, 1), (1, 0)])

    def along_shard(self, value, slot):
        return lax.ppermute(value, "shard", [(i, i ^ slot) for i in range(self.shards)])

    def along_bit_plain(self, value, bit):
        route = [(i, i ^ (1 << bit)) for i in range(self.replicas)]
        return lax.ppermute(value, "replica", route)

    def along_bit(self, value, bit):
        route = []
        for core in range(2):
            physical = bit if core == 0 else self.bits - 1 - bit
            for shard in range(self.shards):
                base = (core * self.shards + shard) * self.replicas
                for replica in range(self.replicas):
                    route.append((base + replica, base + (replica ^ (1 << physical))))
        return lax.ppermute(value, ALL_AXES, route)


def arrange_images(lay, mine, received, blocks, core, live):
    width, block = lay.width, lay.block

    def kernel(scalars, live_ref, mine_ref, other_ref, image_ref, cot_ref):
        here = mine_ref[0]
        there = other_ref[0]
        first = scalars[lay.replicas] == 0
        image = jnp.where(first, here, there)
        cot = jnp.where(first, there, here).astype(F32) * live_ref[0]
        image_ref[...] = jnp.zeros_like(image_ref)
        cot_ref[...] = jnp.zeros_like(cot_ref)
        image_ref[0:SEQ, :] = image
        cot_ref[0:SEQ, :] = cot.astype(LOW)

    scalars = jnp.concatenate([blocks, core[None]]).astype(jnp.int32)
    shape = jax.ShapeDtypeStruct((PAD, width), LOW)
    return pl.pallas_call(
        kernel,
        grid_spec=pltpu.PrefetchScalarGridSpec(
            num_scalar_prefetch=1,
            grid=(lay.replicas,),
            in_specs=[
                pl.BlockSpec(memory_space=pltpu.SMEM),
                pl.BlockSpec((1, SEQ, block), lambda b, s: (s[lay.replicas], 0, s[b])),
                pl.BlockSpec((1, SEQ, block), lambda b, s: (s[lay.replicas], 0, s[b])),
            ],
            out_specs=[pl.BlockSpec((PAD, block), lambda b, s: (0, b))] * 2,
        ),
        out_shape=[shape, shape],
        compiler_params=params(),
        name="arrange_images",
    )(scalars, live, mine, received)


def restore_image(lay, values, blocks, scale):
    def kernel(scalars, scale_ref, in_ref, out_ref):
        out_ref[...] = (in_ref[0:SEQ, :].astype(F32) * scale_ref[0]).astype(LOW)

    return pl.pallas_call(
        kernel,
        grid_spec=pltpu.PrefetchScalarGridSpec(
            num_scalar_prefetch=1,
            grid=(lay.replicas,),
            in_specs=[
                pl.BlockSpec(memory_space=pltpu.SMEM),
                pl.BlockSpec((PAD, lay.block), lambda b, s: (0, b)),
            ],
            out_specs=pl.BlockSpec((SEQ, lay.block), lambda b, s: (0, s[b])),
        ),
        out_shape=jax.ShapeDtypeStruct((SEQ, lay.width), LOW),
        compiler_params=params(),
        name="restore_image",
    )(blocks, scale, values)


def chosen_half(flag, low, high):
    return jnp.where(flag == 0, low, high)


def arrange_attention(lay, mine, received, scalars):
    rep, block = lay.replicas, lay.block
    part = mine[1].shape[0] // 2

    def kernel(s, qkv_mine, qkv_other, out_mine, out_other, first_ref, second_ref):
        first = s[rep + 2] == 0
        half = s[rep + pl.program_id(0)]

        def columns(ref, t):
            start = 2 * t * part
            return chosen_half(
                half, ref[:, start : start + part], ref[:, start + part : start + 2 * part]
            )

        for t in range(3):
            here, there = columns(qkv_mine, t), columns(qkv_other, t)
            first_ref[0, 0, :, t * part : (t + 1) * part] = jnp.where(first, here, there)
            second_ref[0, 0, :, t * part : (t + 1) * part] = jnp.where(first, there, here)
        here, there = out_mine[...].T, out_other[...].T
        first_ref[0, 0, :, 3 * part :] = jnp.where(first, here, there)
        second_ref[0, 0, :, 3 * part :] = jnp.where(first, there, here)

    shape = jax.ShapeDtypeStruct((2, rep, block, 4 * part), LOW)
    qkv_spec = pl.BlockSpec((block, 6 * part), lambda p, b, s: (s[b], 0))
    out_spec = pl.BlockSpec((part, block), lambda p, b, s: (s[rep + p], s[b]))
    return pl.pallas_call(
        kernel,
        grid_spec=pltpu.PrefetchScalarGridSpec(
            num_scalar_prefetch=1,
            grid=(2, rep),
            in_specs=[qkv_spec, qkv_spec, out_spec, out_spec],
            out_specs=[pl.BlockSpec((1, 1, block, 4 * part), lambda p, b, s: (p, b, 0, 0))] * 2,
        ),
        out_shape=[shape, shape],
        compiler_params=params(16),
        name="arrange_attention",
    )(scalars, mine[0], received[0], mine[1], received[1])


def arrange_dense(lay, mine, received, scalars):
    rep, block = lay.replicas, lay.block
    part = mine[0].shape[1] // 2

    def kernel(s, up_mine, up_other, down_mine, down_other, first_ref, second_ref):
        first = s[rep + 2] == 0
        here, there = up_mine[...], up_other[...]
        first_ref[0, 0, :, :part] = jnp.where(first, here, there)
        second_ref[0, 0, :, :part] = jnp.where(first, there, here)
        here, there = down_mine[...].T, down_other[...].T
        first_ref[0, 0, :, part:] = jnp.where(first, here, there)
        second_ref[0, 0, :, part:] = jnp.where(first, there, here)

    shape = jax.ShapeDtypeStruct((2, rep, block, 2 * part), LOW)
    up_spec = pl.BlockSpec((block, part), lambda p, b, s: (s[b], s[rep + p]))
    down_spec = pl.BlockSpec((part, block), lambda p, b, s: (s[rep + p], s[b]))
    return pl.pallas_call(
        kernel,
        grid_spec=pltpu.PrefetchScalarGridSpec(
            num_scalar_prefetch=1,
            grid=(2, rep),
            in_specs=[up_spec, up_spec, down_spec, down_spec],
            out_specs=[pl.BlockSpec((1, 1, block, 2 * part), lambda p, b, s: (p, b, 0, 0))] * 2,
        ),
        out_shape=[shape] * 2,
        compiler_params=params(),
        name="arrange_dense",
    )(scalars, mine[0], received[0], mine[1], received[1])


def first_pieces(lay, qkv, out, up, down, scalars):
    rep, block = lay.replicas, lay.block
    part, wide = out.shape[0] // 2, up.shape[1] // 2

    def kernel(s, qkv_ref, out_ref, up_ref, down_ref, *outs):
        core = s[rep + 2]
        for flag, attention_ref, dense_ref in ((core, *outs[:2]), (1 - core, *outs[2:])):
            for t in range(3):
                start = 2 * t * part
                attention_ref[:, t * part : (t + 1) * part] = chosen_half(
                    flag,
                    qkv_ref[:, start : start + part],
                    qkv_ref[:, start + part : start + 2 * part],
                )
            attention_ref[:, 3 * part :] = chosen_half(flag, out_ref[:part], out_ref[part:]).T
            dense_ref[:, :wide] = chosen_half(flag, up_ref[:, :wide], up_ref[:, wide:])
            dense_ref[:, wide:] = chosen_half(flag, down_ref[:wide], down_ref[wide:]).T

    attention_shape = jax.ShapeDtypeStruct((block, 4 * part), LOW)
    dense_shape = jax.ShapeDtypeStruct((block, 2 * wide), LOW)
    attention_spec = pl.BlockSpec((block, 4 * part), lambda i, s: (0, 0))
    dense_spec = pl.BlockSpec((block, 2 * wide), lambda i, s: (0, 0))
    return pl.pallas_call(
        kernel,
        grid_spec=pltpu.PrefetchScalarGridSpec(
            num_scalar_prefetch=1,
            grid=(1,),
            in_specs=[
                pl.BlockSpec((block, 6 * part), lambda i, s: (s[0], 0)),
                pl.BlockSpec((2 * part, block), lambda i, s: (0, s[0])),
                pl.BlockSpec((block, 2 * wide), lambda i, s: (s[0], 0)),
                pl.BlockSpec((2 * wide, block), lambda i, s: (0, s[0])),
            ],
            out_specs=[attention_spec, dense_spec] * 2,
        ),
        out_shape=[attention_shape, dense_shape] * 2,
        compiler_params=params(16),
        name="first_pieces",
    )(scalars, qkv, out, up, down)


def pick_slots(lay, gathered, slot_order):
    rows, columns = gathered.shape[1:]

    def kernel(_, in_ref, out_ref):
        out_ref[0] = in_ref[...]

    return pl.pallas_call(
        kernel,
        grid_spec=pltpu.PrefetchScalarGridSpec(
            num_scalar_prefetch=1,
            grid=(lay.shards - 1,),
            in_specs=[pl.BlockSpec((1, rows, columns), lambda k, s: (s[k + 1], 0, 0))],
            out_specs=pl.BlockSpec((1, 1, rows, columns), lambda k, s: (0, k, 0, 0)),
        ),
        out_shape=jax.ShapeDtypeStruct((1, lay.shards - 1, rows, columns), LOW),
        compiler_params=params(8),
        name="pick_slots",
    )(slot_order, gathered)


class Order:
    def __init__(self):
        self.token = None

    def tie(self, *values):
        if self.token is None:
            return values
        return lax.optimization_barrier((values, self.token))[0]

    def run(self, step, *values):
        results = step(*self.tie(*values))
        self.token = jax.tree.leaves(results)[0]
        return results

    def absorb(self, *values):
        values, self.token = lax.optimization_barrier((values, self.token))
        return values


class Gather:
    def __init__(self, lay, order, slot_order, pieces, own):
        self.lay, self.order, self.pieces, self.own = lay, order, pieces, own
        self.slot_order = slot_order
        self.state = [None] * len(pieces)
        self.done = [0] * len(pieces)

    def start(self, n):
        (piece,) = self.order.tie(self.pieces[n])
        self.state[n] = (lax.all_gather(piece, "shard"),)

    def step(self, n):
        lay = self.lay
        if self.done[n] == 0:
            near = self.order.run(lambda v: pick_slots(lay, v, self.slot_order), *self.state[n])
        else:
            near = self.order.run(lambda *both: jnp.concatenate(both, axis=0), *self.state[n])
        self.state[n] = (near, lay.along_bit(near, self.done[n]))
        self.done[n] += 1

    def finish(self, n):
        lay = self.lay
        while self.done[n] < lay.bits:
            self.step(n)
        near, far = self.state[n]
        near_other = lay.across_cores(near)
        (far,) = self.order.tie(far)
        return (self.own[n], near, far, near_other, lay.across_cores(far))


def fetch_weights(lay, refs, held, sems, slot):
    own, near, far, near_other, far_other = refs
    half = lay.near
    side, k = divmod(slot, lay.shards)

    def start(source, target):
        pltpu.make_async_copy(source, target, sems.at[slot]).start()

    if k == 0:
        start(own.at[side], held.at[slot])
    elif side == 0:
        start(near.at[:, k - 1], held.at[slot, 0:half])
        start(far.at[:, k - 1], held.at[slot, half : 2 * half])
    else:
        for b in range(half):
            start(near_other.at[b, k - 1], held.at[slot, lay.flip[b]])
            start(far_other.at[b, k - 1], held.at[slot, lay.flip[half + b]])


def await_weights(held, sems, slot):
    pltpu.make_async_copy(held.at[slot], held.at[slot], sems.at[slot]).wait()


def flat(block):
    return block.reshape(block.shape[0] * block.shape[1], block.shape[2])


def layer_call(lay, kernel, name, weights, slotted, whole, late, rows, outs, megabytes):
    slots, width = lay.slots, lay.width
    once = dict(pipeline_mode=pl.Buffered(1))

    def spec(shape, **mode):
        if len(shape) == 3:
            return pl.BlockSpec((1,) + shape[1:], lambda i: (i, 0, 0))
        return pl.BlockSpec(shape, lambda i: (0, 0), **mode)

    anywhere = pl.BlockSpec(memory_space=pltpu.HBM)
    counts = [5 * len(weights), len(slotted), len(whole), len(late), len(rows), len(outs)]

    def body(*refs):
        groups, at = [], 0
        for count in counts + [1, len(weights), len(weights), len(late)]:
            groups.append(refs[at : at + count])
            at += count
        arrays, slot_refs, whole_refs, late_refs, row_refs, out_refs = groups[:6]
        (total,), held, sems, late_held = groups[6:10]
        late_sem = refs[at] if late else None
        step = pl.program_id(0)

        def late_copy(n):
            return pltpu.make_async_copy(late_refs[n], late_held[n], late_sem.at[n])

        @pl.when(step == 0)
        def _():
            for slot in range(slots):
                for n in range(len(weights)):
                    fetch_weights(lay, arrays[5 * n : 5 * n + 5], held[n], sems[n], slot)
            for n in range(len(late)):
                late_copy(n).start()

        def weight(n):
            await_weights(held[n], sems[n], step)
            return flat(held[n][step])

        def late_values():
            for n in range(len(late)):
                late_copy(n).wait()
            return late_held

        kernel(step, weight, slot_refs, whole_refs, late_values, row_refs, out_refs, total)

    arrays = [array for matrix in weights for array in matrix]
    scratch = [pltpu.VMEM((PAD, width), F32)]
    scratch += [pltpu.VMEM((slots,) + matrix[0].shape[1:], LOW) for matrix in weights]
    scratch += [pltpu.SemaphoreType.DMA((slots,)) for _ in weights]
    scratch += [pltpu.VMEM(a.shape, a.dtype) for a in late]
    if late:
        scratch.append(pltpu.SemaphoreType.DMA((len(late),)))
    return pl.pallas_call(
        body,
        grid=(slots,),
        in_specs=[anywhere] * len(arrays)
        + [spec(a.shape) for a in slotted]
        + [spec(a.shape, **once) for a in whole]
        + [anywhere] * len(late)
        + [spec(a.shape, **once) for a in rows],
        out_specs=[spec(o.shape) for o in outs],
        out_shape=outs,
        scratch_shapes=scratch,
        compiler_params=params(megabytes),
        cost_estimate=pl.CostEstimate(flops=1000, bytes_accessed=2**20, transcendentals=0),
        name=name,
    )(*arrays, *slotted, *whole, *late, *rows)


def add_product(lay, step, total, acts, matrix):
    for b in range(lay.replicas):
        columns = slice(b * lay.block, (b + 1) * lay.block)
        term = product(acts, matrix[columns], NT)
        total[:, columns] = jnp.where(step == 0, 0.0, total[:, columns]) + term


def low_shape(*shape):
    return jax.ShapeDtypeStruct(shape, LOW)


def wide_shape(*shape):
    return jax.ShapeDtypeStruct(shape, F32)


def mask_keys(scores, low):
    edge = SEQ // 16 * 16
    valid = lax.broadcasted_iota(jnp.int32, (PAD - edge, 1), 0) < SEQ - edge
    return jnp.concatenate([scores[:edge], jnp.where(valid, scores[edge:], low)], axis=0)


def attend(block, part):
    query, keys, values = block[:, :part], block[:, part : 2 * part], block[:, 2 * part :]
    heads = range(part // HEAD)
    lanes = lax.broadcasted_iota(jnp.int32, (1, part), 1) // HEAD
    query = query * HEAD ** (-0.5)
    turned = values.T
    ones = jnp.ones((16, PAD), LOW)
    scores = [product(keys, jnp.where(lanes == h, query, 0), NT) for h in heads]
    scores = [mask_keys(score, -1e30) for score in scores]
    peaks = [jnp.max(score, axis=0, keepdims=True) for score in scores]
    weights = [jnp.exp(score - peak).astype(LOW) for score, peak in zip(scores, peaks)]
    sums = [
        product(jnp.concatenate([turned[h * HEAD : (h + 1) * HEAD], ones], axis=0), weights[h], NN)
        for h in heads
    ]
    result = jnp.concatenate([s[:HEAD] / s[HEAD : HEAD + 1] for s in sums], axis=0).T
    spot = lax.broadcasted_iota(jnp.int32, (8, 1), 0)
    logs = jnp.zeros((8, PAD), F32)
    for h in heads:
        logs = jnp.where(spot == h, peaks[h] + jnp.log(sums[h][HEAD : HEAD + 1]), logs)
    return result.astype(LOW), logs


def attend_back(block, grads, attended, logs, part):
    query, keys, values = block[:, :part], block[:, part : 2 * part], block[:, 2 * part :]
    heads = range(part // HEAD)
    lanes = lax.broadcasted_iota(jnp.int32, (1, part), 1) // HEAD
    wide = lax.broadcasted_iota(jnp.int32, (1, 128), 1)
    query = query * HEAD ** (-0.5)

    def pick(h, array):
        return jnp.where(lanes == h, array, 0)

    along = grads.astype(F32) * attended.astype(F32)
    inner = jnp.zeros((PAD, 128), F32)
    for h in heads:
        inner = jnp.where(wide == h, jnp.sum(pick(h, along), axis=-1, keepdims=True), inner)
    inner = inner.T
    scores = [product(keys, pick(h, query), NT) for h in heads]
    slopes = [product(values, pick(h, grads), NT) for h in heads]
    chances = [mask_keys(jnp.exp(scores[h] - logs[h : h + 1]), 0.0) for h in heads]
    grad_scores = [(chances[h] * (slopes[h] - inner[h : h + 1])).astype(LOW) for h in heads]
    low = [chance.astype(LOW) for chance in chances]
    value_terms = [product(low[h], grads, NN) for h in heads]
    key_terms = [product(grad_scores[h], query, NN) for h in heads]
    turned = keys.T
    query_terms = [
        product(turned[h * HEAD : (h + 1) * HEAD], grad_scores[h], NN) for h in heads
    ]

    def merge(terms):
        result = terms[0]
        for h in heads:
            result = jnp.where(lanes == h, terms[h], result)
        return result

    return (
        jnp.concatenate(query_terms, axis=0).T * HEAD ** (-0.5),
        merge(key_terms),
        merge(value_terms),
    )


def norm_back(values, grads, gain):
    values, inverse = normalized(values)
    slope = grads * gain
    mean = jnp.mean(slope, axis=-1, keepdims=True)
    along = jnp.mean(slope * values, axis=-1, keepdims=True)
    term = inverse * (slope - mean - values * along)
    return (
        term,
        jnp.sum(grads * values, axis=0, keepdims=True),
        jnp.sum(grads, axis=0, keepdims=True),
    )


def attention_forward(lay, entry, weights, bias, rows):
    slots, width = lay.slots, lay.width
    part = weights[0].shape[3] // 4

    def kernel(step, weight, slotted, whole, late, rows, outs, total):
        normed, mixed, attended, logs, middle, normed_two = outs

        @pl.when(step == 0)
        def _():
            def norm_rows(start, count):
                values, _ = normalized(whole[0][pl.ds(start, count), :].astype(F32))
                normed[pl.ds(start, count), :] = (values * rows[0][...] + rows[1][...]).astype(LOW)

            row_loop(norm_rows)

        matrix = weight(0)
        block = (product(normed[...], matrix[:, : 3 * part], NN) + slotted[0][0]).astype(LOW)
        mixed[0] = block
        result, log_rows = attend(block, part)
        attended[0] = result
        logs[0] = log_rows
        add_product(lay, step, total, result, matrix[:, 3 * part :])

        @pl.when(step == slots - 1)
        def _():
            def finish(start, count):
                at = pl.ds(start, count)
                sums = whole[0][at, :].astype(F32) + total[at, :] + rows[2][...]
                middle[at, :] = sums
                values, _ = normalized(sums)
                normed_two[at, :] = (values * rows[3][...] + rows[4][...]).astype(LOW)

            row_loop(finish)

    return layer_call(
        lay,
        kernel,
        "attention_forward",
        [weights],
        [bias],
        [entry],
        [],
        rows,
        [
            low_shape(PAD, width),
            low_shape(slots, PAD, 3 * part),
            low_shape(slots, PAD, part),
            wide_shape(slots, 8, PAD),
            wide_shape(PAD, width),
            low_shape(PAD, width),
        ],
        40,
    )


def dense_forward(lay, normed_two, middle, weights, bias, b_down):
    slots, width = lay.slots, lay.width
    size = weights[0].shape[3] // 2

    def kernel(step, weight, slotted, whole, late, rows, outs, total):
        active, slope, result = outs
        matrix = weight(0)
        hidden = product(whole[0][...], matrix[:, :size], NN) + slotted[0][0]
        chance = 0.5 + 0.5 * lax.erf(hidden * (0.5**0.5))
        density = jnp.exp(-0.5 * hidden * hidden) * 0.3989422804014327
        active[0] = (hidden * chance).astype(LOW)
        slope[0] = (chance + hidden * density).astype(LOW)
        add_product(lay, step, total, active[0], matrix[:, size:])

        @pl.when(step == slots - 1)
        def _():
            (middle_ref,) = late()
            result[...] = (middle_ref[...] + total[...] + rows[0][...]).astype(LOW)

    per_slot = low_shape(slots, PAD, size)
    return layer_call(
        lay,
        kernel,
        "dense_forward",
        [weights],
        [bias],
        [normed_two],
        [middle],
        [b_down],
        [per_slot, per_slot, low_shape(PAD, width)],
        44,
    )


def dense_backward(lay, tangent, slope, middle, weights, gain_two):
    slots, width = lay.slots, lay.width
    size = weights[0].shape[3] // 2

    def kernel(step, weight, slotted, whole, late, rows, outs, total):
        grad_hidden, up_sums, grad_middle, grad_branch, down_sums, gains, shifts, out_sums = outs

        @pl.when(step == 0)
        def _():
            down_sums[...] = jnp.sum(whole[0][...].astype(F32), axis=0, keepdims=True)
            for ref in (gains, shifts, out_sums):
                ref[...] = jnp.zeros_like(ref)

        matrix = weight(0)
        grad = product(whole[0][...], matrix[:, size:], NN).astype(LOW).astype(F32)
        grad = (grad * slotted[0][0].astype(F32)).astype(LOW)
        grad_hidden[0] = grad
        up_sums[0] = jnp.sum(grad.astype(F32), axis=0, keepdims=True)
        add_product(lay, step, total, grad, matrix[:, :size])

        @pl.when(step == slots - 1)
        def _():
            (middle,) = late()

            def finish(start, count):
                at = pl.ds(start, count)
                term, gain_part, shift_part = norm_back(middle[at, :], total[at, :], rows[0][...])
                sums = whole[0][at, :].astype(F32) + term
                grad_middle[at, :] = sums
                grad_branch[at, :] = sums.astype(LOW)
                gains[...] += gain_part
                shifts[...] += shift_part
                out_sums[...] += jnp.sum(sums, axis=0, keepdims=True)

            row_loop(finish)

    row = wide_shape(1, width)
    return layer_call(
        lay,
        kernel,
        "dense_backward",
        [weights],
        [slope],
        [tangent],
        [middle],
        [gain_two],
        [
            low_shape(slots, PAD, size),
            wide_shape(slots, 1, size),
            wide_shape(PAD, width),
            low_shape(PAD, width),
            row,
            row,
            row,
            row,
        ],
        48,
    )


def attention_backward(
    lay, grad_branch, mixed, attended, logs, entry, grad_middle, weights, gain_one
):
    slots, width = lay.slots, lay.width
    part = weights[0].shape[3] // 4

    def kernel(step, weight, slotted, whole, late, rows, outs, total):
        grad_mixed, qkv_sums, grad_entry, gains, shifts = outs

        @pl.when(step == 0)
        def _():
            for ref in (gains, shifts):
                ref[...] = jnp.zeros_like(ref)

        matrix = weight(0)
        upstream = product(whole[0][...], matrix[:, 3 * part :], NN).astype(LOW)
        parts = attend_back(slotted[0][0], upstream, slotted[1][0], slotted[2][0], part)
        for spot, term in enumerate(parts):
            columns = slice(spot * part, (spot + 1) * part)
            rounded = term.astype(LOW)
            grad_mixed[0, :, columns] = rounded
            qkv_sums[0, :, columns] = jnp.sum(rounded.astype(F32), axis=0, keepdims=True)
        add_product(lay, step, total, grad_mixed[0], matrix[:, : 3 * part])

        @pl.when(step == slots - 1)
        def _():
            entry, grad_middle = late()

            def finish(start, count):
                at = pl.ds(start, count)
                term, gain_part, shift_part = norm_back(
                    entry[at, :].astype(F32), total[at, :], rows[0][...]
                )
                grad_entry[at, :] = (grad_middle[at, :] + term).astype(LOW)
                gains[...] += gain_part
                shifts[...] += shift_part

            row_loop(finish)

    row = wide_shape(1, width)
    return layer_call(
        lay,
        kernel,
        "attention_backward",
        [weights],
        [mixed, attended, logs],
        [grad_branch],
        [entry, grad_middle],
        [gain_one],
        [
            low_shape(slots, PAD, 3 * part),
            wide_shape(slots, 1, 3 * part),
            low_shape(PAD, width),
            row,
            row,
        ],
        48,
    )


def weight_grads(lay, slot_order, pairs):
    half, block, shards, width = lay.near, lay.block, lay.shards, lay.width
    sizes = [pair[2].shape[2] for pair in pairs]
    total = sum(sizes)
    whole = pl.BlockSpec((PAD, width), lambda k, s: (0, 0), pipeline_mode=pl.Buffered(1))
    specs, operands, scratch = [], [], []
    for x, x_other, feats, feats_other in pairs:
        feature_spec = pl.BlockSpec((1, PAD, feats.shape[2]), lambda k, s: (k, 0, 0))
        specs += [whole, whole, feature_spec, feature_spec]
        operands += [x, x_other, feats, feats_other]
        scratch += [pltpu.VMEM((width, PAD), LOW)] * 2

    def kernel(_, *refs):
        far_ref, near_ref = refs[4 * len(pairs) : 4 * len(pairs) + 2]
        turned = refs[4 * len(pairs) + 2 :]

        @pl.when(pl.program_id(0) == 0)
        def _():
            for n in range(len(pairs)):
                for b in range(lay.replicas):
                    rows = slice(b * block, (b + 1) * block)
                    other = slice(lay.flip[b] * block, (lay.flip[b] + 1) * block)
                    turned[2 * n][rows, :] = refs[4 * n][:, rows].T
                    turned[2 * n + 1][rows, :] = refs[4 * n + 1][:, other].T

        start = 0
        for n, size in enumerate(sizes):
            grads = product(turned[2 * n][...], refs[4 * n + 2][0], NN) + product(
                turned[2 * n + 1][...], refs[4 * n + 3][0], NN
            )
            grads = grads.reshape(2 * half, block, size).astype(LOW)
            near_ref[:, 0, :, start : start + size] = grads[:half]
            far_ref[:, 0, :, start : start + size] = grads[half:]
            start += size

    return pl.pallas_call(
        kernel,
        grid_spec=pltpu.PrefetchScalarGridSpec(
            num_scalar_prefetch=1,
            grid=(shards,),
            in_specs=specs,
            out_specs=[pl.BlockSpec((half, 1, block, total), lambda k, s: (0, s[k], 0, 0))] * 2,
            scratch_shapes=scratch,
        ),
        out_shape=[low_shape(half, shards, block, total)] * 2,
        compiler_params=params(28),
        cost_estimate=pl.CostEstimate(flops=1000, bytes_accessed=2**20, transcendentals=0),
        name="weight_grads",
    )(slot_order, *operands)


def add_low(*terms):
    return sum(term.astype(F32) for term in terms).astype(LOW)


def sum_vectors(lay, values, other_values, shard, replica):
    total = values + lay.across_cores(other_values)
    total = jnp.take(total, jnp.arange(lay.replicas, dtype=jnp.int32) ^ replica, axis=1)
    total = jnp.take(total, jnp.arange(lay.shards, dtype=jnp.int32) ^ shard, axis=0)
    total = total.transpose(1, 0, 2)
    for bit in range(lay.bits - 1, -1, -1):
        half = total.shape[0] // 2
        total = total[:half] + lay.along_bit_plain(total[half:], bit)
    total = total[0]
    result = total[0]
    for slot in range(1, lay.shards):
        result = result + lay.along_shard(total[slot], slot)
    return result


def shards(
    boundary_in,
    counts,
    w_qkv,
    b_qkv,
    w_out,
    b_out,
    w_up,
    b_up,
    w_down,
    b_down,
    norm1_gain,
    norm1_shift,
    norm2_gain,
    norm2_shift,
):
    width = boundary_in.shape[4]
    sizes = {axis: lax.axis_size(axis) for axis in ALL_AXES}
    lay = Layout(sizes, width)
    core = lax.axis_index("section").astype(jnp.int32)
    shard = lax.axis_index("shard").astype(jnp.int32)
    replica = lax.axis_index("replica").astype(jnp.int32)
    on_first = core == 0
    heads_wide = w_qkv.shape[3]
    part = heads_wide // 2
    ff_part = w_up.shape[2] // 2
    positions = jnp.arange(lay.replicas, dtype=jnp.int32)
    flips = jnp.asarray(lay.flip, jnp.int32)
    blocks = jnp.where(on_first, positions, flips) ^ replica
    inverse_blocks = jnp.where(on_first, positions ^ replica, flips[positions ^ replica])
    halves = jnp.arange(2, dtype=jnp.int32) ^ core
    scalars = jnp.concatenate([blocks, halves, core[None]])

    slot_order = jnp.arange(lay.shards, dtype=jnp.int32) ^ shard

    order = Order()
    raw_qkv = w_qkv[0].reshape(width, 6 * part)
    raw_out, raw_up, raw_down = w_out[0], w_up[0], w_down[0]
    split_pieces = first_pieces(lay, raw_qkv, raw_out, raw_up, raw_down, scalars)
    first, second = [], []
    for piece, sent in zip(split_pieces[:2], split_pieces[2:]):
        other = lay.across_cores(sent)
        first.append(jnp.where(on_first, piece, other))
        second.append(jnp.where(on_first, other, piece))
    pieces = first + second
    order.token = pieces[0]

    pictures = boundary_in[0, :, 0]
    received = lay.across_cores(pictures)
    live = (shard < counts[replica, core]).astype(F32)[None]
    image, cot = arrange_images(lay, pictures, received, blocks, core, live)

    raw_qkv, raw_out, raw_up, raw_down = order.tie(raw_qkv, raw_out, raw_up, raw_down)
    own_attention = arrange_attention(
        lay,
        (raw_qkv, raw_out),
        (lay.across_cores(raw_qkv), lay.across_cores(raw_out)),
        scalars,
    )
    own_dense = arrange_dense(
        lay,
        (raw_up, raw_down),
        (lay.across_cores(raw_up), lay.across_cores(raw_down)),
        scalars,
    )
    own = (own_attention[0], own_dense[0], own_attention[1], own_dense[1])

    packed = jnp.concatenate(
        [v[0] for v in (b_out, b_down, norm1_gain, norm1_shift, norm2_gain, norm2_shift)]
        + [b_qkv.reshape(-1), b_up.reshape(-1)]
    )
    packed_other = lay.across_cores(packed)
    both = jnp.stack(
        [jnp.where(on_first, packed, packed_other), jnp.where(on_first, packed_other, packed)]
    )
    wide = both[:, : 6 * width].reshape(2, 6, lay.replicas, lay.block)
    wide = jnp.take(wide, blocks, axis=2).reshape(2, 6, 1, width).astype(F32)
    split = both[:, 6 * width :]
    split = jnp.stack([split] + [lay.along_shard(split, k) for k in range(1, lay.shards)])
    split_qkv = split[:, :, : 4 * part].reshape(lay.shards, 2, 2, 2, part)
    split_qkv = jnp.take(split_qkv, halves, axis=3).transpose(1, 3, 0, 2, 4)
    split_qkv = split_qkv.reshape(2, lay.slots, 2, part)
    bias_qkv = jnp.concatenate(
        [split_qkv[:, :, 0], jnp.zeros_like(split_qkv[:, :, 0]), split_qkv[:, :, 1]], axis=-1
    ).reshape(2, lay.slots, 1, 3 * part).astype(F32)
    bias_up = split[:, :, 4 * part :].reshape(lay.shards, 2, 2, ff_part)
    bias_up = jnp.take(bias_up, halves, axis=2).transpose(1, 2, 0, 3)
    bias_up = bias_up.reshape(2, lay.slots, 1, ff_part).astype(F32)

    gather = Gather(lay, order, slot_order, pieces, own)

    kept, weights = [], []
    entry = image
    gather.start(0)
    gather.step(0)
    gather.start(1)
    for layer in range(2):
        vec_out, vec_down, gain_one, shift_one, gain_two, shift_two = wide[layer]
        if layer == 0:
            w_attention = gather.finish(0)
        normed, mixed, attended, logs, middle, normed_two = order.run(
            functools.partial(attention_forward, lay),
            entry,
            w_attention,
            bias_qkv[layer],
            (gain_one, shift_one, vec_out, gain_two, shift_two),
        )
        exchanged = [
            lay.across_cores(value)
            for value in order.tie(normed, normed_two, attended[lay.shards :])
        ]
        if layer == 0:
            gather.step(1)
            gather.start(2)
            for _ in range(1, lay.bits):
                gather.step(1)
            gather.step(2)
            gather.start(3)
            w_dense = gather.finish(1)
            for _ in range(1, lay.bits):
                gather.step(2)
        else:
            w_dense = gather.finish(3)
        active, slope, result = order.run(
            functools.partial(dense_forward, lay),
            normed_two,
            middle,
            w_dense,
            bias_up[layer],
            vec_down,
        )
        exchanged = order.absorb(*exchanged)
        exchanged += tuple(lay.across_cores(v) for v in order.tie(active[lay.shards :]))
        weights.append((w_attention, w_dense))
        if layer == 0:
            gather.step(3)
            w_attention = gather.finish(2)
            for _ in range(1, lay.bits):
                gather.step(3)
        kept.append(
            (entry, normed, mixed, attended, logs, middle, normed_two, active, slope, exchanged)
        )
        entry = result

    sums, vector_sums = {}, {}
    pending = []

    def exchange(*values):
        return [lay.across_cores(value) for value in order.tie(*values)]

    def advance(leave):
        for item in pending[: max(len(pending) - leave, 0)]:
            name, parts, bit = item
            spot = pending.index(item)
            if bit < 0:
                (sums[name],) = order.absorb(parts)
                pending.remove(item)
            elif bit == 0:
                total = order.run(lambda *v: add_low(*v)[0], *parts)
                if name == (0, "attention"):
                    arrived = lax.all_to_all(total, "shard", 0, 0, tiled=True)
                    arrived = jnp.sum(arrived.astype(F32), axis=0)
                else:
                    arrived = lax.psum_scatter(total, "shard", scatter_dimension=0)
                    arrived = arrived.astype(F32)
                pending[spot] = (name, arrived, -1)
            else:
                split = parts[0].shape[0] // 2
                sent = order.run(add_low, *(part[split:] for part in parts))
                arrived = lay.along_bit(sent, bit - 1)
                pending[spot] = (name, [part[:split] for part in parts] + [arrived], bit - 1)

    def reduce(name, *pairs):
        far, near = order.run(lambda *given: weight_grads(lay, slot_order, given), *pairs)
        pending.append((name, [near, lay.along_bit(far, lay.bits - 1)], lay.bits - 1))

    tangent = cot
    for layer in (1, 0):
        w_attention, w_dense = weights[layer]
        vec_out, vec_down, gain_one, shift_one, gain_two, shift_two = wide[layer]
        entry_in, normed, mixed, attended, logs, middle, normed_two, active, slope, other = kept[layer]
        normed_other, normed_two_other, attended_other, active_other = other
        (tangent_other,) = exchange(tangent)
        reduce((layer, "down"), (tangent, tangent_other, active, active_other))
        (
            grad_hidden,
            up_sums,
            grad_middle,
            grad_branch,
            down_sums,
            gain_two_sum,
            shift_two_sum,
            out_sums,
        ) = order.run(
            functools.partial(dense_backward, lay),
            tangent,
            slope,
            middle,
            w_dense,
            gain_two,
        )
        (hidden_other,) = exchange(grad_hidden[lay.shards :])
        advance(0)
        reduce((layer, "up"), (normed_two, normed_two_other, grad_hidden, hidden_other))
        (branch_other,) = exchange(grad_branch)
        grad_mixed, qkv_sums, grad_entry, gain_one_sum, shift_one_sum = order.run(
            functools.partial(attention_backward, lay),
            grad_branch,
            mixed,
            attended,
            logs,
            entry_in,
            grad_middle,
            w_attention,
            gain_one,
        )
        (branch_other,) = order.absorb(branch_other)
        (mixed_other,) = exchange(grad_mixed[lay.shards :])
        advance(0)
        reduce(
            (layer, "attention"),
            (normed, normed_other, grad_mixed, mixed_other),
            (grad_branch, branch_other, attended, attended_other),
        )
        model_sums = jnp.concatenate(
            [out_sums, down_sums, gain_one_sum, shift_one_sum, gain_two_sum, shift_two_sum]
        )
        vector_sums[layer] = (model_sums, up_sums, qkv_sums)
        tangent = grad_entry
    vector_sums = dict(zip(vector_sums, order.tie(*vector_sums.values())))
    (back,) = order.tie(tangent)
    back = restore_image(lay, back, blocks, jnp.ones((1,), F32))
    while pending:
        advance(0)

    def to_owner(first, second):
        keep = jnp.where(on_first, first, second)
        other = lay.across_cores(jnp.where(on_first, second, first))
        return jnp.where(on_first, keep, other), jnp.where(on_first, other, keep)

    down_halves = to_owner(sums[0, "down"], sums[1, "down"])
    up_halves = to_owner(sums[0, "up"], sums[1, "up"])
    attention_halves = to_owner(sums[0, "attention"], sums[1, "attention"])
    grad_w_down = jnp.concatenate(down_halves, axis=1).T[None]
    grad_w_up = jnp.concatenate(up_halves, axis=1)[None]
    grad_w_qkv = jnp.stack(
        [half[:, : 3 * part].reshape(-1, 3, part) for half in attention_halves], axis=2
    ).reshape(1, lay.block, 3, heads_wide)
    grad_w_out = jnp.concatenate([half[:, 3 * part :] for half in attention_halves], axis=1).T[None]

    packs = []
    for model_sums, up_sums, qkv_sums in (vector_sums[0], vector_sums[1]):
        model = jnp.take(model_sums.reshape(6, lay.replicas, lay.block), inverse_blocks, axis=1)
        model = model.reshape(6, lay.shards, lay.replicas, -1).transpose(1, 2, 0, 3)
        ups = jnp.take(up_sums.reshape(2, lay.shards, ff_part), slot_order, axis=1)
        ups = jnp.take(ups, halves, axis=0).transpose(1, 0, 2)
        parts = jnp.take(qkv_sums.reshape(2, lay.shards, 3, part), slot_order, axis=1)
        parts = jnp.take(parts, halves, axis=0)
        parts = jnp.stack([parts[:, :, 0], parts[:, :, 2]]).transpose(2, 0, 1, 3)
        parts = parts.reshape(lay.shards, 2, lay.replicas, -1).transpose(0, 2, 1, 3)
        shape = (lay.shards, lay.replicas, -1)
        packs.append(
            jnp.concatenate(
                [model.reshape(shape), parts.reshape(shape), ups.reshape(shape)], axis=2
            )
        )
    mine = jnp.where(on_first, packs[0], packs[1])
    other = jnp.where(on_first, packs[1], packs[0])
    summed = sum_vectors(lay, mine, other, shard, replica)
    share = width // (lay.shards * lay.replicas)
    vectors = [summed[i * share : (i + 1) * share][None] for i in range(6)]
    grad_b_qkv = summed[6 * share : 8 * share].reshape(1, 2, share)
    grad_b_up = summed[8 * share :][None]

    ahead = restore_image(lay, entry, blocks, live)
    keep = jnp.where(on_first, back, ahead)
    other = lay.across_cores(jnp.where(on_first, ahead, back))
    boundary_out = jnp.stack([jnp.where(on_first, keep, other), jnp.where(on_first, other, keep)])
    boundary_out = boundary_out[None, :, None]
    return (
        boundary_out,
        grad_w_qkv,
        grad_b_qkv,
        grad_w_out,
        vectors[0],
        grad_w_up,
        grad_b_up,
        grad_w_down,
        vectors[1],
        vectors[2],
        vectors[3],
        vectors[4],
        vectors[5],
    )


def solution(mesh):
    spread = P("section", ("shard", "replica"))
    return jax.shard_map(
        shards,
        mesh=mesh,
        in_specs=(
            P("section", None, ("shard", "replica"), None, None),
            P(),
            P("section", None, None, "shard"),
            P("section", None, "shard"),
            P("section", "shard", None),
            P("section", None),
            P("section", None, "shard"),
            P("section", "shard"),
            P("section", "shard", None),
            P("section", None),
            P("section", None),
            P("section", None),
            P("section", None),
            P("section", None),
        ),
        out_specs=(
            P("section", None, ("shard", "replica"), None, None),
            P("section", "replica", None, "shard"),
            P("section", None, ("shard", "replica")),
            P("section", "shard", "replica"),
            spread,
            P("section", "replica", "shard"),
            spread,
            P("section", "shard", "replica"),
            spread,
            spread,
            spread,
            spread,
            spread,
        ),
        check_vma=False,
    )
```

```python
import functools

import jax
import jax.numpy as jnp
from jax import lax
from jax.experimental import pallas as pl
from jax.experimental.pallas import tpu as pltpu
from jax.sharding import PartitionSpec as P

HEAD = 64
SEQ = 577
PAD = 592
CHUNK = 144
LOW = jnp.bfloat16
F32 = jnp.float32
ALL_AXES = ("section", "shard", "replica")
NT = (((1,), (1,)), ((), ()))
NN = (((1,), (0,)), ((), ()))
TN = (((0,), (0,)), ((), ()))


def reverse_bits(value, bits):
    flipped = 0
    for spot in range(bits):
        flipped |= ((value >> spot) & 1) << (bits - 1 - spot)
    return flipped


def product(left, right, dims):
    return lax.dot_general(left, right, dims, preferred_element_type=F32)


def row_loop(body):
    whole = PAD // CHUNK

    def step(index, carry):
        body(pl.multiple_of(index * CHUNK, 16), CHUNK)
        return carry

    lax.fori_loop(0, whole, step, 0)
    if PAD % CHUNK:
        body(whole * CHUNK, PAD % CHUNK)


def params(megabytes=48):
    return pltpu.CompilerParams(vmem_limit_bytes=megabytes * 2**20)


def launch(
    lay, kernel, name, scalars, operands, in_specs, out_specs, out_shape, grid, scratch, megabytes, cost=1000
):
    tokens = lay.after
    count = len(scalars) + len(operands)

    def ordered(*refs):
        rest = refs[count + len(tokens) :]
        rest[len(out_shape)][...] = jnp.zeros((8, 128), F32)
        kernel(*refs[:count], *rest[: len(out_shape)], *rest[len(out_shape) + 1 :])

    token_spec = pl.BlockSpec((8, 128), lambda *_: (0, 0))
    results = pl.pallas_call(
        ordered,
        grid_spec=pltpu.PrefetchScalarGridSpec(
            num_scalar_prefetch=len(scalars),
            grid=grid,
            in_specs=list(in_specs) + [pl.BlockSpec(memory_space=pl.ANY)] * len(tokens),
            out_specs=list(out_specs) + [token_spec],
            scratch_shapes=scratch,
        ),
        out_shape=list(out_shape) + [jax.ShapeDtypeStruct((8, 128), F32)],
        compiler_params=params(megabytes),
        cost_estimate=pl.CostEstimate(flops=cost, bytes_accessed=2**18, transcendentals=0),
        name=name,
    )(*scalars, *operands, *tokens)
    lay.after = [results[-1]]
    return results[:-1]


def normalized(values):
    center = values - jnp.mean(values, axis=-1, keepdims=True)
    spread = jnp.mean(center * center, axis=-1, keepdims=True)
    inverse = lax.rsqrt(spread + 1e-06)
    return center * inverse, inverse


class Layout:
    def __init__(self, mesh_shape, width):
        self.shards = mesh_shape["shard"]
        self.replicas = mesh_shape["replica"]
        self.bits = self.replicas.bit_length() - 1
        self.width = width
        self.block = width // self.replicas
        self.flip = [reverse_bits(b, self.bits) for b in range(self.replicas)]
        self.near = self.replicas // 2
        self.slots = 2 * self.shards
        self.after = []

    def absorb(self, *values):
        for value in values:
            corner = value.reshape((-1,) + value.shape[-2:])[0, :8, :128]
            self.after.append(corner)

    def hold(self, *values):
        values, self.after = lax.optimization_barrier((values, self.after))
        return values

    def across_cores(self, value):
        return lax.ppermute(value, "section", [(0, 1), (1, 0)])

    def along_shard(self, value, slot):
        return lax.ppermute(value, "shard", [(i, i ^ slot) for i in range(self.shards)])

    def along_bit_plain(self, value, bit):
        route = [(i, i ^ (1 << bit)) for i in range(self.replicas)]
        return lax.ppermute(value, "replica", route)

    def along_bit(self, value, bit):
        route = []
        for core in range(2):
            physical = bit if core == 0 else self.bits - 1 - bit
            for shard in range(self.shards):
                base = (core * self.shards + shard) * self.replicas
                for replica in range(self.replicas):
                    route.append((base + replica, base + (replica ^ (1 << physical))))
        return lax.ppermute(value, ALL_AXES, route)


def arrange_images(lay, mine, received, blocks, core, live):
    width, block = lay.width, lay.block

    def kernel(scalars, live_ref, mine_ref, other_ref, image_ref, cot_ref):
        here = mine_ref[0]
        there = other_ref[0]
        first = scalars[lay.replicas] == 0
        image = jnp.where(first, here, there)
        cot = jnp.where(first, there, here).astype(F32) * live_ref[0]
        image_ref[...] = jnp.zeros_like(image_ref)
        cot_ref[...] = jnp.zeros_like(cot_ref)
        image_ref[0:SEQ, :] = image
        cot_ref[0:SEQ, :] = cot.astype(LOW)

    scalars = jnp.concatenate([blocks, core[None]]).astype(jnp.int32)
    shape = jax.ShapeDtypeStruct((PAD, width), LOW)
    whole = pl.BlockSpec((1, SEQ, block), lambda b, s: (s[lay.replicas], 0, s[b]))
    return launch(
        lay,
        kernel,
        "arrange_images",
        [scalars],
        [live, mine, received],
        [pl.BlockSpec(memory_space=pltpu.SMEM), whole, whole],
        [pl.BlockSpec((PAD, block), lambda b, s: (0, b))] * 2,
        [shape, shape],
        (lay.replicas,),
        [],
        24,
    )


def restore_image(lay, values, blocks, scale):
    def kernel(scalars, scale_ref, in_ref, out_ref):
        out_ref[...] = (in_ref[0:SEQ, :].astype(F32) * scale_ref[0]).astype(LOW)

    return launch(
        lay,
        kernel,
        "restore_image",
        [blocks],
        [scale, values],
        [
            pl.BlockSpec(memory_space=pltpu.SMEM),
            pl.BlockSpec((PAD, lay.block), lambda b, s: (0, b)),
        ],
        [pl.BlockSpec((SEQ, lay.block), lambda b, s: (0, s[b]))],
        [jax.ShapeDtypeStruct((SEQ, lay.width), LOW)],
        (lay.replicas,),
        [],
        16,
    )[0]


def chosen_half(flag, low, high):
    return jnp.where(flag == 0, low, high)


def arrange_attention(lay, mine, received, scalars):
    rep, block = lay.replicas, lay.block
    part = mine[1].shape[0] // 2

    def kernel(s, qkv_mine, qkv_other, out_mine, out_other, first_ref, second_ref):
        first = s[rep + 2] == 0
        half = s[rep + pl.program_id(0)]

        def columns(ref, t):
            start = 2 * t * part
            return chosen_half(
                half, ref[:, start : start + part], ref[:, start + part : start + 2 * part]
            )

        for t in range(3):
            here, there = columns(qkv_mine, t), columns(qkv_other, t)
            first_ref[0, 0, :, t * part : (t + 1) * part] = jnp.where(first, here, there)
            second_ref[0, 0, :, t * part : (t + 1) * part] = jnp.where(first, there, here)
        here, there = out_mine[...].T, out_other[...].T
        first_ref[0, 0, :, 3 * part :] = jnp.where(first, here, there)
        second_ref[0, 0, :, 3 * part :] = jnp.where(first, there, here)

    shape = jax.ShapeDtypeStruct((2, rep, block, 4 * part), LOW)
    qkv_spec = pl.BlockSpec((block, 6 * part), lambda p, b, s: (s[b], 0))
    out_spec = pl.BlockSpec((part, block), lambda p, b, s: (s[rep + p], s[b]))
    return launch(
        lay,
        kernel,
        "arrange_attention",
        [scalars],
        [mine[0], received[0], mine[1], received[1]],
        [qkv_spec, qkv_spec, out_spec, out_spec],
        [pl.BlockSpec((1, 1, block, 4 * part), lambda p, b, s: (p, b, 0, 0))] * 2,
        [shape, shape],
        (2, rep),
        [],
        16,
    )


def arrange_dense(lay, mine, received, scalars):
    rep, block = lay.replicas, lay.block
    part = mine[0].shape[1] // 2

    def kernel(s, up_mine, up_other, down_mine, down_other, first_ref, second_ref):
        first = s[rep + 2] == 0
        here, there = up_mine[...], up_other[...]
        first_ref[0, 0, :, :part] = jnp.where(first, here, there)
        second_ref[0, 0, :, :part] = jnp.where(first, there, here)
        here, there = down_mine[...].T, down_other[...].T
        first_ref[0, 0, :, part:] = jnp.where(first, here, there)
        second_ref[0, 0, :, part:] = jnp.where(first, there, here)

    shape = jax.ShapeDtypeStruct((2, rep, block, 2 * part), LOW)
    up_spec = pl.BlockSpec((block, part), lambda p, b, s: (s[b], s[rep + p]))
    down_spec = pl.BlockSpec((part, block), lambda p, b, s: (s[rep + p], s[b]))
    return launch(
        lay,
        kernel,
        "arrange_dense",
        [scalars],
        [mine[0], received[0], mine[1], received[1]],
        [up_spec, up_spec, down_spec, down_spec],
        [pl.BlockSpec((1, 1, block, 2 * part), lambda p, b, s: (p, b, 0, 0))] * 2,
        [shape] * 2,
        (2, rep),
        [],
        16,
    )


def first_pieces(lay, qkv, out, up, down, scalars):
    rep, block = lay.replicas, lay.block
    part, wide = out.shape[0] // 2, up.shape[1] // 2

    def kernel(s, qkv_ref, out_ref, up_ref, down_ref, *outs):
        core = s[rep + 2]
        for flag, attention_ref, dense_ref in ((core, *outs[:2]), (1 - core, *outs[2:])):
            for t in range(3):
                start = 2 * t * part
                attention_ref[:, t * part : (t + 1) * part] = chosen_half(
                    flag,
                    qkv_ref[:, start : start + part],
                    qkv_ref[:, start + part : start + 2 * part],
                )
            attention_ref[:, 3 * part :] = chosen_half(flag, out_ref[:part], out_ref[part:]).T
            dense_ref[:, :wide] = chosen_half(flag, up_ref[:, :wide], up_ref[:, wide:])
            dense_ref[:, wide:] = chosen_half(flag, down_ref[:wide], down_ref[wide:]).T

    attention_shape = jax.ShapeDtypeStruct((block, 4 * part), LOW)
    dense_shape = jax.ShapeDtypeStruct((block, 2 * wide), LOW)
    attention_spec = pl.BlockSpec((block, 4 * part), lambda i, s: (0, 0))
    dense_spec = pl.BlockSpec((block, 2 * wide), lambda i, s: (0, 0))
    return launch(
        lay,
        kernel,
        "first_pieces",
        [scalars],
        [qkv, out, up, down],
        [
            pl.BlockSpec((block, 6 * part), lambda i, s: (s[0], 0)),
            pl.BlockSpec((2 * part, block), lambda i, s: (0, s[0])),
            pl.BlockSpec((block, 2 * wide), lambda i, s: (s[0], 0)),
            pl.BlockSpec((2 * wide, block), lambda i, s: (0, s[0])),
        ],
        [attention_spec, dense_spec] * 2,
        [attention_shape, dense_shape] * 2,
        (1,),
        [],
        16,
    )


def pick_slots(lay, gathered, slot_order):
    rows, columns = gathered.shape[1:]

    def kernel(_, in_ref, out_ref):
        out_ref[0] = in_ref[...]

    return launch(
        lay,
        kernel,
        "pick_slots",
        [slot_order],
        [gathered],
        [pl.BlockSpec((1, rows, columns), lambda k, s: (s[k + 1], 0, 0))],
        [pl.BlockSpec((1, 1, rows, columns), lambda k, s: (0, k, 0, 0))],
        [jax.ShapeDtypeStruct((1, lay.shards - 1, rows, columns), LOW)],
        (lay.shards - 1,),
        [],
        8,
    )[0]


def join(lay, first, second):
    count, rows = first.shape[0], first.shape[1]
    shape = (2 * count,) + first.shape[1:]
    block = (1, rows) + first.shape[2:]

    def kernel(first_ref, second_ref, out_ref):
        step = pl.program_id(0)

        @pl.when(step < count)
        def _():
            out_ref[...] = first_ref[...]

        @pl.when(step >= count)
        def _():
            out_ref[...] = second_ref[...]

    return launch(
        lay,
        kernel,
        "join",
        [],
        [first, second],
        [
            pl.BlockSpec(block, lambda i: (jnp.minimum(i, count - 1), 0, 0, 0)),
            pl.BlockSpec(block, lambda i: (jnp.maximum(i - count, 0), 0, 0, 0)),
        ],
        [pl.BlockSpec(block, lambda i: (i, 0, 0, 0))],
        [jax.ShapeDtypeStruct(shape, LOW)],
        (2 * count,),
        [],
        16,
    )[0]


def copied(lay, value):
    def kernel(in_ref, out_ref):
        out_ref[...] = in_ref[...]

    spec = pl.BlockSpec(value.shape, lambda i: (0, 0))
    shape = jax.ShapeDtypeStruct(value.shape, value.dtype)
    return launch(lay, kernel, "copied", [], [value], [spec], [spec], [shape], (1,), [], 8)[0]


class Gather:
    def __init__(self, lay, slot_order, pieces):
        self.lay, self.pieces, self.slot_order = lay, pieces, slot_order
        self.state = [None] * len(pieces)
        self.done = [0] * len(pieces)

    def start(self, n):
        piece = self.pieces[n] if n == 0 else copied(self.lay, self.pieces[n])
        self.state[n] = lax.all_gather(piece, "shard")

    def step(self, n):
        lay = self.lay
        if self.done[n] == 0:
            near = pick_slots(lay, self.state[n], self.slot_order)
        else:
            near = join(lay, *self.state[n])
        self.state[n] = (near, lay.along_bit(near, self.done[n]))
        self.done[n] += 1

    def finish(self, n, own):
        lay = self.lay
        while self.done[n] < lay.bits:
            self.step(n)
        near, far = self.state[n]
        (far,) = lay.hold(far)
        return (own, near, far, lay.across_cores(near), lay.across_cores(far))


def fetch_weights(lay, refs, held, sems, slot):
    own, near, far, near_other, far_other = refs
    half = lay.near
    side, k = divmod(slot, lay.shards)

    def start(source, target):
        pltpu.make_async_copy(source, target, sems.at[slot]).start()

    if k == 0:
        start(own.at[side], held.at[slot])
    elif side == 0:
        start(near.at[:, k - 1], held.at[slot, 0:half])
        start(far.at[:, k - 1], held.at[slot, half : 2 * half])
    else:
        for b in range(half):
            start(near_other.at[b, k - 1], held.at[slot, lay.flip[b]])
            start(far_other.at[b, k - 1], held.at[slot, lay.flip[half + b]])


def await_weights(held, sems, slot):
    pltpu.make_async_copy(held.at[slot], held.at[slot], sems.at[slot]).wait()


def flat(block):
    return block.reshape(block.shape[0] * block.shape[1], block.shape[2])


def layer_call(lay, kernel, name, weights, slotted, whole, late, rows, outs, megabytes):
    slots, width, shards = lay.slots, lay.width, lay.shards
    once = dict(pipeline_mode=pl.Buffered(1))

    def own_half(i):
        return (jnp.minimum(i, shards), 0, 0)

    def other_half(i):
        return (jnp.where(i < shards, shards, i - shards), 0, 0)

    def spec(shape, **mode):
        if len(shape) == 3:
            return pl.BlockSpec((1,) + shape[1:], lambda i: (i, 0, 0))
        return pl.BlockSpec(shape, lambda i: (0, 0), **mode)

    out_specs, out_shape = [], []
    for o in outs:
        if len(o.shape) == 3 and o.shape[0] == shards + 1:
            out_specs += [pl.BlockSpec((1,) + o.shape[1:], m) for m in (own_half, other_half)]
            out_shape += [o, o]
        else:
            out_specs.append(spec(o.shape))
            out_shape.append(o)
    outs = out_shape
    anywhere = pl.BlockSpec(memory_space=pltpu.HBM)
    counts = [5 * len(weights), len(slotted), len(whole), len(late), len(rows), len(outs)]

    def body(*refs):
        groups, at = [], 0
        for count in counts + [1, len(weights), len(weights), len(late)]:
            groups.append(refs[at : at + count])
            at += count
        arrays, slot_refs, whole_refs, late_refs, row_refs, out_refs = groups[:6]
        (total,), held, sems, late_held = groups[6:10]
        late_sem = refs[at] if late else None
        step = pl.program_id(0)

        def late_copy(n):
            return pltpu.make_async_copy(late_refs[n], late_held[n], late_sem.at[n])

        @pl.when(step == 0)
        def _():
            for slot in range(slots):
                for n in range(len(weights)):
                    fetch_weights(lay, arrays[5 * n : 5 * n + 5], held[n], sems[n], slot)
            for n in range(len(late)):
                late_copy(n).start()

        def weight(n):
            await_weights(held[n], sems[n], step)
            return flat(held[n][step])

        def late_values():
            for n in range(len(late)):
                late_copy(n).wait()
            return late_held

        kernel(step, weight, slot_refs, whole_refs, late_values, row_refs, out_refs, total)

    arrays = [array for matrix in weights for array in matrix]
    scratch = [pltpu.VMEM((PAD, width), F32)]
    scratch += [pltpu.VMEM((slots,) + matrix[0].shape[1:], LOW) for matrix in weights]
    scratch += [pltpu.SemaphoreType.DMA((slots,)) for _ in weights]
    scratch += [pltpu.VMEM(a.shape, a.dtype) for a in late]
    if late:
        scratch.append(pltpu.SemaphoreType.DMA((len(late),)))
    return launch(
        lay,
        body,
        name,
        [],
        [*arrays, *slotted, *whole, *late, *rows],
        [anywhere] * len(arrays)
        + [spec(a.shape) for a in slotted]
        + [spec(a.shape, **once) for a in whole]
        + [anywhere] * len(late)
        + [spec(a.shape, **once) for a in rows],
        out_specs,
        out_shape,
        (slots,),
        scratch,
        megabytes,
    )


def add_product(lay, step, total, acts, matrix):
    for b in range(lay.replicas):
        columns = slice(b * lay.block, (b + 1) * lay.block)
        term = product(acts, matrix[columns], NT)
        total[:, columns] = jnp.where(step == 0, 0.0, total[:, columns]) + term


def low_shape(*shape):
    return jax.ShapeDtypeStruct(shape, LOW)


def wide_shape(*shape):
    return jax.ShapeDtypeStruct(shape, F32)


def mask_keys(scores, low):
    edge = SEQ // 16 * 16
    valid = lax.broadcasted_iota(jnp.int32, (PAD - edge, 1), 0) < SEQ - edge
    return jnp.concatenate([scores[:edge], jnp.where(valid, scores[edge:], low)], axis=0)


def attend(block, part):
    query, keys, values = block[:, :part], block[:, part : 2 * part], block[:, 2 * part :]
    heads = range(part // HEAD)
    lanes = lax.broadcasted_iota(jnp.int32, (1, part), 1) // HEAD
    query = query * HEAD ** (-0.5)
    turned = values.T
    ones = jnp.ones((16, PAD), LOW)
    scores = [product(keys, jnp.where(lanes == h, query, 0), NT) for h in heads]
    scores = [mask_keys(score, -1e30) for score in scores]
    peaks = [jnp.max(score, axis=0, keepdims=True) for score in scores]
    weights = [jnp.exp(score - peak).astype(LOW) for score, peak in zip(scores, peaks)]
    sums = [
        product(jnp.concatenate([turned[h * HEAD : (h + 1) * HEAD], ones], axis=0), weights[h], NN)
        for h in heads
    ]
    result = jnp.concatenate([s[:HEAD] / s[HEAD : HEAD + 1] for s in sums], axis=0).T
    spot = lax.broadcasted_iota(jnp.int32, (8, 1), 0)
    logs = jnp.zeros((8, PAD), F32)
    for h in heads:
        logs = jnp.where(spot == h, peaks[h] + jnp.log(sums[h][HEAD : HEAD + 1]), logs)
    return result.astype(LOW), logs


def attend_back(block, grads, attended, logs, part):
    query, keys, values = block[:, :part], block[:, part : 2 * part], block[:, 2 * part :]
    heads = range(part // HEAD)
    lanes = lax.broadcasted_iota(jnp.int32, (1, part), 1) // HEAD
    wide = lax.broadcasted_iota(jnp.int32, (1, 128), 1)
    query = query * HEAD ** (-0.5)

    def pick(h, array):
        return jnp.where(lanes == h, array, 0)

    along = grads.astype(F32) * attended.astype(F32)
    inner = jnp.zeros((PAD, 128), F32)
    for h in heads:
        inner = jnp.where(wide == h, jnp.sum(pick(h, along), axis=-1, keepdims=True), inner)
    inner = inner.T
    scores = [product(keys, pick(h, query), NT) for h in heads]
    slopes = [product(values, pick(h, grads), NT) for h in heads]
    chances = [mask_keys(jnp.exp(scores[h] - logs[h : h + 1]), 0.0) for h in heads]
    grad_scores = [(chances[h] * (slopes[h] - inner[h : h + 1])).astype(LOW) for h in heads]
    low = [chance.astype(LOW) for chance in chances]
    value_terms = [product(low[h], grads, NN) for h in heads]
    key_terms = [product(grad_scores[h], query, NN) for h in heads]
    turned = keys.T
    query_terms = [
        product(turned[h * HEAD : (h + 1) * HEAD], grad_scores[h], NN) for h in heads
    ]

    def merge(terms):
        result = terms[0]
        for h in heads:
            result = jnp.where(lanes == h, terms[h], result)
        return result

    return (
        jnp.concatenate(query_terms, axis=0).T * HEAD ** (-0.5),
        merge(key_terms),
        merge(value_terms),
    )


def norm_back(values, grads, gain):
    values, inverse = normalized(values)
    slope = grads * gain
    mean = jnp.mean(slope, axis=-1, keepdims=True)
    along = jnp.mean(slope * values, axis=-1, keepdims=True)
    term = inverse * (slope - mean - values * along)
    return (
        term,
        jnp.sum(grads * values, axis=0, keepdims=True),
        jnp.sum(grads, axis=0, keepdims=True),
    )


def attention_forward(lay, entry, weights, bias, rows):
    slots, width = lay.slots, lay.width
    part = weights[0].shape[3] // 4

    def kernel(step, weight, slotted, whole, late, rows, outs, total):
        normed, mixed, attended, logs, middle, normed_two = outs

        @pl.when(step == 0)
        def _():
            def norm_rows(start, count):
                values, _ = normalized(whole[0][pl.ds(start, count), :].astype(F32))
                normed[pl.ds(start, count), :] = (values * rows[0][...] + rows[1][...]).astype(LOW)

            row_loop(norm_rows)

        matrix = weight(0)
        block = (product(normed[...], matrix[:, : 3 * part], NN) + slotted[0][0]).astype(LOW)
        mixed[0] = block
        result, log_rows = attend(block, part)
        attended[0] = result
        logs[0] = log_rows
        add_product(lay, step, total, result, matrix[:, 3 * part :])

        @pl.when(step == slots - 1)
        def _():
            def finish(start, count):
                at = pl.ds(start, count)
                sums = whole[0][at, :].astype(F32) + total[at, :] + rows[2][...]
                middle[at, :] = sums
                values, _ = normalized(sums)
                normed_two[at, :] = (values * rows[3][...] + rows[4][...]).astype(LOW)

            row_loop(finish)

    return layer_call(
        lay,
        kernel,
        "attention_forward",
        [weights],
        [bias],
        [entry],
        [],
        rows,
        [
            low_shape(PAD, width),
            low_shape(slots, PAD, 3 * part),
            low_shape(slots, PAD, part),
            wide_shape(slots, 8, PAD),
            wide_shape(PAD, width),
            low_shape(PAD, width),
        ],
        40,
    )


def dense_forward(lay, normed_two, middle, weights, bias, b_down):
    slots, width = lay.slots, lay.width
    size = weights[0].shape[3] // 2

    def kernel(step, weight, slotted, whole, late, rows, outs, total):
        active, active_sent, slope, result = outs
        matrix = weight(0)
        hidden = product(whole[0][...], matrix[:, :size], NN) + slotted[0][0]
        chance = 0.5 + 0.5 * lax.erf(hidden * (0.5**0.5))
        density = jnp.exp(-0.5 * hidden * hidden) * 0.3989422804014327
        low = (hidden * chance).astype(LOW)
        active[0] = low
        active_sent[0] = low
        slope[0] = (chance + hidden * density).astype(LOW)
        add_product(lay, step, total, low, matrix[:, size:])

        @pl.when(step == slots - 1)
        def _():
            (middle_ref,) = late()
            result[...] = (middle_ref[...] + total[...] + rows[0][...]).astype(LOW)

    return layer_call(
        lay,
        kernel,
        "dense_forward",
        [weights],
        [bias],
        [normed_two],
        [middle],
        [b_down],
        [
            low_shape(lay.shards + 1, PAD, size),
            low_shape(slots, PAD, size),
            low_shape(PAD, width),
        ],
        46,
    )


def dense_backward(lay, tangent, slope, middle, weights, gain_two):
    slots, width = lay.slots, lay.width
    size = weights[0].shape[3] // 2

    def kernel(step, weight, slotted, whole, late, rows, outs, total):
        grad_hidden, hidden_sent, up_sums, grad_middle, grad_branch = outs[:5]
        down_sums, gains, shifts, out_sums = outs[5:]

        @pl.when(step == 0)
        def _():
            down_sums[...] = jnp.sum(whole[0][...].astype(F32), axis=0, keepdims=True)
            for ref in (gains, shifts, out_sums):
                ref[...] = jnp.zeros_like(ref)

        matrix = weight(0)
        grad = product(whole[0][...], matrix[:, size:], NN).astype(LOW).astype(F32)
        grad = (grad * slotted[0][0].astype(F32)).astype(LOW)
        grad_hidden[0] = grad
        hidden_sent[0] = grad
        up_sums[0] = jnp.sum(grad.astype(F32), axis=0, keepdims=True)
        add_product(lay, step, total, grad, matrix[:, :size])

        @pl.when(step == slots - 1)
        def _():
            (middle,) = late()

            def finish(start, count):
                at = pl.ds(start, count)
                term, gain_part, shift_part = norm_back(middle[at, :], total[at, :], rows[0][...])
                sums = whole[0][at, :].astype(F32) + term
                grad_middle[at, :] = sums
                grad_branch[at, :] = sums.astype(LOW)
                gains[...] += gain_part
                shifts[...] += shift_part
                out_sums[...] += jnp.sum(sums, axis=0, keepdims=True)

            row_loop(finish)

    row = wide_shape(1, width)
    return layer_call(
        lay,
        kernel,
        "dense_backward",
        [weights],
        [slope],
        [tangent],
        [middle],
        [gain_two],
        [
            low_shape(lay.shards + 1, PAD, size),
            wide_shape(slots, 1, size),
            wide_shape(PAD, width),
            low_shape(PAD, width),
            row,
            row,
            row,
            row,
        ],
        48,
    )


def attention_backward(
    lay, grad_branch, mixed, attended, logs, entry, grad_middle, weights, gain_one
):
    slots, width = lay.slots, lay.width
    part = weights[0].shape[3] // 4

    def kernel(step, weight, slotted, whole, late, rows, outs, total):
        grad_mixed, mixed_sent, qkv_sums, grad_entry, gains, shifts = outs

        @pl.when(step == 0)
        def _():
            for ref in (gains, shifts):
                ref[...] = jnp.zeros_like(ref)

        matrix = weight(0)
        upstream = product(whole[0][...], matrix[:, 3 * part :], NN).astype(LOW)
        parts = attend_back(slotted[0][0], upstream, slotted[1][0], slotted[2][0], part)
        for spot, term in enumerate(parts):
            columns = slice(spot * part, (spot + 1) * part)
            rounded = term.astype(LOW)
            grad_mixed[0, :, columns] = rounded
            mixed_sent[0, :, columns] = rounded
            qkv_sums[0, :, columns] = jnp.sum(rounded.astype(F32), axis=0, keepdims=True)
        add_product(lay, step, total, grad_mixed[0], matrix[:, : 3 * part])

        @pl.when(step == slots - 1)
        def _():
            entry, grad_middle = late()

            def finish(start, count):
                at = pl.ds(start, count)
                term, gain_part, shift_part = norm_back(
                    entry[at, :].astype(F32), total[at, :], rows[0][...]
                )
                grad_entry[at, :] = (grad_middle[at, :] + term).astype(LOW)
                gains[...] += gain_part
                shifts[...] += shift_part

            row_loop(finish)

    row = wide_shape(1, width)
    return layer_call(
        lay,
        kernel,
        "attention_backward",
        [weights],
        [mixed, attended, logs],
        [grad_branch],
        [entry, grad_middle],
        [gain_one],
        [
            low_shape(lay.shards + 1, PAD, 3 * part),
            wide_shape(slots, 1, 3 * part),
            low_shape(PAD, width),
            row,
            row,
        ],
        48,
    )


def weight_grads(lay, slot_order, pairs, cost):
    half, block, shards, width = lay.near, lay.block, lay.shards, lay.width
    sizes = [pair[2].shape[2] for pair in pairs]
    total = sum(sizes)
    whole = pl.BlockSpec((PAD, width), lambda k, s: (0, 0), pipeline_mode=pl.Buffered(1))
    specs, operands, scratch = [], [], []
    for x, x_other, feats, feats_other in pairs:
        feature_spec = pl.BlockSpec((1, PAD, feats.shape[2]), lambda k, s: (k, 0, 0))
        specs += [whole, whole, feature_spec, feature_spec]
        operands += [x, x_other, feats, feats_other]
        scratch += [pltpu.VMEM((width, PAD), LOW)] * 2

    def kernel(_, *refs):
        far_ref, near_ref = refs[4 * len(pairs) : 4 * len(pairs) + 2]
        turned = refs[4 * len(pairs) + 2 :]

        @pl.when(pl.program_id(0) == 0)
        def _():
            for n in range(len(pairs)):
                for b in range(lay.replicas):
                    rows = slice(b * block, (b + 1) * block)
                    other = slice(lay.flip[b] * block, (lay.flip[b] + 1) * block)
                    turned[2 * n][rows, :] = refs[4 * n][:, rows].T
                    turned[2 * n + 1][rows, :] = refs[4 * n + 1][:, other].T

        start = 0
        for n, size in enumerate(sizes):
            grads = product(turned[2 * n][...], refs[4 * n + 2][0], NN) + product(
                turned[2 * n + 1][...], refs[4 * n + 3][0], NN
            )
            grads = grads.reshape(2 * half, block, size).astype(LOW)
            near_ref[:, 0, :, start : start + size] = grads[:half]
            far_ref[:, 0, :, start : start + size] = grads[half:]
            start += size

    return launch(
        lay,
        kernel,
        "weight_grads",
        [slot_order],
        operands,
        specs,
        [pl.BlockSpec((half, 1, block, total), lambda k, s: (0, s[k], 0, 0))] * 2,
        [low_shape(half, shards, block, total)] * 2,
        (shards,),
        scratch,
        28,
        cost,
    )


def add_blocks(lay, *groups, cost=10**10):
    count = min(array.shape[0] - start for group in groups for array, start in group)
    widths = [group[0][0].shape[3] for group in groups]
    middle = groups[0][0][0].shape[1:3]

    def kernel(*refs):
        at, column = 0, 0
        for group, width in zip(groups, widths):
            total = refs[at][...].astype(F32)
            for ref in refs[at + 1 : at + len(group)]:
                total = total + ref[...].astype(F32)
            refs[-1][..., column : column + width] = total.astype(LOW)
            at, column = at + len(group), column + width

    def spec(start, width):
        return pl.BlockSpec((1,) + middle + (width,), lambda i: (i + start, 0, 0, 0))

    return launch(
        lay,
        kernel,
        "add_blocks",
        [],
        [array for group in groups for array, _ in group],
        [spec(start, width) for group, width in zip(groups, widths) for _, start in group],
        [spec(0, sum(widths))],
        [jax.ShapeDtypeStruct((count,) + middle + (sum(widths),), LOW)],
        (count,),
        [],
        28,
        cost,
    )[0]


def pause(lay, cost=4 * 10**10):
    def kernel(out_ref):
        out_ref[...] = jnp.zeros_like(out_ref)

    spec = pl.BlockSpec((8, 128), lambda i: (0, 0))
    shape = jax.ShapeDtypeStruct((8, 128), F32)
    launch(lay, kernel, "pause", [], [], [], [spec], [shape], (1,), [], 8, cost)


def pack_vectors(lay, sums, blocks, slot_order, core):
    rep, block, shards = lay.replicas, lay.block, lay.shards
    assert rep == shards
    wide = sums[0][1].shape[2]
    operands = [v for layer in (0, 1) for v in (*sums[layer][0], *sums[layer][1:])]

    def kernel(s, *refs):
        keep_ref, send_ref = refs[16:]
        owner = s[rep + shards]
        keep_ref[...] = jnp.zeros_like(keep_ref)
        send_ref[...] = jnp.zeros_like(send_ref)
        here, there = refs[:8], refs[8:16]

        def chosen(n, index, mine):
            first = (owner == 0) if mine else (owner != 0)
            return jnp.where(first, here[n][index], there[n][index])

        for out_ref, mine in ((keep_ref, True), (send_ref, False)):
            for n in range(6):
                for b in range(rep):
                    columns = slice(b * block, (b + 1) * block)
                    value = chosen(n, (slice(None), columns), mine)
                    out_ref[s[b] ^ s[rep], n : n + 1, :block] = value
            for side in range(2):
                half = side ^ owner
                for k in range(shards):
                    slot = side * shards + k
                    ups = chosen(6, slot, mine)
                    parts = chosen(7, slot, mine)
                    out_ref[k, pl.ds(8 + half, 1), :] = ups
                    out_ref[k, pl.ds(6 + half, 1), : parts.shape[1]] = parts

    def spec(array):
        return pl.BlockSpec(array.shape, lambda i, s, n=array.ndim: (0,) * n)

    scalars = jnp.concatenate([blocks, slot_order, core[None]])
    shape = jax.ShapeDtypeStruct((shards, 16, wide), F32)
    keep, send = launch(
        lay,
        kernel,
        "pack_vectors",
        [scalars],
        operands,
        [spec(v) for v in operands],
        [pl.BlockSpec(shape.shape, lambda i, s: (0, 0, 0))] * 2,
        [shape] * 2,
        (1,),
        [],
        8,
    )
    return keep, send


def shards(
    boundary_in,
    counts,
    w_qkv,
    b_qkv,
    w_out,
    b_out,
    w_up,
    b_up,
    w_down,
    b_down,
    norm1_gain,
    norm1_shift,
    norm2_gain,
    norm2_shift,
):
    width = boundary_in.shape[4]
    sizes = {axis: lax.axis_size(axis) for axis in ALL_AXES}
    lay = Layout(sizes, width)
    core = lax.axis_index("section").astype(jnp.int32)
    shard = lax.axis_index("shard").astype(jnp.int32)
    replica = lax.axis_index("replica").astype(jnp.int32)
    on_first = core == 0
    heads_wide = w_qkv.shape[3]
    part = heads_wide // 2
    ff_part = w_up.shape[2] // 2
    positions = jnp.arange(lay.replicas, dtype=jnp.int32)
    flips = jnp.asarray(lay.flip, jnp.int32)
    blocks = jnp.where(on_first, positions, flips) ^ replica
    inverse_blocks = jnp.where(on_first, positions ^ replica, flips[positions ^ replica])
    halves = jnp.arange(2, dtype=jnp.int32) ^ core
    scalars = jnp.concatenate([blocks, halves, core[None]])

    slot_order = jnp.arange(lay.shards, dtype=jnp.int32) ^ shard

    raw_qkv = w_qkv[0].reshape(width, 6 * part)
    raw_out, raw_up, raw_down = w_out[0], w_up[0], w_down[0]
    split_pieces = first_pieces(lay, raw_qkv, raw_out, raw_up, raw_down, scalars)
    first, second = [], []
    for piece, sent in zip(split_pieces[:2], split_pieces[2:]):
        other = lay.across_cores(sent)
        first.append(jnp.where(on_first, piece, other))
        second.append(jnp.where(on_first, other, piece))
    pieces = first + second
    pictures = boundary_in[0, :, 0]
    received = lay.across_cores(pictures)
    live = (shard < counts[replica, core]).astype(F32)[None]
    gather = Gather(lay, slot_order, pieces)
    gather.start(0)
    image, cot = arrange_images(lay, pictures, received, blocks, core, live)

    raws = (raw_qkv, raw_out, raw_up, raw_down)
    raws_other = [lay.across_cores(raw) for raw in raws]
    own_attention = arrange_attention(lay, raws[:2], raws_other[:2], scalars)

    packed = jnp.concatenate(
        [v[0] for v in (b_out, b_down, norm1_gain, norm1_shift, norm2_gain, norm2_shift)]
        + [b_qkv.reshape(-1), b_up.reshape(-1)]
    )
    packed_other = lay.across_cores(packed)
    both = jnp.stack(
        [jnp.where(on_first, packed, packed_other), jnp.where(on_first, packed_other, packed)]
    )
    wide = both[:, : 6 * width].reshape(2, 6, lay.replicas, lay.block)
    wide = jnp.take(wide, blocks, axis=2).reshape(2, 6, 1, width).astype(F32)
    split = both[:, 6 * width :]
    split = jnp.stack([split] + [lay.along_shard(split, k) for k in range(1, lay.shards)])
    split_qkv = split[:, :, : 4 * part].reshape(lay.shards, 2, 2, 2, part)
    split_qkv = jnp.take(split_qkv, halves, axis=3).transpose(1, 3, 0, 2, 4)
    split_qkv = split_qkv.reshape(2, lay.slots, 2, part)
    bias_qkv = jnp.concatenate(
        [split_qkv[:, :, 0], jnp.zeros_like(split_qkv[:, :, 0]), split_qkv[:, :, 1]], axis=-1
    ).reshape(2, lay.slots, 1, 3 * part).astype(F32)
    bias_up = split[:, :, 4 * part :].reshape(lay.shards, 2, 2, ff_part)
    bias_up = jnp.take(bias_up, halves, axis=2).transpose(1, 2, 0, 3)
    bias_up = bias_up.reshape(2, lay.slots, 1, ff_part).astype(F32)

    kept, weights = [], []
    entry = image
    gather.step(0)
    gather.start(1)
    gather.step(0)
    gather.start(2)
    gather.step(1)
    gather.start(3)
    w_attention = gather.finish(0, own_attention[0])
    for layer in range(2):
        vec_out, vec_down, gain_one, shift_one, gain_two, shift_two = wide[layer]
        normed, mixed, attended, logs, middle, normed_two = attention_forward(
            lay,
            entry,
            w_attention,
            bias_qkv[layer],
            (gain_one, shift_one, vec_out, gain_two, shift_two),
        )
        exchanged = [
            lay.across_cores(value) for value in (normed, normed_two, attended[lay.shards :])
        ]
        if layer == 0:
            gather.step(1)
            gather.step(2)
            lay.absorb(*exchanged)
            own_dense = arrange_dense(lay, raws[2:], raws_other[2:], scalars)
            gather.step(3)
            w_dense = gather.finish(1, own_dense[0])
            gather.step(2)
            pause(lay)
        else:
            w_dense = gather.finish(3, own_dense[1])
            lay.absorb(kept[0][-1][-1])
            pause(lay)
        active, active_sent, slope, result = dense_forward(
            lay,
            normed_two,
            middle,
            w_dense,
            bias_up[layer],
            vec_down,
        )
        weights.append((w_attention, w_dense))
        exchanged.append(lay.across_cores(active_sent))
        if layer == 0:
            w_attention = gather.finish(2, own_attention[1])
            gather.step(3)
            pause(lay)
        kept.append(
            (entry, normed, mixed, attended, logs, middle, normed_two, active, slope, exchanged)
        )
        entry = result

    terms, sums, vector_sums, latest = {}, {}, {}, {}

    def begin(name, *pairs, cost=1000):
        far, near = weight_grads(lay, slot_order, pairs, cost)
        arrived = lay.along_bit(far, lay.bits - 1)
        terms[name] = [(near, 0), (arrived, 0)]

    def halve(name, cost=10**10):
        for bit in range(lay.bits - 2, -1, -1):
            split = 1 << bit
            group = [(array, start + split) for array, start in terms[name]]
            sent = add_blocks(lay, group, cost=cost)
            terms[name] = terms[name] + [(lay.along_bit(sent, bit), 0)]

    def collect(names, direct, cost=10**10):
        total = add_blocks(lay, *(terms[name] for name in names), cost=cost)[0]
        if direct:
            latest[names] = lax.all_to_all(total, "shard", 0, 0, tiled=True)
        else:
            latest[names] = lax.psum_scatter(total, "shard", scatter_dimension=0)[None]

    def settle(*all_names):
        for names, total in zip(all_names, lay.hold(*(latest[names] for names in all_names))):
            spread(names, total)

    def spread(names, total):
        total = jnp.sum(total.astype(F32), axis=0)
        at = 0
        for name in names:
            size = terms[name][0][0].shape[3]
            sums[name] = total[:, at : at + size]
            at += size

    tangent = cot
    for layer in (1, 0):
        tangent_other = lay.across_cores(tangent)
        w_attention, w_dense = weights[layer]
        vec_out, vec_down, gain_one, shift_one, gain_two, shift_two = wide[layer]
        entry_in, normed, mixed, attended, logs, middle, normed_two, active, slope, other = kept[layer]
        normed_other, normed_two_other, attended_other, active_other = other
        begin((layer, "down"), (tangent, tangent_other, active, active_other))
        (
            grad_hidden,
            hidden_sent,
            up_sums,
            grad_middle,
            grad_branch,
            down_sums,
            gain_two_sum,
            shift_two_sum,
            out_sums,
        ) = dense_backward(lay, tangent, slope, middle, w_dense, gain_two)
        branch_other, hidden_other = lay.across_cores(grad_branch), lay.across_cores(hidden_sent)
        out_pair = (grad_branch, branch_other, attended, attended_other)
        if layer == 1:
            halve((1, "down"))
        else:
            settle(((1, "down"),))
            collect(((1, "out"), (1, "up")), False)
            halve((1, "qkv"))
        begin((layer, "out"), out_pair, cost=4 * 10**10)
        if layer == 0:
            halve((0, "down"))
        begin((layer, "up"), (normed_two, normed_two_other, grad_hidden, hidden_other))
        if layer == 0:
            collect(((1, "qkv"), (0, "down")), True)
        grad_mixed, mixed_sent, qkv_sums, grad_entry, gain_one_sum, shift_one_sum = (
            attention_backward(
                lay,
                grad_branch,
                mixed,
                attended,
                logs,
                entry_in,
                grad_middle,
                w_attention,
                gain_one,
            )
        )
        tangent = grad_entry
        mixed_other = lay.across_cores(mixed_sent)
        vector_sums[layer] = (
            [out_sums, down_sums, gain_one_sum, shift_one_sum, gain_two_sum, shift_two_sum],
            up_sums,
            qkv_sums,
        )
        if layer == 1:
            collect(((1, "down"),), False)
        if layer == 0:
            keep, send = pack_vectors(lay, vector_sums, blocks, slot_order, core)
            send = lay.across_cores(send)
        halve((layer, "out"))
        if layer == 0:
            (send,) = lay.hold(send)
            summed = keep + send
            coming = [lay.along_shard(summed[k], k) for k in range(1, lay.shards)]
        halve((layer, "up"))
        if layer == 0:
            settle(((1, "out"), (1, "up")), ((1, "qkv"), (0, "down")))
            pause(lay, 10**10)
        begin((layer, "qkv"), (normed, normed_other, grad_mixed, mixed_other))
    summed = sum(lay.hold(*coming), summed[0])
    coming = lay.along_bit_plain(summed, 0)
    collect(((0, "out"), (0, "up")), False, cost=1000)
    halve((0, "qkv"), cost=1000)
    for bit in range(lay.bits):
        (coming,) = lay.hold(coming)
        summed = summed + coming
        if bit + 1 < lay.bits:
            coming = lay.along_bit_plain(summed, bit + 1)
        if bit == 0:
            back = restore_image(lay, tangent, blocks, jnp.ones((1,), F32))
            ahead = restore_image(lay, entry, blocks, live)
    collect(((0, "qkv"),), True, cost=1000)
    last = (((0, "out"), (0, "up")), ((0, "qkv"),))
    for names, total in zip(last, lax.optimization_barrier([latest[names] for names in last])):
        spread(names, total)

    def to_owner(first, second):
        keep = jnp.where(on_first, first, second)
        other = lay.across_cores(jnp.where(on_first, second, first))
        return jnp.where(on_first, keep, other), jnp.where(on_first, other, keep)

    down_halves = to_owner(sums[0, "down"], sums[1, "down"])
    up_halves = to_owner(sums[0, "up"], sums[1, "up"])
    out_halves = to_owner(sums[0, "out"], sums[1, "out"])
    qkv_halves = to_owner(sums[0, "qkv"], sums[1, "qkv"])
    grad_w_down = jnp.concatenate(down_halves, axis=1).T[None]
    grad_w_up = jnp.concatenate(up_halves, axis=1)[None]
    grad_w_qkv = jnp.stack(
        [half.reshape(-1, 3, part) for half in qkv_halves], axis=2
    ).reshape(1, lay.block, 3, heads_wide)
    grad_w_out = jnp.concatenate(out_halves, axis=1).T[None]

    share = lay.block // lay.replicas
    model = lax.dynamic_slice_in_dim(summed[:6, : lay.block], replica * share, share, 1)
    vectors = [model[i : i + 1] for i in range(6)]
    parts = summed[6:8, : 3 * part].reshape(2, 3, part)
    parts = jnp.stack([parts[:, 0], parts[:, 2]]).reshape(2, 2 * part)
    grad_b_qkv = lax.dynamic_slice_in_dim(parts, replica * share, share, 1)[None]
    share_up = 2 * ff_part // lay.replicas
    ups = summed[8:10, :ff_part].reshape(1, 2 * ff_part)
    grad_b_up = lax.dynamic_slice_in_dim(ups, replica * share_up, share_up, 1)

    keep = jnp.where(on_first, back, ahead)
    other = lay.across_cores(jnp.where(on_first, ahead, back))
    boundary_out = jnp.stack([jnp.where(on_first, keep, other), jnp.where(on_first, other, keep)])
    boundary_out = boundary_out[None, :, None]
    return (
        boundary_out,
        grad_w_qkv,
        grad_b_qkv,
        grad_w_out,
        vectors[0],
        grad_w_up,
        grad_b_up,
        grad_w_down,
        vectors[1],
        vectors[2],
        vectors[3],
        vectors[4],
        vectors[5],
    )


def solution(mesh):
    spread = P("section", ("shard", "replica"))
    return jax.shard_map(
        shards,
        mesh=mesh,
        in_specs=(
            P("section", None, ("shard", "replica"), None, None),
            P(),
            P("section", None, None, "shard"),
            P("section", None, "shard"),
            P("section", "shard", None),
            P("section", None),
            P("section", None, "shard"),
            P("section", "shard"),
            P("section", "shard", None),
            P("section", None),
            P("section", None),
            P("section", None),
            P("section", None),
            P("section", None),
        ),
        out_specs=(
            P("section", None, ("shard", "replica"), None, None),
            P("section", "replica", None, "shard"),
            P("section", None, ("shard", "replica")),
            P("section", "shard", "replica"),
            spread,
            P("section", "replica", "shard"),
            spread,
            P("section", "shard", "replica"),
            spread,
            spread,
            spread,
            spread,
            spread,
        ),
        check_vma=False,
    )
```

```python
import functools

import jax
import jax.numpy as jnp
from jax import lax
from jax.experimental import pallas as pl
from jax.experimental.pallas import tpu as pltpu
from jax.sharding import PartitionSpec as P

HEAD = 64
SEQ = 577
PAD = 592
CHUNK = 144
LOW = jnp.bfloat16
F32 = jnp.float32
ALL_AXES = ("section", "shard", "replica")
NT = (((1,), (1,)), ((), ()))
NN = (((1,), (0,)), ((), ()))
TN = (((0,), (0,)), ((), ()))


def reverse_bits(value, bits):
    flipped = 0
    for spot in range(bits):
        flipped |= ((value >> spot) & 1) << (bits - 1 - spot)
    return flipped


def product(left, right, dims):
    return lax.dot_general(left, right, dims, preferred_element_type=F32)


def row_loop(body):
    whole = PAD // CHUNK

    def step(index, carry):
        body(pl.multiple_of(index * CHUNK, 16), CHUNK)
        return carry

    lax.fori_loop(0, whole, step, 0)
    if PAD % CHUNK:
        body(whole * CHUNK, PAD % CHUNK)


def params(megabytes=48):
    return pltpu.CompilerParams(vmem_limit_bytes=megabytes * 2**20)


def launch(
    lay, kernel, name, scalars, operands, in_specs, out_specs, out_shape, grid, scratch, megabytes, cost=1000
):
    tokens = lay.after
    count = len(scalars) + len(operands)

    def ordered(*refs):
        rest = refs[count + len(tokens) :]
        rest[len(out_shape)][...] = jnp.zeros((8, 128), F32)
        kernel(*refs[:count], *rest[: len(out_shape)], *rest[len(out_shape) + 1 :])

    token_spec = pl.BlockSpec((8, 128), lambda *_: (0, 0))
    results = pl.pallas_call(
        ordered,
        grid_spec=pltpu.PrefetchScalarGridSpec(
            num_scalar_prefetch=len(scalars),
            grid=grid,
            in_specs=list(in_specs) + [pl.BlockSpec(memory_space=pl.ANY)] * len(tokens),
            out_specs=list(out_specs) + [token_spec],
            scratch_shapes=scratch,
        ),
        out_shape=list(out_shape) + [jax.ShapeDtypeStruct((8, 128), F32)],
        compiler_params=params(megabytes),
        cost_estimate=pl.CostEstimate(flops=cost, bytes_accessed=2**18, transcendentals=0),
        name=name,
    )(*scalars, *operands, *tokens)
    lay.after = [results[-1]]
    return results[:-1]


def normalized(values):
    center = values - jnp.mean(values, axis=-1, keepdims=True)
    spread = jnp.mean(center * center, axis=-1, keepdims=True)
    inverse = lax.rsqrt(spread + 1e-06)
    return center * inverse, inverse


class Layout:
    def __init__(self, mesh_shape, width):
        self.shards = mesh_shape["shard"]
        self.replicas = mesh_shape["replica"]
        self.bits = self.replicas.bit_length() - 1
        self.width = width
        self.block = width // self.replicas
        self.flip = [reverse_bits(b, self.bits) for b in range(self.replicas)]
        self.near = self.replicas // 2
        self.slots = 2 * self.shards
        self.after = []

    def absorb(self, *values):
        for value in values:
            corner = value.reshape((-1,) + value.shape[-2:])[0, :8, :128]
            self.after.append(corner)

    def hold(self, *values):
        values, self.after = lax.optimization_barrier((values, self.after))
        return values

    def across_cores(self, value):
        return lax.ppermute(value, "section", [(0, 1), (1, 0)])

    def along_shard(self, value, slot):
        return lax.ppermute(value, "shard", [(i, i ^ slot) for i in range(self.shards)])

    def along_bit_plain(self, value, bit):
        route = [(i, i ^ (1 << bit)) for i in range(self.replicas)]
        return lax.ppermute(value, "replica", route)

    def along_bit(self, value, bit):
        route = []
        for core in range(2):
            physical = bit if core == 0 else self.bits - 1 - bit
            for shard in range(self.shards):
                base = (core * self.shards + shard) * self.replicas
                for replica in range(self.replicas):
                    route.append((base + replica, base + (replica ^ (1 << physical))))
        return lax.ppermute(value, ALL_AXES, route)


def arrange_images(lay, mine, received, blocks, core, live):
    width, block = lay.width, lay.block

    def kernel(scalars, live_ref, mine_ref, other_ref, image_ref, cot_ref):
        here = mine_ref[0]
        there = other_ref[0]
        first = scalars[lay.replicas] == 0
        image = jnp.where(first, here, there)
        cot = jnp.where(first, there, here).astype(F32) * live_ref[0]
        image_ref[...] = jnp.zeros_like(image_ref)
        cot_ref[...] = jnp.zeros_like(cot_ref)
        image_ref[0:SEQ, :] = image
        cot_ref[0:SEQ, :] = cot.astype(LOW)

    scalars = jnp.concatenate([blocks, core[None]]).astype(jnp.int32)
    shape = jax.ShapeDtypeStruct((PAD, width), LOW)
    whole = pl.BlockSpec((1, SEQ, block), lambda b, s: (s[lay.replicas], 0, s[b]))
    return launch(
        lay,
        kernel,
        "arrange_images",
        [scalars],
        [live, mine, received],
        [pl.BlockSpec(memory_space=pltpu.SMEM), whole, whole],
        [pl.BlockSpec((PAD, block), lambda b, s: (0, b))] * 2,
        [shape, shape],
        (lay.replicas,),
        [],
        24,
    )


def restore_image(lay, values, blocks, scale):
    def kernel(scalars, scale_ref, in_ref, out_ref):
        out_ref[...] = (in_ref[0:SEQ, :].astype(F32) * scale_ref[0]).astype(LOW)

    return launch(
        lay,
        kernel,
        "restore_image",
        [blocks],
        [scale, values],
        [
            pl.BlockSpec(memory_space=pltpu.SMEM),
            pl.BlockSpec((PAD, lay.block), lambda b, s: (0, b)),
        ],
        [pl.BlockSpec((SEQ, lay.block), lambda b, s: (0, s[b]))],
        [jax.ShapeDtypeStruct((SEQ, lay.width), LOW)],
        (lay.replicas,),
        [],
        16,
    )[0]


def chosen_half(flag, low, high):
    return jnp.where(flag == 0, low, high)


def arrange_attention(lay, mine, received, scalars):
    rep, block = lay.replicas, lay.block
    part = mine[1].shape[0] // 2

    def kernel(s, qkv_mine, qkv_other, out_mine, out_other, first_ref, second_ref):
        first = s[rep + 2] == 0
        half = s[rep + pl.program_id(0)]

        def columns(ref, t):
            start = 2 * t * part
            return chosen_half(
                half, ref[:, start : start + part], ref[:, start + part : start + 2 * part]
            )

        for t in range(3):
            here, there = columns(qkv_mine, t), columns(qkv_other, t)
            first_ref[0, 0, :, t * part : (t + 1) * part] = jnp.where(first, here, there)
            second_ref[0, 0, :, t * part : (t + 1) * part] = jnp.where(first, there, here)
        here, there = out_mine[...].T, out_other[...].T
        first_ref[0, 0, :, 3 * part :] = jnp.where(first, here, there)
        second_ref[0, 0, :, 3 * part :] = jnp.where(first, there, here)

    shape = jax.ShapeDtypeStruct((2, rep, block, 4 * part), LOW)
    qkv_spec = pl.BlockSpec((block, 6 * part), lambda p, b, s: (s[b], 0))
    out_spec = pl.BlockSpec((part, block), lambda p, b, s: (s[rep + p], s[b]))
    return launch(
        lay,
        kernel,
        "arrange_attention",
        [scalars],
        [mine[0], received[0], mine[1], received[1]],
        [qkv_spec, qkv_spec, out_spec, out_spec],
        [pl.BlockSpec((1, 1, block, 4 * part), lambda p, b, s: (p, b, 0, 0))] * 2,
        [shape, shape],
        (2, rep),
        [],
        16,
    )


def arrange_dense(lay, mine, received, scalars):
    rep, block = lay.replicas, lay.block
    part = mine[0].shape[1] // 2

    def kernel(s, up_mine, up_other, down_mine, down_other, first_ref, second_ref):
        first = s[rep + 2] == 0
        here, there = up_mine[...], up_other[...]
        first_ref[0, 0, :, :part] = jnp.where(first, here, there)
        second_ref[0, 0, :, :part] = jnp.where(first, there, here)
        here, there = down_mine[...].T, down_other[...].T
        first_ref[0, 0, :, part:] = jnp.where(first, here, there)
        second_ref[0, 0, :, part:] = jnp.where(first, there, here)

    shape = jax.ShapeDtypeStruct((2, rep, block, 2 * part), LOW)
    up_spec = pl.BlockSpec((block, part), lambda p, b, s: (s[b], s[rep + p]))
    down_spec = pl.BlockSpec((part, block), lambda p, b, s: (s[rep + p], s[b]))
    return launch(
        lay,
        kernel,
        "arrange_dense",
        [scalars],
        [mine[0], received[0], mine[1], received[1]],
        [up_spec, up_spec, down_spec, down_spec],
        [pl.BlockSpec((1, 1, block, 2 * part), lambda p, b, s: (p, b, 0, 0))] * 2,
        [shape] * 2,
        (2, rep),
        [],
        16,
    )


def first_pieces(lay, qkv, out, up, down, scalars):
    rep, block = lay.replicas, lay.block
    part, wide = out.shape[0] // 2, up.shape[1] // 2

    def kernel(s, qkv_ref, out_ref, up_ref, down_ref, *outs):
        core = s[rep + 2]
        for flag, attention_ref, dense_ref in ((core, *outs[:2]), (1 - core, *outs[2:])):
            for t in range(3):
                start = 2 * t * part
                attention_ref[:, t * part : (t + 1) * part] = chosen_half(
                    flag,
                    qkv_ref[:, start : start + part],
                    qkv_ref[:, start + part : start + 2 * part],
                )
            attention_ref[:, 3 * part :] = chosen_half(flag, out_ref[:part], out_ref[part:]).T
            dense_ref[:, :wide] = chosen_half(flag, up_ref[:, :wide], up_ref[:, wide:])
            dense_ref[:, wide:] = chosen_half(flag, down_ref[:wide], down_ref[wide:]).T

    attention_shape = jax.ShapeDtypeStruct((block, 4 * part), LOW)
    dense_shape = jax.ShapeDtypeStruct((block, 2 * wide), LOW)
    attention_spec = pl.BlockSpec((block, 4 * part), lambda i, s: (0, 0))
    dense_spec = pl.BlockSpec((block, 2 * wide), lambda i, s: (0, 0))
    return launch(
        lay,
        kernel,
        "first_pieces",
        [scalars],
        [qkv, out, up, down],
        [
            pl.BlockSpec((block, 6 * part), lambda i, s: (s[0], 0)),
            pl.BlockSpec((2 * part, block), lambda i, s: (0, s[0])),
            pl.BlockSpec((block, 2 * wide), lambda i, s: (s[0], 0)),
            pl.BlockSpec((2 * wide, block), lambda i, s: (0, s[0])),
        ],
        [attention_spec, dense_spec] * 2,
        [attention_shape, dense_shape] * 2,
        (1,),
        [],
        16,
    )


def pick_slots(lay, gathered, slot_order):
    rows, columns = gathered.shape[1:]

    def kernel(_, in_ref, out_ref):
        out_ref[0] = in_ref[...]

    return launch(
        lay,
        kernel,
        "pick_slots",
        [slot_order],
        [gathered],
        [pl.BlockSpec((1, rows, columns), lambda k, s: (s[k + 1], 0, 0))],
        [pl.BlockSpec((1, 1, rows, columns), lambda k, s: (0, k, 0, 0))],
        [jax.ShapeDtypeStruct((1, lay.shards - 1, rows, columns), LOW)],
        (lay.shards - 1,),
        [],
        8,
    )[0]


def join(lay, first, second):
    count, rows = first.shape[0], first.shape[1]
    shape = (2 * count,) + first.shape[1:]
    block = (1, rows) + first.shape[2:]

    def kernel(first_ref, second_ref, out_ref):
        step = pl.program_id(0)

        @pl.when(step < count)
        def _():
            out_ref[...] = first_ref[...]

        @pl.when(step >= count)
        def _():
            out_ref[...] = second_ref[...]

    return launch(
        lay,
        kernel,
        "join",
        [],
        [first, second],
        [
            pl.BlockSpec(block, lambda i: (jnp.minimum(i, count - 1), 0, 0, 0)),
            pl.BlockSpec(block, lambda i: (jnp.maximum(i - count, 0), 0, 0, 0)),
        ],
        [pl.BlockSpec(block, lambda i: (i, 0, 0, 0))],
        [jax.ShapeDtypeStruct(shape, LOW)],
        (2 * count,),
        [],
        16,
    )[0]


def copied(lay, value):
    def kernel(in_ref, out_ref):
        out_ref[...] = in_ref[...]

    spec = pl.BlockSpec(value.shape, lambda i: (0, 0))
    shape = jax.ShapeDtypeStruct(value.shape, value.dtype)
    return launch(lay, kernel, "copied", [], [value], [spec], [spec], [shape], (1,), [], 8)[0]


class Gather:
    def __init__(self, lay, slot_order, pieces):
        self.lay, self.pieces, self.slot_order = lay, pieces, slot_order
        self.state = [None] * len(pieces)
        self.done = [0] * len(pieces)

    def start(self, n):
        piece = self.pieces[n] if n == 0 else copied(self.lay, self.pieces[n])
        self.state[n] = lax.all_gather(piece, "shard")

    def step(self, n):
        lay = self.lay
        if self.done[n] == 0:
            near = pick_slots(lay, self.state[n], self.slot_order)
        else:
            near = join(lay, *self.state[n])
        self.state[n] = (near, lay.along_bit(near, self.done[n]))
        self.done[n] += 1

    def finish(self, n, own):
        lay = self.lay
        while self.done[n] < lay.bits:
            self.step(n)
        near, far = self.state[n]
        (far,) = lay.hold(far)
        return (own, near, far, lay.across_cores(near), lay.across_cores(far))


def fetch_weights(lay, refs, held, sems, slot):
    own, near, far, near_other, far_other = refs
    half = lay.near
    side, k = divmod(slot, lay.shards)

    def start(source, target):
        pltpu.make_async_copy(source, target, sems.at[slot]).start()

    if k == 0:
        start(own.at[side], held.at[slot])
    elif side == 0:
        start(near.at[:, k - 1], held.at[slot, 0:half])
        start(far.at[:, k - 1], held.at[slot, half : 2 * half])
    else:
        for b in range(half):
            start(near_other.at[b, k - 1], held.at[slot, lay.flip[b]])
            start(far_other.at[b, k - 1], held.at[slot, lay.flip[half + b]])


def await_weights(held, sems, slot):
    pltpu.make_async_copy(held.at[slot], held.at[slot], sems.at[slot]).wait()


def flat(block):
    return block.reshape(block.shape[0] * block.shape[1], block.shape[2])


def layer_call(lay, kernel, name, weights, slotted, whole, late, rows, outs, megabytes):
    slots, width, shards = lay.slots, lay.width, lay.shards
    once = dict(pipeline_mode=pl.Buffered(1))

    def own_half(i):
        return (jnp.minimum(i, shards), 0, 0)

    def other_half(i):
        return (jnp.where(i < shards, shards, i - shards), 0, 0)

    def spec(shape, **mode):
        if len(shape) == 3:
            return pl.BlockSpec((1,) + shape[1:], lambda i: (i, 0, 0))
        return pl.BlockSpec(shape, lambda i: (0, 0), **mode)

    out_specs, out_shape = [], []
    for o in outs:
        if len(o.shape) == 3 and o.shape[0] == shards + 1:
            out_specs += [pl.BlockSpec((1,) + o.shape[1:], m) for m in (own_half, other_half)]
            out_shape += [o, o]
        else:
            out_specs.append(spec(o.shape))
            out_shape.append(o)
    outs = out_shape
    anywhere = pl.BlockSpec(memory_space=pltpu.HBM)
    counts = [5 * len(weights), len(slotted), len(whole), len(late), len(rows), len(outs)]

    def body(*refs):
        groups, at = [], 0
        for count in counts + [1, len(weights), len(weights), len(late)]:
            groups.append(refs[at : at + count])
            at += count
        arrays, slot_refs, whole_refs, late_refs, row_refs, out_refs = groups[:6]
        (total,), held, sems, late_held = groups[6:10]
        late_sem = refs[at] if late else None
        step = pl.program_id(0)

        def late_copy(n):
            return pltpu.make_async_copy(late_refs[n], late_held[n], late_sem.at[n])

        @pl.when(step == 0)
        def _():
            for slot in range(slots):
                for n in range(len(weights)):
                    fetch_weights(lay, arrays[5 * n : 5 * n + 5], held[n], sems[n], slot)
            for n in range(len(late)):
                late_copy(n).start()

        def weight(n):
            await_weights(held[n], sems[n], step)
            return flat(held[n][step])

        def late_values():
            for n in range(len(late)):
                late_copy(n).wait()
            return late_held

        kernel(step, weight, slot_refs, whole_refs, late_values, row_refs, out_refs, total)

    arrays = [array for matrix in weights for array in matrix]
    scratch = [pltpu.VMEM((PAD, width), F32)]
    scratch += [pltpu.VMEM((slots,) + matrix[0].shape[1:], LOW) for matrix in weights]
    scratch += [pltpu.SemaphoreType.DMA((slots,)) for _ in weights]
    scratch += [pltpu.VMEM(a.shape, a.dtype) for a in late]
    if late:
        scratch.append(pltpu.SemaphoreType.DMA((len(late),)))
    return launch(
        lay,
        body,
        name,
        [],
        [*arrays, *slotted, *whole, *late, *rows],
        [anywhere] * len(arrays)
        + [spec(a.shape) for a in slotted]
        + [spec(a.shape, **once) for a in whole]
        + [anywhere] * len(late)
        + [spec(a.shape, **once) for a in rows],
        out_specs,
        out_shape,
        (slots,),
        scratch,
        megabytes,
    )


def add_product(lay, step, total, acts, matrix):
    for b in range(lay.replicas):
        columns = slice(b * lay.block, (b + 1) * lay.block)
        term = product(acts, matrix[columns], NT)
        total[:, columns] = jnp.where(step == 0, 0.0, total[:, columns]) + term


def low_shape(*shape):
    return jax.ShapeDtypeStruct(shape, LOW)


def wide_shape(*shape):
    return jax.ShapeDtypeStruct(shape, F32)


def mask_keys(scores, low):
    edge = SEQ // 16 * 16
    valid = lax.broadcasted_iota(jnp.int32, (PAD - edge, 1), 0) < SEQ - edge
    return jnp.concatenate([scores[:edge], jnp.where(valid, scores[edge:], low)], axis=0)


def attend(block, part):
    query, keys, values = block[:, :part], block[:, part : 2 * part], block[:, 2 * part :]
    heads = range(part // HEAD)
    lanes = lax.broadcasted_iota(jnp.int32, (1, part), 1) // HEAD
    query = query * HEAD ** (-0.5)
    turned = values.T
    ones = jnp.ones((16, PAD), LOW)
    scores = [product(keys, jnp.where(lanes == h, query, 0), NT) for h in heads]
    scores = [mask_keys(score, -1e30) for score in scores]
    peaks = [jnp.max(score, axis=0, keepdims=True) for score in scores]
    weights = [jnp.exp(score - peak).astype(LOW) for score, peak in zip(scores, peaks)]
    sums = [
        product(jnp.concatenate([turned[h * HEAD : (h + 1) * HEAD], ones], axis=0), weights[h], NN)
        for h in heads
    ]
    result = jnp.concatenate([s[:HEAD] / s[HEAD : HEAD + 1] for s in sums], axis=0).T
    spot = lax.broadcasted_iota(jnp.int32, (8, 1), 0)
    logs = jnp.zeros((8, PAD), F32)
    for h in heads:
        logs = jnp.where(spot == h, peaks[h] + jnp.log(sums[h][HEAD : HEAD + 1]), logs)
    return result.astype(LOW), logs


def attend_back(block, grads, attended, logs, part):
    query, keys, values = block[:, :part], block[:, part : 2 * part], block[:, 2 * part :]
    heads = range(part // HEAD)
    lanes = lax.broadcasted_iota(jnp.int32, (1, part), 1) // HEAD
    wide = lax.broadcasted_iota(jnp.int32, (1, 128), 1)
    query = query * HEAD ** (-0.5)

    def pick(h, array):
        return jnp.where(lanes == h, array, 0)

    along = grads.astype(F32) * attended.astype(F32)
    inner = jnp.zeros((PAD, 128), F32)
    for h in heads:
        inner = jnp.where(wide == h, jnp.sum(pick(h, along), axis=-1, keepdims=True), inner)
    inner = inner.T
    scores = [product(keys, pick(h, query), NT) for h in heads]
    slopes = [product(values, pick(h, grads), NT) for h in heads]
    chances = [mask_keys(jnp.exp(scores[h] - logs[h : h + 1]), 0.0) for h in heads]
    grad_scores = [(chances[h] * (slopes[h] - inner[h : h + 1])).astype(LOW) for h in heads]
    low = [chance.astype(LOW) for chance in chances]
    value_terms = [product(low[h], grads, NN) for h in heads]
    key_terms = [product(grad_scores[h], query, NN) for h in heads]
    turned = keys.T
    query_terms = [
        product(turned[h * HEAD : (h + 1) * HEAD], grad_scores[h], NN) for h in heads
    ]

    def merge(terms):
        result = terms[0]
        for h in heads:
            result = jnp.where(lanes == h, terms[h], result)
        return result

    return (
        jnp.concatenate(query_terms, axis=0).T * HEAD ** (-0.5),
        merge(key_terms),
        merge(value_terms),
    )


def norm_back(values, grads, gain):
    values, inverse = normalized(values)
    slope = grads * gain
    mean = jnp.mean(slope, axis=-1, keepdims=True)
    along = jnp.mean(slope * values, axis=-1, keepdims=True)
    term = inverse * (slope - mean - values * along)
    return (
        term,
        jnp.sum(grads * values, axis=0, keepdims=True),
        jnp.sum(grads, axis=0, keepdims=True),
    )


def attention_forward(lay, entry, weights, bias, rows):
    slots, width = lay.slots, lay.width
    part = weights[0].shape[3] // 4

    def kernel(step, weight, slotted, whole, late, rows, outs, total):
        normed, mixed, attended, logs, middle, normed_two = outs

        @pl.when(step == 0)
        def _():
            def norm_rows(start, count):
                values, _ = normalized(whole[0][pl.ds(start, count), :].astype(F32))
                normed[pl.ds(start, count), :] = (values * rows[0][...] + rows[1][...]).astype(LOW)

            row_loop(norm_rows)

        matrix = weight(0)
        block = (product(normed[...], matrix[:, : 3 * part], NN) + slotted[0][0]).astype(LOW)
        mixed[0] = block
        result, log_rows = attend(block, part)
        attended[0] = result
        logs[0] = log_rows
        add_product(lay, step, total, result, matrix[:, 3 * part :])

        @pl.when(step == slots - 1)
        def _():
            def finish(start, count):
                at = pl.ds(start, count)
                sums = whole[0][at, :].astype(F32) + total[at, :] + rows[2][...]
                middle[at, :] = sums
                values, _ = normalized(sums)
                normed_two[at, :] = (values * rows[3][...] + rows[4][...]).astype(LOW)

            row_loop(finish)

    return layer_call(
        lay,
        kernel,
        "attention_forward",
        [weights],
        [bias],
        [entry],
        [],
        rows,
        [
            low_shape(PAD, width),
            low_shape(slots, PAD, 3 * part),
            low_shape(slots, PAD, part),
            wide_shape(slots, 8, PAD),
            wide_shape(PAD, width),
            low_shape(PAD, width),
        ],
        40,
    )


def dense_forward(lay, normed_two, middle, weights, bias, b_down):
    slots, width = lay.slots, lay.width
    size = weights[0].shape[3] // 2

    def kernel(step, weight, slotted, whole, late, rows, outs, total):
        active, active_sent, slope, result = outs
        matrix = weight(0)
        hidden = product(whole[0][...], matrix[:, :size], NN) + slotted[0][0]
        chance = 0.5 + 0.5 * lax.erf(hidden * (0.5**0.5))
        density = jnp.exp(-0.5 * hidden * hidden) * 0.3989422804014327
        low = (hidden * chance).astype(LOW)
        active[0] = low
        active_sent[0] = low
        slope[0] = (chance + hidden * density).astype(LOW)
        add_product(lay, step, total, low, matrix[:, size:])

        @pl.when(step == slots - 1)
        def _():
            (middle_ref,) = late()
            result[...] = (middle_ref[...] + total[...] + rows[0][...]).astype(LOW)

    return layer_call(
        lay,
        kernel,
        "dense_forward",
        [weights],
        [bias],
        [normed_two],
        [middle],
        [b_down],
        [
            low_shape(lay.shards + 1, PAD, size),
            low_shape(slots, PAD, size),
            low_shape(PAD, width),
        ],
        46,
    )


def dense_backward(lay, tangent, slope, middle, weights, gain_two):
    slots, width = lay.slots, lay.width
    size = weights[0].shape[3] // 2

    def kernel(step, weight, slotted, whole, late, rows, outs, total):
        grad_hidden, hidden_sent, up_sums, grad_middle, grad_branch = outs[:5]
        down_sums, gains, shifts, out_sums = outs[5:]

        @pl.when(step == 0)
        def _():
            down_sums[...] = jnp.sum(whole[0][...].astype(F32), axis=0, keepdims=True)
            for ref in (gains, shifts, out_sums):
                ref[...] = jnp.zeros_like(ref)

        matrix = weight(0)
        grad = product(whole[0][...], matrix[:, size:], NN).astype(LOW).astype(F32)
        grad = (grad * slotted[0][0].astype(F32)).astype(LOW)
        grad_hidden[0] = grad
        hidden_sent[0] = grad
        up_sums[0] = jnp.sum(grad.astype(F32), axis=0, keepdims=True)
        add_product(lay, step, total, grad, matrix[:, :size])

        @pl.when(step == slots - 1)
        def _():
            (middle,) = late()

            def finish(start, count):
                at = pl.ds(start, count)
                term, gain_part, shift_part = norm_back(middle[at, :], total[at, :], rows[0][...])
                sums = whole[0][at, :].astype(F32) + term
                grad_middle[at, :] = sums
                grad_branch[at, :] = sums.astype(LOW)
                gains[...] += gain_part
                shifts[...] += shift_part
                out_sums[...] += jnp.sum(sums, axis=0, keepdims=True)

            row_loop(finish)

    row = wide_shape(1, width)
    return layer_call(
        lay,
        kernel,
        "dense_backward",
        [weights],
        [slope],
        [tangent],
        [middle],
        [gain_two],
        [
            low_shape(lay.shards + 1, PAD, size),
            wide_shape(slots, 1, size),
            wide_shape(PAD, width),
            low_shape(PAD, width),
            row,
            row,
            row,
            row,
        ],
        48,
    )


def attention_backward(
    lay, grad_branch, mixed, attended, logs, entry, grad_middle, weights, gain_one
):
    slots, width = lay.slots, lay.width
    part = weights[0].shape[3] // 4

    def kernel(step, weight, slotted, whole, late, rows, outs, total):
        grad_mixed, mixed_sent, qkv_sums, grad_entry, gains, shifts = outs

        @pl.when(step == 0)
        def _():
            for ref in (gains, shifts):
                ref[...] = jnp.zeros_like(ref)

        matrix = weight(0)
        upstream = product(whole[0][...], matrix[:, 3 * part :], NN).astype(LOW)
        parts = attend_back(slotted[0][0], upstream, slotted[1][0], slotted[2][0], part)
        for spot, term in enumerate(parts):
            columns = slice(spot * part, (spot + 1) * part)
            rounded = term.astype(LOW)
            grad_mixed[0, :, columns] = rounded
            mixed_sent[0, :, columns] = rounded
            qkv_sums[0, :, columns] = jnp.sum(rounded.astype(F32), axis=0, keepdims=True)
        add_product(lay, step, total, grad_mixed[0], matrix[:, : 3 * part])

        @pl.when(step == slots - 1)
        def _():
            entry, grad_middle = late()

            def finish(start, count):
                at = pl.ds(start, count)
                term, gain_part, shift_part = norm_back(
                    entry[at, :].astype(F32), total[at, :], rows[0][...]
                )
                grad_entry[at, :] = (grad_middle[at, :] + term).astype(LOW)
                gains[...] += gain_part
                shifts[...] += shift_part

            row_loop(finish)

    row = wide_shape(1, width)
    return layer_call(
        lay,
        kernel,
        "attention_backward",
        [weights],
        [mixed, attended, logs],
        [grad_branch],
        [entry, grad_middle],
        [gain_one],
        [
            low_shape(lay.shards + 1, PAD, 3 * part),
            wide_shape(slots, 1, 3 * part),
            low_shape(PAD, width),
            row,
            row,
        ],
        48,
    )


def weight_grads(lay, slot_order, pairs, cost):
    half, block, shards, width = lay.near, lay.block, lay.shards, lay.width
    sizes = [pair[2].shape[2] for pair in pairs]
    total = sum(sizes)
    whole = pl.BlockSpec((PAD, width), lambda k, s: (0, 0), pipeline_mode=pl.Buffered(1))
    specs, operands, scratch = [], [], []
    for x, x_other, feats, feats_other in pairs:
        feature_spec = pl.BlockSpec((1, PAD, feats.shape[2]), lambda k, s: (k, 0, 0))
        specs += [whole, whole, feature_spec, feature_spec]
        operands += [x, x_other, feats, feats_other]
        scratch += [pltpu.VMEM((width, PAD), LOW)] * 2

    def kernel(_, *refs):
        far_ref, near_ref = refs[4 * len(pairs) : 4 * len(pairs) + 2]
        turned = refs[4 * len(pairs) + 2 :]

        @pl.when(pl.program_id(0) == 0)
        def _():
            for n in range(len(pairs)):
                for b in range(lay.replicas):
                    rows = slice(b * block, (b + 1) * block)
                    other = slice(lay.flip[b] * block, (lay.flip[b] + 1) * block)
                    turned[2 * n][rows, :] = refs[4 * n][:, rows].T
                    turned[2 * n + 1][rows, :] = refs[4 * n + 1][:, other].T

        start = 0
        for n, size in enumerate(sizes):
            grads = product(turned[2 * n][...], refs[4 * n + 2][0], NN) + product(
                turned[2 * n + 1][...], refs[4 * n + 3][0], NN
            )
            grads = grads.reshape(2 * half, block, size).astype(LOW)
            near_ref[:, 0, :, start : start + size] = grads[:half]
            far_ref[:, 0, :, start : start + size] = grads[half:]
            start += size

    return launch(
        lay,
        kernel,
        "weight_grads",
        [slot_order],
        operands,
        specs,
        [pl.BlockSpec((half, 1, block, total), lambda k, s: (0, s[k], 0, 0))] * 2,
        [low_shape(half, shards, block, total)] * 2,
        (shards,),
        scratch,
        28,
        cost,
    )


def add_blocks(lay, *groups, cost=10**10):
    count = min(array.shape[0] - start for group in groups for array, start in group)
    widths = [group[0][0].shape[3] for group in groups]
    middle = groups[0][0][0].shape[1:3]

    def kernel(*refs):
        at, column = 0, 0
        for group, width in zip(groups, widths):
            total = refs[at][...].astype(F32)
            for ref in refs[at + 1 : at + len(group)]:
                total = total + ref[...].astype(F32)
            refs[-1][..., column : column + width] = total.astype(LOW)
            at, column = at + len(group), column + width

    def spec(start, width):
        return pl.BlockSpec((1,) + middle + (width,), lambda i: (i + start, 0, 0, 0))

    return launch(
        lay,
        kernel,
        "add_blocks",
        [],
        [array for group in groups for array, _ in group],
        [spec(start, width) for group, width in zip(groups, widths) for _, start in group],
        [spec(0, sum(widths))],
        [jax.ShapeDtypeStruct((count,) + middle + (sum(widths),), LOW)],
        (count,),
        [],
        28,
        cost,
    )[0]


def pause(lay, cost=4 * 10**10):
    def kernel(out_ref):
        out_ref[...] = jnp.zeros_like(out_ref)

    spec = pl.BlockSpec((8, 128), lambda i: (0, 0))
    shape = jax.ShapeDtypeStruct((8, 128), F32)
    launch(lay, kernel, "pause", [], [], [], [spec], [shape], (1,), [], 8, cost)


def pack_vectors(lay, sums, blocks, slot_order, core):
    rep, block, shards = lay.replicas, lay.block, lay.shards
    assert rep == shards
    wide = sums[0][1].shape[2]
    operands = [v for layer in (0, 1) for v in (*sums[layer][0], *sums[layer][1:])]

    def kernel(s, *refs):
        keep_ref, send_ref = refs[16:]
        owner = s[rep + shards]
        keep_ref[...] = jnp.zeros_like(keep_ref)
        send_ref[...] = jnp.zeros_like(send_ref)
        here, there = refs[:8], refs[8:16]

        def chosen(n, index, mine):
            first = (owner == 0) if mine else (owner != 0)
            return jnp.where(first, here[n][index], there[n][index])

        for out_ref, mine in ((keep_ref, True), (send_ref, False)):
            for n in range(6):
                for b in range(rep):
                    columns = slice(b * block, (b + 1) * block)
                    value = chosen(n, (slice(None), columns), mine)
                    out_ref[s[b] ^ s[rep], n : n + 1, :block] = value
            for side in range(2):
                half = side ^ owner
                for k in range(shards):
                    slot = side * shards + k
                    ups = chosen(6, slot, mine)
                    parts = chosen(7, slot, mine)
                    out_ref[k, pl.ds(8 + half, 1), :] = ups
                    out_ref[k, pl.ds(6 + half, 1), : parts.shape[1]] = parts

    def spec(array):
        return pl.BlockSpec(array.shape, lambda i, s, n=array.ndim: (0,) * n)

    scalars = jnp.concatenate([blocks, slot_order, core[None]])
    shape = jax.ShapeDtypeStruct((shards, 16, wide), F32)
    keep, send = launch(
        lay,
        kernel,
        "pack_vectors",
        [scalars],
        operands,
        [spec(v) for v in operands],
        [pl.BlockSpec(shape.shape, lambda i, s: (0, 0, 0))] * 2,
        [shape] * 2,
        (1,),
        [],
        8,
    )
    return keep, send


def shards(
    boundary_in,
    counts,
    w_qkv,
    b_qkv,
    w_out,
    b_out,
    w_up,
    b_up,
    w_down,
    b_down,
    norm1_gain,
    norm1_shift,
    norm2_gain,
    norm2_shift,
):
    width = boundary_in.shape[4]
    sizes = {axis: lax.axis_size(axis) for axis in ALL_AXES}
    lay = Layout(sizes, width)
    core = lax.axis_index("section").astype(jnp.int32)
    shard = lax.axis_index("shard").astype(jnp.int32)
    replica = lax.axis_index("replica").astype(jnp.int32)
    on_first = core == 0
    heads_wide = w_qkv.shape[3]
    part = heads_wide // 2
    ff_part = w_up.shape[2] // 2
    positions = jnp.arange(lay.replicas, dtype=jnp.int32)
    flips = jnp.asarray(lay.flip, jnp.int32)
    blocks = jnp.where(on_first, positions, flips) ^ replica
    inverse_blocks = jnp.where(on_first, positions ^ replica, flips[positions ^ replica])
    halves = jnp.arange(2, dtype=jnp.int32) ^ core
    scalars = jnp.concatenate([blocks, halves, core[None]])

    slot_order = jnp.arange(lay.shards, dtype=jnp.int32) ^ shard

    raw_qkv = w_qkv[0].reshape(width, 6 * part)
    raw_out, raw_up, raw_down = w_out[0], w_up[0], w_down[0]
    split_pieces = first_pieces(lay, raw_qkv, raw_out, raw_up, raw_down, scalars)
    first, second = [], []
    for piece, sent in zip(split_pieces[:2], split_pieces[2:]):
        other = lay.across_cores(sent)
        first.append(jnp.where(on_first, piece, other))
        second.append(jnp.where(on_first, other, piece))
    pieces = first + second
    (pictures,) = lay.hold(boundary_in[0, :, 0])
    received = lay.across_cores(pictures)
    live = (shard < counts[replica, core]).astype(F32)[None]
    gather = Gather(lay, slot_order, pieces)
    gather.start(0)
    image, cot = arrange_images(lay, pictures, received, blocks, core, live)

    raws = (raw_qkv, raw_out, raw_up, raw_down)
    raws_other = [lay.across_cores(raw) for raw in raws]
    own_attention = arrange_attention(lay, raws[:2], raws_other[:2], scalars)

    packed = jnp.concatenate(
        [v[0] for v in (b_out, b_down, norm1_gain, norm1_shift, norm2_gain, norm2_shift)]
        + [b_qkv.reshape(-1), b_up.reshape(-1)]
    )
    packed_other = lay.across_cores(packed)
    both = jnp.stack(
        [jnp.where(on_first, packed, packed_other), jnp.where(on_first, packed_other, packed)]
    )
    wide = both[:, : 6 * width].reshape(2, 6, lay.replicas, lay.block)
    wide = jnp.take(wide, blocks, axis=2).reshape(2, 6, 1, width).astype(F32)
    split = both[:, 6 * width :]
    split = jnp.stack([split] + [lay.along_shard(split, k) for k in range(1, lay.shards)])
    split_qkv = split[:, :, : 4 * part].reshape(lay.shards, 2, 2, 2, part)
    split_qkv = jnp.take(split_qkv, halves, axis=3).transpose(1, 3, 0, 2, 4)
    split_qkv = split_qkv.reshape(2, lay.slots, 2, part)
    bias_qkv = jnp.concatenate(
        [split_qkv[:, :, 0], jnp.zeros_like(split_qkv[:, :, 0]), split_qkv[:, :, 1]], axis=-1
    ).reshape(2, lay.slots, 1, 3 * part).astype(F32)
    bias_up = split[:, :, 4 * part :].reshape(lay.shards, 2, 2, ff_part)
    bias_up = jnp.take(bias_up, halves, axis=2).transpose(1, 2, 0, 3)
    bias_up = bias_up.reshape(2, lay.slots, 1, ff_part).astype(F32)

    kept, weights = [], []
    entry = image
    gather.step(0)
    gather.start(1)
    gather.step(0)
    gather.start(2)
    gather.step(1)
    gather.start(3)
    w_attention = gather.finish(0, own_attention[0])
    for layer in range(2):
        vec_out, vec_down, gain_one, shift_one, gain_two, shift_two = wide[layer]
        normed, mixed, attended, logs, middle, normed_two = attention_forward(
            lay,
            entry,
            w_attention,
            bias_qkv[layer],
            (gain_one, shift_one, vec_out, gain_two, shift_two),
        )
        exchanged = [
            lay.across_cores(value) for value in (normed, normed_two, attended[lay.shards :])
        ]
        if layer == 0:
            gather.step(1)
            gather.step(2)
            lay.absorb(*exchanged)
            own_dense = arrange_dense(lay, raws[2:], raws_other[2:], scalars)
            gather.step(3)
            w_dense = gather.finish(1, own_dense[0])
            gather.step(2)
            pause(lay)
        else:
            w_dense = gather.finish(3, own_dense[1])
            lay.absorb(kept[0][-1][-1])
            pause(lay)
        active, active_sent, slope, result = dense_forward(
            lay,
            normed_two,
            middle,
            w_dense,
            bias_up[layer],
            vec_down,
        )
        weights.append((w_attention, w_dense))
        exchanged.append(lay.across_cores(active_sent))
        if layer == 0:
            w_attention = gather.finish(2, own_attention[1])
            gather.step(3)
            pause(lay)
        kept.append(
            (entry, normed, mixed, attended, logs, middle, normed_two, active, slope, exchanged)
        )
        entry = result

    terms, sums, vector_sums, latest = {}, {}, {}, {}

    def begin(name, *pairs, cost=1000):
        far, near = weight_grads(lay, slot_order, pairs, cost)
        arrived = lay.along_bit(far, lay.bits - 1)
        terms[name] = [(near, 0), (arrived, 0)]

    def halve(name, cost=10**10):
        for bit in range(lay.bits - 2, -1, -1):
            split = 1 << bit
            group = [(array, start + split) for array, start in terms[name]]
            sent = add_blocks(lay, group, cost=cost)
            terms[name] = terms[name] + [(lay.along_bit(sent, bit), 0)]

    def collect(names, direct, cost=10**10):
        total = add_blocks(lay, *(terms[name] for name in names), cost=cost)[0]
        if direct:
            latest[names] = lax.all_to_all(total, "shard", 0, 0, tiled=True)
        else:
            latest[names] = lax.psum_scatter(total, "shard", scatter_dimension=0)[None]

    def settle(*all_names):
        for names, total in zip(all_names, lay.hold(*(latest[names] for names in all_names))):
            spread(names, total)

    def spread(names, total):
        total = jnp.sum(total.astype(F32), axis=0)
        at = 0
        for name in names:
            size = terms[name][0][0].shape[3]
            sums[name] = total[:, at : at + size]
            at += size

    tangent = cot
    for layer in (1, 0):
        w_attention, w_dense = weights[layer]
        vec_out, vec_down, gain_one, shift_one, gain_two, shift_two = wide[layer]
        entry_in, normed, mixed, attended, logs, middle, normed_two, active, slope, other = kept[layer]
        normed_other, normed_two_other, attended_other, active_other = other
        if layer == 1:
            begin((1, "down"), (tangent, lay.across_cores(tangent), active, active_other))
        (
            grad_hidden,
            hidden_sent,
            up_sums,
            grad_middle,
            grad_branch,
            down_sums,
            gain_two_sum,
            shift_two_sum,
            out_sums,
        ) = dense_backward(lay, tangent, slope, middle, w_dense, gain_two)
        branch_other, hidden_other = lay.across_cores(grad_branch), lay.across_cores(hidden_sent)
        out_pair = (grad_branch, branch_other, attended, attended_other)
        if layer == 1:
            halve((1, "down"))
        else:
            settle(((1, "down"),))
            collect(((1, "out"), (1, "up")), False)
            halve((0, "down"))
        begin((layer, "out"), out_pair, cost=4 * 10**10)
        if layer == 0:
            halve((1, "qkv"))
        begin((layer, "up"), (normed_two, normed_two_other, grad_hidden, hidden_other))
        if layer == 0:
            collect(((1, "qkv"), (0, "down")), True)
        grad_mixed, mixed_sent, qkv_sums, grad_entry, gain_one_sum, shift_one_sum = (
            attention_backward(
                lay,
                grad_branch,
                mixed,
                attended,
                logs,
                entry_in,
                grad_middle,
                w_attention,
                gain_one,
            )
        )
        tangent = grad_entry
        mixed_other = lay.across_cores(mixed_sent)
        vector_sums[layer] = (
            [out_sums, down_sums, gain_one_sum, shift_one_sum, gain_two_sum, shift_two_sum],
            up_sums,
            qkv_sums,
        )
        if layer == 1:
            collect(((1, "down"),), False)
        if layer == 0:
            keep, send = pack_vectors(lay, vector_sums, blocks, slot_order, core)
            send = lay.across_cores(send)
        halve((layer, "out"))
        if layer == 0:
            (send,) = lay.hold(send)
            summed = keep + send
            coming = [lay.along_shard(summed[k], k) for k in range(1, lay.shards)]
        halve((layer, "up"))
        if layer == 0:
            settle(((1, "out"), (1, "up")), ((1, "qkv"), (0, "down")))
            pause(lay, 10**10)
        if layer == 1:
            active, active_other = kept[0][7], kept[0][9][3]
            begin((0, "down"), (tangent, lay.across_cores(tangent), active, active_other))
        begin((layer, "qkv"), (normed, normed_other, grad_mixed, mixed_other))
    summed = sum(lay.hold(*coming), summed[0])
    coming = lay.along_bit_plain(summed, 0)
    back = restore_image(lay, tangent, blocks, jnp.ones((1,), F32))
    ahead = restore_image(lay, entry, blocks, live)
    collect(((0, "out"), (0, "up")), False, cost=2 * 10**10)
    halve((0, "qkv"), cost=1000)
    back, ahead = lay.hold(back, ahead)
    for bit in range(lay.bits):
        (coming,) = lay.hold(coming)
        summed = summed + coming
        if bit + 1 < lay.bits:
            coming = lay.along_bit_plain(summed, bit + 1)
    collect(((0, "qkv"),), True, cost=1000)
    last = (((0, "out"), (0, "up")), ((0, "qkv"),))
    for names, total in zip(last, lax.optimization_barrier([latest[names] for names in last])):
        spread(names, total)

    def to_owner(first, second):
        keep = jnp.where(on_first, first, second)
        other = lay.across_cores(jnp.where(on_first, second, first))
        return jnp.where(on_first, keep, other), jnp.where(on_first, other, keep)

    down_halves = to_owner(sums[0, "down"], sums[1, "down"])
    up_halves = to_owner(sums[0, "up"], sums[1, "up"])
    out_halves = to_owner(sums[0, "out"], sums[1, "out"])
    qkv_halves = to_owner(sums[0, "qkv"], sums[1, "qkv"])
    grad_w_down = jnp.concatenate(down_halves, axis=1).T[None]
    grad_w_up = jnp.concatenate(up_halves, axis=1)[None]
    grad_w_qkv = jnp.stack(
        [half.reshape(-1, 3, part) for half in qkv_halves], axis=2
    ).reshape(1, lay.block, 3, heads_wide)
    grad_w_out = jnp.concatenate(out_halves, axis=1).T[None]

    share = lay.block // lay.replicas
    model = lax.dynamic_slice_in_dim(summed[:6, : lay.block], replica * share, share, 1)
    vectors = [model[i : i + 1] for i in range(6)]
    parts = summed[6:8, : 3 * part].reshape(2, 3, part)
    parts = jnp.stack([parts[:, 0], parts[:, 2]]).reshape(2, 2 * part)
    grad_b_qkv = lax.dynamic_slice_in_dim(parts, replica * share, share, 1)[None]
    share_up = 2 * ff_part // lay.replicas
    ups = summed[8:10, :ff_part].reshape(1, 2 * ff_part)
    grad_b_up = lax.dynamic_slice_in_dim(ups, replica * share_up, share_up, 1)

    keep = jnp.where(on_first, back, ahead)
    other = lay.across_cores(jnp.where(on_first, ahead, back))
    boundary_out = jnp.stack([jnp.where(on_first, keep, other), jnp.where(on_first, other, keep)])
    boundary_out = boundary_out[None, :, None]
    return (
        boundary_out,
        grad_w_qkv,
        grad_b_qkv,
        grad_w_out,
        vectors[0],
        grad_w_up,
        grad_b_up,
        grad_w_down,
        vectors[1],
        vectors[2],
        vectors[3],
        vectors[4],
        vectors[5],
    )


def solution(mesh):
    spread = P("section", ("shard", "replica"))
    return jax.shard_map(
        shards,
        mesh=mesh,
        in_specs=(
            P("section", None, ("shard", "replica"), None, None),
            P(),
            P("section", None, None, "shard"),
            P("section", None, "shard"),
            P("section", "shard", None),
            P("section", None),
            P("section", None, "shard"),
            P("section", "shard"),
            P("section", "shard", None),
            P("section", None),
            P("section", None),
            P("section", None),
            P("section", None),
            P("section", None),
        ),
        out_specs=(
            P("section", None, ("shard", "replica"), None, None),
            P("section", "replica", None, "shard"),
            P("section", None, ("shard", "replica")),
            P("section", "shard", "replica"),
            spread,
            P("section", "replica", "shard"),
            spread,
            P("section", "shard", "replica"),
            spread,
            spread,
            spread,
            spread,
            spread,
        ),
        check_vma=False,
    )
```

```python
import functools

import jax
import jax.numpy as jnp
from jax import lax
from jax.experimental import pallas as pl
from jax.experimental.pallas import tpu as pltpu
from jax.sharding import PartitionSpec as P

HEAD = 64
SEQ = 577
PAD = 592
CHUNK = 144
LOW = jnp.bfloat16
F32 = jnp.float32
ALL_AXES = ("section", "shard", "replica")
NT = (((1,), (1,)), ((), ()))
NN = (((1,), (0,)), ((), ()))
TN = (((0,), (0,)), ((), ()))


def reverse_bits(value, bits):
    flipped = 0
    for spot in range(bits):
        flipped |= ((value >> spot) & 1) << (bits - 1 - spot)
    return flipped


def product(left, right, dims):
    return lax.dot_general(left, right, dims, preferred_element_type=F32)


def row_loop(body):
    whole = PAD // CHUNK

    def step(index, carry):
        body(pl.multiple_of(index * CHUNK, 16), CHUNK)
        return carry

    lax.fori_loop(0, whole, step, 0)
    if PAD % CHUNK:
        body(whole * CHUNK, PAD % CHUNK)


def params(megabytes=48):
    return pltpu.CompilerParams(vmem_limit_bytes=megabytes * 2**20)


def launch(
    lay, kernel, name, scalars, operands, in_specs, out_specs, out_shape, grid, scratch, megabytes, cost=1000
):
    tokens = lay.after
    count = len(scalars) + len(operands)

    def ordered(*refs):
        rest = refs[count + len(tokens) :]
        rest[len(out_shape)][...] = jnp.zeros((8, 128), F32)
        kernel(*refs[:count], *rest[: len(out_shape)], *rest[len(out_shape) + 1 :])

    token_spec = pl.BlockSpec((8, 128), lambda *_: (0, 0))
    results = pl.pallas_call(
        ordered,
        grid_spec=pltpu.PrefetchScalarGridSpec(
            num_scalar_prefetch=len(scalars),
            grid=grid,
            in_specs=list(in_specs) + [pl.BlockSpec(memory_space=pl.ANY)] * len(tokens),
            out_specs=list(out_specs) + [token_spec],
            scratch_shapes=scratch,
        ),
        out_shape=list(out_shape) + [jax.ShapeDtypeStruct((8, 128), F32)],
        compiler_params=params(megabytes),
        cost_estimate=pl.CostEstimate(flops=cost, bytes_accessed=2**18, transcendentals=0),
        name=name,
    )(*scalars, *operands, *tokens)
    lay.after = [results[-1]]
    return results[:-1]


def normalized(values):
    center = values - jnp.mean(values, axis=-1, keepdims=True)
    spread = jnp.mean(center * center, axis=-1, keepdims=True)
    inverse = lax.rsqrt(spread + 1e-06)
    return center * inverse, inverse


class Layout:
    def __init__(self, mesh_shape, width):
        self.shards = mesh_shape["shard"]
        self.replicas = mesh_shape["replica"]
        self.bits = self.replicas.bit_length() - 1
        self.width = width
        self.block = width // self.replicas
        self.flip = [reverse_bits(b, self.bits) for b in range(self.replicas)]
        self.near = self.replicas // 2
        self.slots = 2 * self.shards
        self.after = []

    def absorb(self, *values):
        for value in values:
            corner = value.reshape((-1,) + value.shape[-2:])[0, :8, :128]
            self.after.append(corner)

    def hold(self, *values):
        values, self.after = lax.optimization_barrier((values, self.after))
        return values

    def across_cores(self, value):
        return lax.ppermute(value, "section", [(0, 1), (1, 0)])

    def along_shard(self, value, slot):
        return lax.ppermute(value, "shard", [(i, i ^ slot) for i in range(self.shards)])

    def along_bit_plain(self, value, bit):
        route = [(i, i ^ (1 << bit)) for i in range(self.replicas)]
        return lax.ppermute(value, "replica", route)

    def along_bit(self, value, bit):
        route = []
        for core in range(2):
            physical = bit if core == 0 else self.bits - 1 - bit
            for shard in range(self.shards):
                base = (core * self.shards + shard) * self.replicas
                for replica in range(self.replicas):
                    route.append((base + replica, base + (replica ^ (1 << physical))))
        return lax.ppermute(value, ALL_AXES, route)


def arrange_images(lay, mine, received, blocks, core, live):
    width, block = lay.width, lay.block

    def kernel(scalars, live_ref, mine_ref, other_ref, image_ref, cot_ref):
        here = mine_ref[0]
        there = other_ref[0]
        first = scalars[lay.replicas] == 0
        image = jnp.where(first, here, there)
        cot = jnp.where(first, there, here).astype(F32) * live_ref[0]
        image_ref[...] = jnp.zeros_like(image_ref)
        cot_ref[...] = jnp.zeros_like(cot_ref)
        image_ref[0:SEQ, :] = image
        cot_ref[0:SEQ, :] = cot.astype(LOW)

    scalars = jnp.concatenate([blocks, core[None]]).astype(jnp.int32)
    shape = jax.ShapeDtypeStruct((PAD, width), LOW)
    whole = pl.BlockSpec((1, SEQ, block), lambda b, s: (s[lay.replicas], 0, s[b]))
    return launch(
        lay,
        kernel,
        "arrange_images",
        [scalars],
        [live, mine, received],
        [pl.BlockSpec(memory_space=pltpu.SMEM), whole, whole],
        [pl.BlockSpec((PAD, block), lambda b, s: (0, b))] * 2,
        [shape, shape],
        (lay.replicas,),
        [],
        24,
    )


def restore_image(lay, values, blocks, scale):
    def kernel(scalars, scale_ref, in_ref, out_ref):
        out_ref[...] = (in_ref[0:SEQ, :].astype(F32) * scale_ref[0]).astype(LOW)

    return launch(
        lay,
        kernel,
        "restore_image",
        [blocks],
        [scale, values],
        [
            pl.BlockSpec(memory_space=pltpu.SMEM),
            pl.BlockSpec((PAD, lay.block), lambda b, s: (0, b)),
        ],
        [pl.BlockSpec((SEQ, lay.block), lambda b, s: (0, s[b]))],
        [jax.ShapeDtypeStruct((SEQ, lay.width), LOW)],
        (lay.replicas,),
        [],
        16,
    )[0]


def chosen_half(flag, low, high):
    return jnp.where(flag == 0, low, high)


def arrange_attention(lay, mine, received, scalars):
    rep, block = lay.replicas, lay.block
    part = mine[1].shape[0] // 2

    def kernel(s, qkv_mine, qkv_other, out_mine, out_other, first_ref, second_ref):
        first = s[rep + 2] == 0
        half = s[rep + pl.program_id(0)]

        def columns(ref, t):
            start = 2 * t * part
            return chosen_half(
                half, ref[:, start : start + part], ref[:, start + part : start + 2 * part]
            )

        for t in range(3):
            here, there = columns(qkv_mine, t), columns(qkv_other, t)
            first_ref[0, 0, :, t * part : (t + 1) * part] = jnp.where(first, here, there)
            second_ref[0, 0, :, t * part : (t + 1) * part] = jnp.where(first, there, here)
        here, there = out_mine[...].T, out_other[...].T
        first_ref[0, 0, :, 3 * part :] = jnp.where(first, here, there)
        second_ref[0, 0, :, 3 * part :] = jnp.where(first, there, here)

    shape = jax.ShapeDtypeStruct((2, rep, block, 4 * part), LOW)
    qkv_spec = pl.BlockSpec((block, 6 * part), lambda p, b, s: (s[b], 0))
    out_spec = pl.BlockSpec((part, block), lambda p, b, s: (s[rep + p], s[b]))
    return launch(
        lay,
        kernel,
        "arrange_attention",
        [scalars],
        [mine[0], received[0], mine[1], received[1]],
        [qkv_spec, qkv_spec, out_spec, out_spec],
        [pl.BlockSpec((1, 1, block, 4 * part), lambda p, b, s: (p, b, 0, 0))] * 2,
        [shape, shape],
        (2, rep),
        [],
        16,
    )


def arrange_dense(lay, mine, received, scalars):
    rep, block = lay.replicas, lay.block
    part = mine[0].shape[1] // 2

    def kernel(s, up_mine, up_other, down_mine, down_other, first_ref, second_ref):
        first = s[rep + 2] == 0
        here, there = up_mine[...], up_other[...]
        first_ref[0, 0, :, :part] = jnp.where(first, here, there)
        second_ref[0, 0, :, :part] = jnp.where(first, there, here)
        here, there = down_mine[...].T, down_other[...].T
        first_ref[0, 0, :, part:] = jnp.where(first, here, there)
        second_ref[0, 0, :, part:] = jnp.where(first, there, here)

    shape = jax.ShapeDtypeStruct((2, rep, block, 2 * part), LOW)
    up_spec = pl.BlockSpec((block, part), lambda p, b, s: (s[b], s[rep + p]))
    down_spec = pl.BlockSpec((part, block), lambda p, b, s: (s[rep + p], s[b]))
    return launch(
        lay,
        kernel,
        "arrange_dense",
        [scalars],
        [mine[0], received[0], mine[1], received[1]],
        [up_spec, up_spec, down_spec, down_spec],
        [pl.BlockSpec((1, 1, block, 2 * part), lambda p, b, s: (p, b, 0, 0))] * 2,
        [shape] * 2,
        (2, rep),
        [],
        16,
    )


def first_pieces(lay, qkv, out, up, down, scalars):
    rep, block = lay.replicas, lay.block
    part, wide = out.shape[0] // 2, up.shape[1] // 2

    def kernel(s, qkv_ref, out_ref, up_ref, down_ref, *outs):
        core = s[rep + 2]
        for flag, attention_ref, dense_ref in ((core, *outs[:2]), (1 - core, *outs[2:])):
            for t in range(3):
                start = 2 * t * part
                attention_ref[:, t * part : (t + 1) * part] = chosen_half(
                    flag,
                    qkv_ref[:, start : start + part],
                    qkv_ref[:, start + part : start + 2 * part],
                )
            attention_ref[:, 3 * part :] = chosen_half(flag, out_ref[:part], out_ref[part:]).T
            dense_ref[:, :wide] = chosen_half(flag, up_ref[:, :wide], up_ref[:, wide:])
            dense_ref[:, wide:] = chosen_half(flag, down_ref[:wide], down_ref[wide:]).T

    attention_shape = jax.ShapeDtypeStruct((block, 4 * part), LOW)
    dense_shape = jax.ShapeDtypeStruct((block, 2 * wide), LOW)
    attention_spec = pl.BlockSpec((block, 4 * part), lambda i, s: (0, 0))
    dense_spec = pl.BlockSpec((block, 2 * wide), lambda i, s: (0, 0))
    return launch(
        lay,
        kernel,
        "first_pieces",
        [scalars],
        [qkv, out, up, down],
        [
            pl.BlockSpec((block, 6 * part), lambda i, s: (s[0], 0)),
            pl.BlockSpec((2 * part, block), lambda i, s: (0, s[0])),
            pl.BlockSpec((block, 2 * wide), lambda i, s: (s[0], 0)),
            pl.BlockSpec((2 * wide, block), lambda i, s: (0, s[0])),
        ],
        [attention_spec, dense_spec] * 2,
        [attention_shape, dense_shape] * 2,
        (1,),
        [],
        16,
    )


def pick_slots(lay, gathered, slot_order):
    rows, columns = gathered.shape[1:]

    def kernel(_, in_ref, out_ref):
        out_ref[0] = in_ref[...]

    return launch(
        lay,
        kernel,
        "pick_slots",
        [slot_order],
        [gathered],
        [pl.BlockSpec((1, rows, columns), lambda k, s: (s[k + 1], 0, 0))],
        [pl.BlockSpec((1, 1, rows, columns), lambda k, s: (0, k, 0, 0))],
        [jax.ShapeDtypeStruct((1, lay.shards - 1, rows, columns), LOW)],
        (lay.shards - 1,),
        [],
        8,
    )[0]


def join(lay, first, second):
    count, rows = first.shape[0], first.shape[1]
    shape = (2 * count,) + first.shape[1:]
    block = (1, rows) + first.shape[2:]

    def kernel(first_ref, second_ref, out_ref):
        step = pl.program_id(0)

        @pl.when(step < count)
        def _():
            out_ref[...] = first_ref[...]

        @pl.when(step >= count)
        def _():
            out_ref[...] = second_ref[...]

    return launch(
        lay,
        kernel,
        "join",
        [],
        [first, second],
        [
            pl.BlockSpec(block, lambda i: (jnp.minimum(i, count - 1), 0, 0, 0)),
            pl.BlockSpec(block, lambda i: (jnp.maximum(i - count, 0), 0, 0, 0)),
        ],
        [pl.BlockSpec(block, lambda i: (i, 0, 0, 0))],
        [jax.ShapeDtypeStruct(shape, LOW)],
        (2 * count,),
        [],
        16,
    )[0]


def copied(lay, value):
    def kernel(in_ref, out_ref):
        out_ref[...] = in_ref[...]

    spec = pl.BlockSpec(value.shape, lambda i: (0, 0))
    shape = jax.ShapeDtypeStruct(value.shape, value.dtype)
    return launch(lay, kernel, "copied", [], [value], [spec], [spec], [shape], (1,), [], 8)[0]


class Gather:
    def __init__(self, lay, slot_order, pieces):
        self.lay, self.pieces, self.slot_order = lay, pieces, slot_order
        self.state = [None] * len(pieces)
        self.done = [0] * len(pieces)

    def start(self, n):
        piece = self.pieces[n] if n == 0 else copied(self.lay, self.pieces[n])
        self.state[n] = lax.all_gather(piece, "shard")

    def step(self, n):
        lay = self.lay
        if self.done[n] == 0:
            near = pick_slots(lay, self.state[n], self.slot_order)
        else:
            near = join(lay, *self.state[n])
        self.state[n] = (near, lay.along_bit(near, self.done[n]))
        self.done[n] += 1

    def finish(self, n, own):
        lay = self.lay
        while self.done[n] < lay.bits:
            self.step(n)
        near, far = self.state[n]
        (far,) = lay.hold(far)
        return (own, near, far, lay.across_cores(near), lay.across_cores(far))


def fetch_weights(lay, refs, held, sems, slot):
    own, near, far, near_other, far_other = refs
    half = lay.near
    side, k = divmod(slot, lay.shards)

    def start(source, target):
        pltpu.make_async_copy(source, target, sems.at[slot]).start()

    if k == 0:
        start(own.at[side], held.at[slot])
    elif side == 0:
        start(near.at[:, k - 1], held.at[slot, 0:half])
        start(far.at[:, k - 1], held.at[slot, half : 2 * half])
    else:
        for b in range(half):
            start(near_other.at[b, k - 1], held.at[slot, lay.flip[b]])
            start(far_other.at[b, k - 1], held.at[slot, lay.flip[half + b]])


def await_weights(held, sems, slot):
    pltpu.make_async_copy(held.at[slot], held.at[slot], sems.at[slot]).wait()


def flat(block):
    return block.reshape(block.shape[0] * block.shape[1], block.shape[2])


def layer_call(lay, kernel, name, weights, slotted, whole, late, rows, outs, megabytes):
    slots, width, shards = lay.slots, lay.width, lay.shards
    once = dict(pipeline_mode=pl.Buffered(1))

    def own_half(i):
        return (jnp.minimum(i, shards), 0, 0)

    def other_half(i):
        return (jnp.where(i < shards, shards, i - shards), 0, 0)

    def spec(shape, **mode):
        if len(shape) == 3:
            return pl.BlockSpec((1,) + shape[1:], lambda i: (i, 0, 0))
        return pl.BlockSpec(shape, lambda i: (0, 0), **mode)

    out_specs, out_shape = [], []
    for o in outs:
        if len(o.shape) == 3 and o.shape[0] == shards + 1:
            out_specs += [pl.BlockSpec((1,) + o.shape[1:], m) for m in (own_half, other_half)]
            out_shape += [o, o]
        else:
            out_specs.append(spec(o.shape))
            out_shape.append(o)
    outs = out_shape
    anywhere = pl.BlockSpec(memory_space=pltpu.HBM)
    counts = [5 * len(weights), len(slotted), len(whole), len(late), len(rows), len(outs)]

    def body(*refs):
        groups, at = [], 0
        for count in counts + [1, len(weights), len(weights), len(late)]:
            groups.append(refs[at : at + count])
            at += count
        arrays, slot_refs, whole_refs, late_refs, row_refs, out_refs = groups[:6]
        (total,), held, sems, late_held = groups[6:10]
        late_sem = refs[at] if late else None
        step = pl.program_id(0)

        def late_copy(n):
            return pltpu.make_async_copy(late_refs[n], late_held[n], late_sem.at[n])

        @pl.when(step == 0)
        def _():
            for slot in range(slots):
                for n in range(len(weights)):
                    fetch_weights(lay, arrays[5 * n : 5 * n + 5], held[n], sems[n], slot)
            for n in range(len(late)):
                late_copy(n).start()

        def weight(n):
            await_weights(held[n], sems[n], step)
            return flat(held[n][step])

        def late_values():
            for n in range(len(late)):
                late_copy(n).wait()
            return late_held

        kernel(step, weight, slot_refs, whole_refs, late_values, row_refs, out_refs, total)

    arrays = [array for matrix in weights for array in matrix]
    scratch = [pltpu.VMEM((PAD, width), F32)]
    scratch += [pltpu.VMEM((slots,) + matrix[0].shape[1:], LOW) for matrix in weights]
    scratch += [pltpu.SemaphoreType.DMA((slots,)) for _ in weights]
    scratch += [pltpu.VMEM(a.shape, a.dtype) for a in late]
    if late:
        scratch.append(pltpu.SemaphoreType.DMA((len(late),)))
    return launch(
        lay,
        body,
        name,
        [],
        [*arrays, *slotted, *whole, *late, *rows],
        [anywhere] * len(arrays)
        + [spec(a.shape) for a in slotted]
        + [spec(a.shape, **once) for a in whole]
        + [anywhere] * len(late)
        + [spec(a.shape, **once) for a in rows],
        out_specs,
        out_shape,
        (slots,),
        scratch,
        megabytes,
    )


def add_product(lay, step, total, acts, matrix):
    for b in range(lay.replicas):
        columns = slice(b * lay.block, (b + 1) * lay.block)
        term = product(acts, matrix[columns], NT)
        total[:, columns] = jnp.where(step == 0, 0.0, total[:, columns]) + term


def low_shape(*shape):
    return jax.ShapeDtypeStruct(shape, LOW)


def wide_shape(*shape):
    return jax.ShapeDtypeStruct(shape, F32)


def mask_keys(scores, low):
    edge = SEQ // 16 * 16
    valid = lax.broadcasted_iota(jnp.int32, (PAD - edge, 1), 0) < SEQ - edge
    return jnp.concatenate([scores[:edge], jnp.where(valid, scores[edge:], low)], axis=0)


def attend(block, part):
    query, keys, values = block[:, :part], block[:, part : 2 * part], block[:, 2 * part :]
    heads = range(part // HEAD)
    lanes = lax.broadcasted_iota(jnp.int32, (1, part), 1) // HEAD
    query = query * HEAD ** (-0.5)
    turned = values.T
    ones = jnp.ones((16, PAD), LOW)
    scores = [product(keys, jnp.where(lanes == h, query, 0), NT) for h in heads]
    scores = [mask_keys(score, -1e30) for score in scores]
    peaks = [jnp.max(score, axis=0, keepdims=True) for score in scores]
    weights = [jnp.exp(score - peak).astype(LOW) for score, peak in zip(scores, peaks)]
    sums = [
        product(jnp.concatenate([turned[h * HEAD : (h + 1) * HEAD], ones], axis=0), weights[h], NN)
        for h in heads
    ]
    result = jnp.concatenate([s[:HEAD] / s[HEAD : HEAD + 1] for s in sums], axis=0).T
    spot = lax.broadcasted_iota(jnp.int32, (8, 1), 0)
    logs = jnp.zeros((8, PAD), F32)
    for h in heads:
        logs = jnp.where(spot == h, peaks[h] + jnp.log(sums[h][HEAD : HEAD + 1]), logs)
    return result.astype(LOW), logs


def attend_back(block, grads, attended, logs, part):
    query, keys, values = block[:, :part], block[:, part : 2 * part], block[:, 2 * part :]
    heads = range(part // HEAD)
    lanes = lax.broadcasted_iota(jnp.int32, (1, part), 1) // HEAD
    wide = lax.broadcasted_iota(jnp.int32, (1, 128), 1)
    query = query * HEAD ** (-0.5)

    def pick(h, array):
        return jnp.where(lanes == h, array, 0)

    along = grads.astype(F32) * attended.astype(F32)
    inner = jnp.zeros((PAD, 128), F32)
    for h in heads:
        inner = jnp.where(wide == h, jnp.sum(pick(h, along), axis=-1, keepdims=True), inner)
    inner = inner.T
    scores = [product(keys, pick(h, query), NT) for h in heads]
    slopes = [product(values, pick(h, grads), NT) for h in heads]
    chances = [mask_keys(jnp.exp(scores[h] - logs[h : h + 1]), 0.0) for h in heads]
    grad_scores = [(chances[h] * (slopes[h] - inner[h : h + 1])).astype(LOW) for h in heads]
    low = [chance.astype(LOW) for chance in chances]
    value_terms = [product(low[h], grads, NN) for h in heads]
    key_terms = [product(grad_scores[h], query, NN) for h in heads]
    turned = keys.T
    query_terms = [
        product(turned[h * HEAD : (h + 1) * HEAD], grad_scores[h], NN) for h in heads
    ]

    def merge(terms):
        result = terms[0]
        for h in heads:
            result = jnp.where(lanes == h, terms[h], result)
        return result

    return (
        jnp.concatenate(query_terms, axis=0).T * HEAD ** (-0.5),
        merge(key_terms),
        merge(value_terms),
    )


def norm_back(values, grads, gain):
    values, inverse = normalized(values)
    slope = grads * gain
    mean = jnp.mean(slope, axis=-1, keepdims=True)
    along = jnp.mean(slope * values, axis=-1, keepdims=True)
    term = inverse * (slope - mean - values * along)
    return (
        term,
        jnp.sum(grads * values, axis=0, keepdims=True),
        jnp.sum(grads, axis=0, keepdims=True),
    )


def attention_forward(lay, entry, weights, bias, rows):
    slots, width = lay.slots, lay.width
    part = weights[0].shape[3] // 4

    def kernel(step, weight, slotted, whole, late, rows, outs, total):
        normed, mixed, attended, logs, middle, normed_two = outs

        @pl.when(step == 0)
        def _():
            def norm_rows(start, count):
                values, _ = normalized(whole[0][pl.ds(start, count), :].astype(F32))
                normed[pl.ds(start, count), :] = (values * rows[0][...] + rows[1][...]).astype(LOW)

            row_loop(norm_rows)

        matrix = weight(0)
        block = (product(normed[...], matrix[:, : 3 * part], NN) + slotted[0][0]).astype(LOW)
        mixed[0] = block
        result, log_rows = attend(block, part)
        attended[0] = result
        logs[0] = log_rows
        add_product(lay, step, total, result, matrix[:, 3 * part :])

        @pl.when(step == slots - 1)
        def _():
            def finish(start, count):
                at = pl.ds(start, count)
                sums = whole[0][at, :].astype(F32) + total[at, :] + rows[2][...]
                middle[at, :] = sums
                values, _ = normalized(sums)
                normed_two[at, :] = (values * rows[3][...] + rows[4][...]).astype(LOW)

            row_loop(finish)

    return layer_call(
        lay,
        kernel,
        "attention_forward",
        [weights],
        [bias],
        [entry],
        [],
        rows,
        [
            low_shape(PAD, width),
            low_shape(slots, PAD, 3 * part),
            low_shape(slots, PAD, part),
            wide_shape(slots, 8, PAD),
            wide_shape(PAD, width),
            low_shape(PAD, width),
        ],
        40,
    )


def dense_forward(lay, normed_two, middle, weights, bias, b_down):
    slots, width = lay.slots, lay.width
    size = weights[0].shape[3] // 2

    def kernel(step, weight, slotted, whole, late, rows, outs, total):
        active, active_sent, slope, result = outs
        matrix = weight(0)
        hidden = product(whole[0][...], matrix[:, :size], NN) + slotted[0][0]
        chance = 0.5 + 0.5 * lax.erf(hidden * (0.5**0.5))
        density = jnp.exp(-0.5 * hidden * hidden) * 0.3989422804014327
        low = (hidden * chance).astype(LOW)
        active[0] = low
        active_sent[0] = low
        slope[0] = (chance + hidden * density).astype(LOW)
        add_product(lay, step, total, low, matrix[:, size:])

        @pl.when(step == slots - 1)
        def _():
            (middle_ref,) = late()
            result[...] = (middle_ref[...] + total[...] + rows[0][...]).astype(LOW)

    return layer_call(
        lay,
        kernel,
        "dense_forward",
        [weights],
        [bias],
        [normed_two],
        [middle],
        [b_down],
        [
            low_shape(lay.shards + 1, PAD, size),
            low_shape(slots, PAD, size),
            low_shape(PAD, width),
        ],
        46,
    )


def dense_backward(lay, tangent, slope, middle, weights, gain_two):
    slots, width = lay.slots, lay.width
    size = weights[0].shape[3] // 2

    def kernel(step, weight, slotted, whole, late, rows, outs, total):
        grad_hidden, hidden_sent, up_sums, grad_middle, grad_branch = outs[:5]
        down_sums, gains, shifts, out_sums = outs[5:]

        @pl.when(step == 0)
        def _():
            down_sums[...] = jnp.sum(whole[0][...].astype(F32), axis=0, keepdims=True)
            for ref in (gains, shifts, out_sums):
                ref[...] = jnp.zeros_like(ref)

        matrix = weight(0)
        grad = product(whole[0][...], matrix[:, size:], NN).astype(LOW).astype(F32)
        grad = (grad * slotted[0][0].astype(F32)).astype(LOW)
        grad_hidden[0] = grad
        hidden_sent[0] = grad
        up_sums[0] = jnp.sum(grad.astype(F32), axis=0, keepdims=True)
        add_product(lay, step, total, grad, matrix[:, :size])

        @pl.when(step == slots - 1)
        def _():
            (middle,) = late()

            def finish(start, count):
                at = pl.ds(start, count)
                term, gain_part, shift_part = norm_back(middle[at, :], total[at, :], rows[0][...])
                sums = whole[0][at, :].astype(F32) + term
                grad_middle[at, :] = sums
                grad_branch[at, :] = sums.astype(LOW)
                gains[...] += gain_part
                shifts[...] += shift_part
                out_sums[...] += jnp.sum(sums, axis=0, keepdims=True)

            row_loop(finish)

    row = wide_shape(1, width)
    return layer_call(
        lay,
        kernel,
        "dense_backward",
        [weights],
        [slope],
        [tangent],
        [middle],
        [gain_two],
        [
            low_shape(lay.shards + 1, PAD, size),
            wide_shape(slots, 1, size),
            wide_shape(PAD, width),
            low_shape(PAD, width),
            row,
            row,
            row,
            row,
        ],
        48,
    )


def attention_backward(
    lay, grad_branch, mixed, attended, logs, entry, grad_middle, weights, gain_one
):
    slots, width = lay.slots, lay.width
    part = weights[0].shape[3] // 4

    def kernel(step, weight, slotted, whole, late, rows, outs, total):
        grad_mixed, mixed_sent, qkv_sums, grad_entry, gains, shifts = outs

        @pl.when(step == 0)
        def _():
            for ref in (gains, shifts):
                ref[...] = jnp.zeros_like(ref)

        matrix = weight(0)
        upstream = product(whole[0][...], matrix[:, 3 * part :], NN).astype(LOW)
        parts = attend_back(slotted[0][0], upstream, slotted[1][0], slotted[2][0], part)
        for spot, term in enumerate(parts):
            columns = slice(spot * part, (spot + 1) * part)
            rounded = term.astype(LOW)
            grad_mixed[0, :, columns] = rounded
            mixed_sent[0, :, columns] = rounded
            qkv_sums[0, :, columns] = jnp.sum(rounded.astype(F32), axis=0, keepdims=True)
        add_product(lay, step, total, grad_mixed[0], matrix[:, : 3 * part])

        @pl.when(step == slots - 1)
        def _():
            entry, grad_middle = late()

            def finish(start, count):
                at = pl.ds(start, count)
                term, gain_part, shift_part = norm_back(
                    entry[at, :].astype(F32), total[at, :], rows[0][...]
                )
                grad_entry[at, :] = (grad_middle[at, :] + term).astype(LOW)
                gains[...] += gain_part
                shifts[...] += shift_part

            row_loop(finish)

    row = wide_shape(1, width)
    return layer_call(
        lay,
        kernel,
        "attention_backward",
        [weights],
        [mixed, attended, logs],
        [grad_branch],
        [entry, grad_middle],
        [gain_one],
        [
            low_shape(lay.shards + 1, PAD, 3 * part),
            wide_shape(slots, 1, 3 * part),
            low_shape(PAD, width),
            row,
            row,
        ],
        48,
    )


def weight_grads(lay, slot_order, pairs, cost):
    half, block, shards, width = lay.near, lay.block, lay.shards, lay.width
    sizes = [pair[2].shape[2] for pair in pairs]
    total = sum(sizes)
    whole = pl.BlockSpec((PAD, width), lambda k, s: (0, 0), pipeline_mode=pl.Buffered(1))
    specs, operands, scratch = [], [], []
    for x, x_other, feats, feats_other in pairs:
        feature_spec = pl.BlockSpec((1, PAD, feats.shape[2]), lambda k, s: (k, 0, 0))
        specs += [whole, whole, feature_spec, feature_spec]
        operands += [x, x_other, feats, feats_other]

    def kernel(_, *refs):
        far_ref, near_ref = refs[4 * len(pairs) :]
        start = 0
        for n, size in enumerate(sizes):
            x, x_other, feats, feats_other = refs[4 * n : 4 * n + 4]
            for b in range(2 * half):
                mine = slice(b * block, (b + 1) * block)
                other = slice(lay.flip[b] * block, (lay.flip[b] + 1) * block)
                grads = product(x[:, mine], feats[0], TN)
                grads = (grads + product(x_other[:, other], feats_other[0], TN)).astype(LOW)
                ref = near_ref if b < half else far_ref
                ref[b % half, 0, :, start : start + size] = grads
            start += size

    return launch(
        lay,
        kernel,
        "weight_grads",
        [slot_order],
        operands,
        specs,
        [pl.BlockSpec((half, 1, block, total), lambda k, s: (0, s[k], 0, 0))] * 2,
        [low_shape(half, shards, block, total)] * 2,
        (shards,),
        scratch,
        28,
        cost,
    )


def add_blocks(lay, *groups, cost=10**10):
    count = min(array.shape[0] - start for group in groups for array, start in group)
    widths = [group[0][0].shape[3] for group in groups]
    middle = groups[0][0][0].shape[1:3]

    def kernel(*refs):
        at, column = 0, 0
        for group, width in zip(groups, widths):
            total = refs[at][...].astype(F32)
            for ref in refs[at + 1 : at + len(group)]:
                total = total + ref[...].astype(F32)
            refs[-1][..., column : column + width] = total.astype(LOW)
            at, column = at + len(group), column + width

    def spec(start, width):
        return pl.BlockSpec((1,) + middle + (width,), lambda i: (i + start, 0, 0, 0))

    return launch(
        lay,
        kernel,
        "add_blocks",
        [],
        [array for group in groups for array, _ in group],
        [spec(start, width) for group, width in zip(groups, widths) for _, start in group],
        [spec(0, sum(widths))],
        [jax.ShapeDtypeStruct((count,) + middle + (sum(widths),), LOW)],
        (count,),
        [],
        28,
        cost,
    )[0]


def pause(lay, cost=4 * 10**10):
    def kernel(out_ref):
        out_ref[...] = jnp.zeros_like(out_ref)

    spec = pl.BlockSpec((8, 128), lambda i: (0, 0))
    shape = jax.ShapeDtypeStruct((8, 128), F32)
    launch(lay, kernel, "pause", [], [], [], [spec], [shape], (1,), [], 8, cost)


def pack_vectors(lay, sums, blocks, slot_order, core):
    rep, block, shards = lay.replicas, lay.block, lay.shards
    assert rep == shards
    wide = sums[0][1].shape[2]
    operands = [v for layer in (0, 1) for v in (*sums[layer][0], *sums[layer][1:])]

    def kernel(s, *refs):
        keep_ref, send_ref = refs[16:]
        owner = s[rep + shards]
        keep_ref[...] = jnp.zeros_like(keep_ref)
        send_ref[...] = jnp.zeros_like(send_ref)
        here, there = refs[:8], refs[8:16]

        def chosen(n, index, mine):
            first = (owner == 0) if mine else (owner != 0)
            return jnp.where(first, here[n][index], there[n][index])

        for out_ref, mine in ((keep_ref, True), (send_ref, False)):
            for n in range(6):
                for b in range(rep):
                    columns = slice(b * block, (b + 1) * block)
                    value = chosen(n, (slice(None), columns), mine)
                    out_ref[s[b] ^ s[rep], n : n + 1, :block] = value
            for side in range(2):
                half = side ^ owner
                for k in range(shards):
                    slot = side * shards + k
                    ups = chosen(6, slot, mine)
                    parts = chosen(7, slot, mine)
                    out_ref[k, pl.ds(8 + half, 1), :] = ups
                    out_ref[k, pl.ds(6 + half, 1), : parts.shape[1]] = parts

    def spec(array):
        return pl.BlockSpec(array.shape, lambda i, s, n=array.ndim: (0,) * n)

    scalars = jnp.concatenate([blocks, slot_order, core[None]])
    shape = jax.ShapeDtypeStruct((shards, 16, wide), F32)
    keep, send = launch(
        lay,
        kernel,
        "pack_vectors",
        [scalars],
        operands,
        [spec(v) for v in operands],
        [pl.BlockSpec(shape.shape, lambda i, s: (0, 0, 0))] * 2,
        [shape] * 2,
        (1,),
        [],
        8,
    )
    return keep, send


def shards(
    boundary_in,
    counts,
    w_qkv,
    b_qkv,
    w_out,
    b_out,
    w_up,
    b_up,
    w_down,
    b_down,
    norm1_gain,
    norm1_shift,
    norm2_gain,
    norm2_shift,
):
    width = boundary_in.shape[4]
    sizes = {axis: lax.axis_size(axis) for axis in ALL_AXES}
    lay = Layout(sizes, width)
    core = lax.axis_index("section").astype(jnp.int32)
    shard = lax.axis_index("shard").astype(jnp.int32)
    replica = lax.axis_index("replica").astype(jnp.int32)
    on_first = core == 0
    heads_wide = w_qkv.shape[3]
    part = heads_wide // 2
    ff_part = w_up.shape[2] // 2
    positions = jnp.arange(lay.replicas, dtype=jnp.int32)
    flips = jnp.asarray(lay.flip, jnp.int32)
    blocks = jnp.where(on_first, positions, flips) ^ replica
    inverse_blocks = jnp.where(on_first, positions ^ replica, flips[positions ^ replica])
    halves = jnp.arange(2, dtype=jnp.int32) ^ core
    scalars = jnp.concatenate([blocks, halves, core[None]])

    slot_order = jnp.arange(lay.shards, dtype=jnp.int32) ^ shard

    raw_qkv = w_qkv[0].reshape(width, 6 * part)
    raw_out, raw_up, raw_down = w_out[0], w_up[0], w_down[0]
    split_pieces = first_pieces(lay, raw_qkv, raw_out, raw_up, raw_down, scalars)
    first, second = [], []
    for piece, sent in zip(split_pieces[:2], split_pieces[2:]):
        other = lay.across_cores(sent)
        first.append(jnp.where(on_first, piece, other))
        second.append(jnp.where(on_first, other, piece))
    pieces = first + second
    (pictures,) = lay.hold(boundary_in[0, :, 0])
    received = lay.across_cores(pictures)
    live = (shard < counts[replica, core]).astype(F32)[None]
    gather = Gather(lay, slot_order, pieces)
    gather.start(0)
    image, cot = arrange_images(lay, pictures, received, blocks, core, live)

    raws = (raw_qkv, raw_out, raw_up, raw_down)
    raws_other = [lay.across_cores(raw) for raw in raws]
    own_attention = arrange_attention(lay, raws[:2], raws_other[:2], scalars)

    packed = jnp.concatenate(
        [v[0] for v in (b_out, b_down, norm1_gain, norm1_shift, norm2_gain, norm2_shift)]
        + [b_qkv.reshape(-1), b_up.reshape(-1)]
    )
    packed_other = lay.across_cores(packed)
    both = jnp.stack(
        [jnp.where(on_first, packed, packed_other), jnp.where(on_first, packed_other, packed)]
    )
    wide = both[:, : 6 * width].reshape(2, 6, lay.replicas, lay.block)
    wide = jnp.take(wide, blocks, axis=2).reshape(2, 6, 1, width).astype(F32)
    split = both[:, 6 * width :]
    split = jnp.stack([split] + [lay.along_shard(split, k) for k in range(1, lay.shards)])
    split_qkv = split[:, :, : 4 * part].reshape(lay.shards, 2, 2, 2, part)
    split_qkv = jnp.take(split_qkv, halves, axis=3).transpose(1, 3, 0, 2, 4)
    split_qkv = split_qkv.reshape(2, lay.slots, 2, part)
    bias_qkv = jnp.concatenate(
        [split_qkv[:, :, 0], jnp.zeros_like(split_qkv[:, :, 0]), split_qkv[:, :, 1]], axis=-1
    ).reshape(2, lay.slots, 1, 3 * part).astype(F32)
    bias_up = split[:, :, 4 * part :].reshape(lay.shards, 2, 2, ff_part)
    bias_up = jnp.take(bias_up, halves, axis=2).transpose(1, 2, 0, 3)
    bias_up = bias_up.reshape(2, lay.slots, 1, ff_part).astype(F32)

    kept, weights = [], []
    entry = image
    gather.step(0)
    gather.start(1)
    gather.step(0)
    gather.start(2)
    gather.step(1)
    gather.start(3)
    w_attention = gather.finish(0, own_attention[0])
    for layer in range(2):
        vec_out, vec_down, gain_one, shift_one, gain_two, shift_two = wide[layer]
        normed, mixed, attended, logs, middle, normed_two = attention_forward(
            lay,
            entry,
            w_attention,
            bias_qkv[layer],
            (gain_one, shift_one, vec_out, gain_two, shift_two),
        )
        exchanged = [
            lay.across_cores(value) for value in (normed, normed_two, attended[lay.shards :])
        ]
        if layer == 0:
            gather.step(1)
            gather.step(2)
            lay.absorb(*exchanged)
            own_dense = arrange_dense(lay, raws[2:], raws_other[2:], scalars)
            gather.step(3)
            w_dense = gather.finish(1, own_dense[0])
            gather.step(2)
            pause(lay)
        else:
            w_dense = gather.finish(3, own_dense[1])
            lay.absorb(kept[0][-1][-1])
            pause(lay)
        active, active_sent, slope, result = dense_forward(
            lay,
            normed_two,
            middle,
            w_dense,
            bias_up[layer],
            vec_down,
        )
        weights.append((w_attention, w_dense))
        exchanged.append(lay.across_cores(active_sent))
        if layer == 0:
            w_attention = gather.finish(2, own_attention[1])
            gather.step(3)
            pause(lay)
        kept.append(
            (entry, normed, mixed, attended, logs, middle, normed_two, active, slope, exchanged)
        )
        entry = result

    terms, sums, vector_sums, latest = {}, {}, {}, {}

    def begin(name, *pairs, cost=1000):
        far, near = weight_grads(lay, slot_order, pairs, cost)
        arrived = lay.along_bit(far, lay.bits - 1)
        terms[name] = [(near, 0), (arrived, 0)]

    def halve(name, cost=10**10):
        for bit in range(lay.bits - 2, -1, -1):
            split = 1 << bit
            group = [(array, start + split) for array, start in terms[name]]
            sent = add_blocks(lay, group, cost=cost)
            terms[name] = terms[name] + [(lay.along_bit(sent, bit), 0)]

    def collect(names, direct, cost=10**10, beside=None):
        total = add_blocks(lay, *(terms[name] for name in names), cost=cost)[0]
        if beside is not None:
            total, beside = lax.optimization_barrier((total, beside))
        if direct:
            latest[names] = lax.all_to_all(total, "shard", 0, 0, tiled=True)
        else:
            latest[names] = lax.psum_scatter(total, "shard", scatter_dimension=0)[None]
        return beside

    def settle(*all_names):
        for names, total in zip(all_names, lay.hold(*(latest[names] for names in all_names))):
            spread(names, total)

    def spread(names, total):
        total = jnp.sum(total.astype(F32), axis=0)
        at = 0
        for name in names:
            size = terms[name][0][0].shape[3]
            sums[name] = total[:, at : at + size]
            at += size

    tangent = cot
    for layer in (1, 0):
        w_attention, w_dense = weights[layer]
        vec_out, vec_down, gain_one, shift_one, gain_two, shift_two = wide[layer]
        entry_in, normed, mixed, attended, logs, middle, normed_two, active, slope, other = kept[layer]
        normed_other, normed_two_other, attended_other, active_other = other
        if layer == 1:
            begin((1, "down"), (tangent, lay.across_cores(tangent), active, active_other))
        (
            grad_hidden,
            hidden_sent,
            up_sums,
            grad_middle,
            grad_branch,
            down_sums,
            gain_two_sum,
            shift_two_sum,
            out_sums,
        ) = dense_backward(lay, tangent, slope, middle, w_dense, gain_two)
        branch_other, hidden_other = lay.across_cores(grad_branch), lay.across_cores(hidden_sent)
        out_pair = (grad_branch, branch_other, attended, attended_other)
        if layer == 1:
            halve((1, "down"))
        else:
            settle(((1, "down"),))
            collect(((1, "out"), (1, "up")), False)
            halve((0, "down"))
        begin((layer, "out"), out_pair, cost=4 * 10**10)
        if layer == 0:
            halve((1, "qkv"))
        begin((layer, "up"), (normed_two, normed_two_other, grad_hidden, hidden_other))
        if layer == 0:
            collect(((1, "qkv"), (0, "down")), True)
        grad_mixed, mixed_sent, qkv_sums, grad_entry, gain_one_sum, shift_one_sum = (
            attention_backward(
                lay,
                grad_branch,
                mixed,
                attended,
                logs,
                entry_in,
                grad_middle,
                w_attention,
                gain_one,
            )
        )
        tangent = grad_entry
        if layer == 1:
            mixed_other = lay.across_cores(mixed_sent)
        vector_sums[layer] = (
            [out_sums, down_sums, gain_one_sum, shift_one_sum, gain_two_sum, shift_two_sum],
            up_sums,
            qkv_sums,
        )
        if layer == 1:
            collect(((1, "down"),), False)
        if layer == 0:
            keep, send = pack_vectors(lay, vector_sums, blocks, slot_order, core)
            send = lay.across_cores(send)
        halve((layer, "out"))
        if layer == 0:
            (send,) = lay.hold(send)
            summed = keep + send
        if layer == 0:
            (mixed_sent,) = lay.hold(mixed_sent)
            mixed_other = lay.across_cores(mixed_sent)
        halve((layer, "up"))
        if layer == 1:
            active, active_other = kept[0][7], kept[0][9][3]
            begin((0, "down"), (tangent, lay.across_cores(tangent), active, active_other))
        begin((layer, "qkv"), (normed, normed_other, grad_mixed, mixed_other))
    (summed,) = lay.hold(summed)
    coming = lay.along_bit_plain(summed, 0)
    settle(((1, "out"), (1, "up")))
    back = restore_image(lay, tangent, blocks, jnp.ones((1,), F32))
    ahead = restore_image(lay, entry, blocks, live)
    (coming,) = lay.hold(coming)
    for bit in range(1, lay.bits):
        summed = summed + coming
        coming = lay.along_bit_plain(summed, bit)
    collect(((0, "out"), (0, "up")), False, cost=2 * 10**10)
    halve((0, "qkv"), cost=1000)
    settle(((1, "qkv"), (0, "down")))
    back, ahead, coming = lay.hold(back, ahead, coming)
    summed = summed + coming
    coming = [lay.along_shard(summed[k], k) for k in range(1, lay.shards)]
    coming = collect(((0, "qkv"),), True, cost=1000, beside=coming)
    summed = sum(coming, summed[0])
    last = (((0, "out"), (0, "up")), ((0, "qkv"),))
    for names, total in zip(last, lax.optimization_barrier([latest[names] for names in last])):
        spread(names, total)

    def to_owner(first, second):
        keep = jnp.where(on_first, first, second)
        other = lay.across_cores(jnp.where(on_first, second, first))
        return jnp.where(on_first, keep, other), jnp.where(on_first, other, keep)

    down_halves = to_owner(sums[0, "down"], sums[1, "down"])
    up_halves = to_owner(sums[0, "up"], sums[1, "up"])
    out_halves = to_owner(sums[0, "out"], sums[1, "out"])
    qkv_halves = to_owner(sums[0, "qkv"], sums[1, "qkv"])
    grad_w_down = jnp.concatenate(down_halves, axis=1).T[None]
    grad_w_up = jnp.concatenate(up_halves, axis=1)[None]
    grad_w_qkv = jnp.stack(
        [half.reshape(-1, 3, part) for half in qkv_halves], axis=2
    ).reshape(1, lay.block, 3, heads_wide)
    grad_w_out = jnp.concatenate(out_halves, axis=1).T[None]

    share = lay.block // lay.replicas
    model = lax.dynamic_slice_in_dim(summed[:6, : lay.block], replica * share, share, 1)
    vectors = [model[i : i + 1] for i in range(6)]
    parts = summed[6:8, : 3 * part].reshape(2, 3, part)
    parts = jnp.stack([parts[:, 0], parts[:, 2]]).reshape(2, 2 * part)
    grad_b_qkv = lax.dynamic_slice_in_dim(parts, replica * share, share, 1)[None]
    share_up = 2 * ff_part // lay.replicas
    ups = summed[8:10, :ff_part].reshape(1, 2 * ff_part)
    grad_b_up = lax.dynamic_slice_in_dim(ups, replica * share_up, share_up, 1)

    keep = jnp.where(on_first, back, ahead)
    other = lay.across_cores(jnp.where(on_first, ahead, back))
    boundary_out = jnp.stack([jnp.where(on_first, keep, other), jnp.where(on_first, other, keep)])
    boundary_out = boundary_out[None, :, None]
    return (
        boundary_out,
        grad_w_qkv,
        grad_b_qkv,
        grad_w_out,
        vectors[0],
        grad_w_up,
        grad_b_up,
        grad_w_down,
        vectors[1],
        vectors[2],
        vectors[3],
        vectors[4],
        vectors[5],
    )


def solution(mesh):
    spread = P("section", ("shard", "replica"))
    return jax.shard_map(
        shards,
        mesh=mesh,
        in_specs=(
            P("section", None, ("shard", "replica"), None, None),
            P(),
            P("section", None, None, "shard"),
            P("section", None, "shard"),
            P("section", "shard", None),
            P("section", None),
            P("section", None, "shard"),
            P("section", "shard"),
            P("section", "shard", None),
            P("section", None),
            P("section", None),
            P("section", None),
            P("section", None),
            P("section", None),
        ),
        out_specs=(
            P("section", None, ("shard", "replica"), None, None),
            P("section", "replica", None, "shard"),
            P("section", None, ("shard", "replica")),
            P("section", "shard", "replica"),
            spread,
            P("section", "replica", "shard"),
            spread,
            P("section", "shard", "replica"),
            spread,
            spread,
            spread,
            spread,
            spread,
        ),
        check_vma=False,
    )
```

```python
import functools

import jax
import jax.numpy as jnp
from jax import lax
from jax.experimental import pallas as pl
from jax.experimental.pallas import tpu as pltpu
from jax.sharding import PartitionSpec as P

HEAD = 64
SEQ = 577
PAD = 592
CHUNK = 144
LOW = jnp.bfloat16
F32 = jnp.float32
ALL_AXES = ("section", "shard", "replica")
NT = (((1,), (1,)), ((), ()))
NN = (((1,), (0,)), ((), ()))
TN = (((0,), (0,)), ((), ()))


def reverse_bits(value, bits):
    flipped = 0
    for spot in range(bits):
        flipped |= ((value >> spot) & 1) << (bits - 1 - spot)
    return flipped


def product(left, right, dims):
    return lax.dot_general(left, right, dims, preferred_element_type=F32)


def row_loop(body):
    whole = PAD // CHUNK

    def step(index, carry):
        body(pl.multiple_of(index * CHUNK, 16), CHUNK)
        return carry

    lax.fori_loop(0, whole, step, 0)
    if PAD % CHUNK:
        body(whole * CHUNK, PAD % CHUNK)


def params(megabytes=48):
    return pltpu.CompilerParams(vmem_limit_bytes=megabytes * 2**20)


def launch(
    lay, kernel, name, scalars, operands, in_specs, out_specs, out_shape, grid, scratch, megabytes, cost=1000
):
    tokens = lay.after
    count = len(scalars) + len(operands)

    def ordered(*refs):
        rest = refs[count + len(tokens) :]
        rest[len(out_shape)][...] = jnp.zeros((8, 128), F32)
        kernel(*refs[:count], *rest[: len(out_shape)], *rest[len(out_shape) + 1 :])

    token_spec = pl.BlockSpec((8, 128), lambda *_: (0, 0))
    results = pl.pallas_call(
        ordered,
        grid_spec=pltpu.PrefetchScalarGridSpec(
            num_scalar_prefetch=len(scalars),
            grid=grid,
            in_specs=list(in_specs) + [pl.BlockSpec(memory_space=pl.ANY)] * len(tokens),
            out_specs=list(out_specs) + [token_spec],
            scratch_shapes=scratch,
        ),
        out_shape=list(out_shape) + [jax.ShapeDtypeStruct((8, 128), F32)],
        compiler_params=params(megabytes),
        cost_estimate=pl.CostEstimate(flops=cost, bytes_accessed=2**18, transcendentals=0),
        name=name,
    )(*scalars, *operands, *tokens)
    lay.after = [results[-1]]
    return results[:-1]


def normalized(values):
    center = values - jnp.mean(values, axis=-1, keepdims=True)
    spread = jnp.mean(center * center, axis=-1, keepdims=True)
    inverse = lax.rsqrt(spread + 1e-06)
    return center * inverse, inverse


class Layout:
    def __init__(self, mesh_shape, width):
        self.shards = mesh_shape["shard"]
        self.replicas = mesh_shape["replica"]
        self.bits = self.replicas.bit_length() - 1
        self.width = width
        self.block = width // self.replicas
        self.flip = [reverse_bits(b, self.bits) for b in range(self.replicas)]
        self.near = self.replicas // 2
        self.slots = 2 * self.shards
        self.after = []

    def absorb(self, *values):
        for value in values:
            corner = value.reshape((-1,) + value.shape[-2:])[0, :8, :128]
            self.after.append(corner)

    def hold(self, *values):
        values, self.after = lax.optimization_barrier((values, self.after))
        return values

    def across_cores(self, value):
        return lax.ppermute(value, "section", [(0, 1), (1, 0)])

    def along_shard(self, value, slot):
        return lax.ppermute(value, "shard", [(i, i ^ slot) for i in range(self.shards)])

    def along_bit_plain(self, value, bit):
        route = [(i, i ^ (1 << bit)) for i in range(self.replicas)]
        return lax.ppermute(value, "replica", route)

    def along_bit(self, value, bit):
        route = []
        for core in range(2):
            physical = bit if core == 0 else self.bits - 1 - bit
            for shard in range(self.shards):
                base = (core * self.shards + shard) * self.replicas
                for replica in range(self.replicas):
                    route.append((base + replica, base + (replica ^ (1 << physical))))
        return lax.ppermute(value, ALL_AXES, route)


def arrange_images(lay, mine, received, blocks, core, live):
    width, block = lay.width, lay.block

    def kernel(scalars, live_ref, mine_ref, other_ref, image_ref, cot_ref):
        here = mine_ref[0]
        there = other_ref[0]
        first = scalars[lay.replicas] == 0
        image = jnp.where(first, here, there)
        cot = jnp.where(first, there, here).astype(F32) * live_ref[0]
        image_ref[...] = jnp.zeros_like(image_ref)
        cot_ref[...] = jnp.zeros_like(cot_ref)
        image_ref[0:SEQ, :] = image
        cot_ref[0:SEQ, :] = cot.astype(LOW)

    scalars = jnp.concatenate([blocks, core[None]]).astype(jnp.int32)
    shape = jax.ShapeDtypeStruct((PAD, width), LOW)
    whole = pl.BlockSpec((1, SEQ, block), lambda b, s: (s[lay.replicas], 0, s[b]))
    return launch(
        lay,
        kernel,
        "arrange_images",
        [scalars],
        [live, mine, received],
        [pl.BlockSpec(memory_space=pltpu.SMEM), whole, whole],
        [pl.BlockSpec((PAD, block), lambda b, s: (0, b))] * 2,
        [shape, shape],
        (lay.replicas,),
        [],
        24,
    )


def restore_image(lay, values, blocks, scale):
    def kernel(scalars, scale_ref, in_ref, out_ref):
        out_ref[...] = (in_ref[0:SEQ, :].astype(F32) * scale_ref[0]).astype(LOW)

    return launch(
        lay,
        kernel,
        "restore_image",
        [blocks],
        [scale, values],
        [
            pl.BlockSpec(memory_space=pltpu.SMEM),
            pl.BlockSpec((PAD, lay.block), lambda b, s: (0, b)),
        ],
        [pl.BlockSpec((SEQ, lay.block), lambda b, s: (0, s[b]))],
        [jax.ShapeDtypeStruct((SEQ, lay.width), LOW)],
        (lay.replicas,),
        [],
        16,
    )[0]


def chosen_half(flag, low, high):
    return jnp.where(flag == 0, low, high)


def arrange_attention(lay, mine, received, scalars):
    rep, block = lay.replicas, lay.block
    part = mine[1].shape[0] // 2

    def kernel(s, qkv_mine, qkv_other, out_mine, out_other, first_ref, second_ref):
        first = s[rep + 2] == 0
        half = s[rep + pl.program_id(0)]

        def columns(ref, t):
            start = 2 * t * part
            return chosen_half(
                half, ref[:, start : start + part], ref[:, start + part : start + 2 * part]
            )

        for t in range(3):
            here, there = columns(qkv_mine, t), columns(qkv_other, t)
            first_ref[0, 0, :, t * part : (t + 1) * part] = jnp.where(first, here, there)
            second_ref[0, 0, :, t * part : (t + 1) * part] = jnp.where(first, there, here)
        here, there = out_mine[...].T, out_other[...].T
        first_ref[0, 0, :, 3 * part :] = jnp.where(first, here, there)
        second_ref[0, 0, :, 3 * part :] = jnp.where(first, there, here)

    shape = jax.ShapeDtypeStruct((2, rep, block, 4 * part), LOW)
    qkv_spec = pl.BlockSpec((block, 6 * part), lambda p, b, s: (s[b], 0))
    out_spec = pl.BlockSpec((part, block), lambda p, b, s: (s[rep + p], s[b]))
    return launch(
        lay,
        kernel,
        "arrange_attention",
        [scalars],
        [mine[0], received[0], mine[1], received[1]],
        [qkv_spec, qkv_spec, out_spec, out_spec],
        [pl.BlockSpec((1, 1, block, 4 * part), lambda p, b, s: (p, b, 0, 0))] * 2,
        [shape, shape],
        (2, rep),
        [],
        16,
    )


def arrange_dense(lay, mine, received, scalars):
    rep, block = lay.replicas, lay.block
    part = mine[0].shape[1] // 2

    def kernel(s, up_mine, up_other, down_mine, down_other, first_ref, second_ref):
        first = s[rep + 2] == 0
        here, there = up_mine[...], up_other[...]
        first_ref[0, 0, :, :part] = jnp.where(first, here, there)
        second_ref[0, 0, :, :part] = jnp.where(first, there, here)
        here, there = down_mine[...].T, down_other[...].T
        first_ref[0, 0, :, part:] = jnp.where(first, here, there)
        second_ref[0, 0, :, part:] = jnp.where(first, there, here)

    shape = jax.ShapeDtypeStruct((2, rep, block, 2 * part), LOW)
    up_spec = pl.BlockSpec((block, part), lambda p, b, s: (s[b], s[rep + p]))
    down_spec = pl.BlockSpec((part, block), lambda p, b, s: (s[rep + p], s[b]))
    return launch(
        lay,
        kernel,
        "arrange_dense",
        [scalars],
        [mine[0], received[0], mine[1], received[1]],
        [up_spec, up_spec, down_spec, down_spec],
        [pl.BlockSpec((1, 1, block, 2 * part), lambda p, b, s: (p, b, 0, 0))] * 2,
        [shape] * 2,
        (2, rep),
        [],
        16,
    )


def first_pieces(lay, qkv, out, up, down, scalars):
    rep, block = lay.replicas, lay.block
    part, wide = out.shape[0] // 2, up.shape[1] // 2

    def kernel(s, qkv_ref, out_ref, up_ref, down_ref, *outs):
        core = s[rep + 2]
        for flag, attention_ref, dense_ref in ((core, *outs[:2]), (1 - core, *outs[2:])):
            for t in range(3):
                start = 2 * t * part
                attention_ref[:, t * part : (t + 1) * part] = chosen_half(
                    flag,
                    qkv_ref[:, start : start + part],
                    qkv_ref[:, start + part : start + 2 * part],
                )
            attention_ref[:, 3 * part :] = chosen_half(flag, out_ref[:part], out_ref[part:]).T
            dense_ref[:, :wide] = chosen_half(flag, up_ref[:, :wide], up_ref[:, wide:])
            dense_ref[:, wide:] = chosen_half(flag, down_ref[:wide], down_ref[wide:]).T

    attention_shape = jax.ShapeDtypeStruct((block, 4 * part), LOW)
    dense_shape = jax.ShapeDtypeStruct((block, 2 * wide), LOW)
    attention_spec = pl.BlockSpec((block, 4 * part), lambda i, s: (0, 0))
    dense_spec = pl.BlockSpec((block, 2 * wide), lambda i, s: (0, 0))
    return launch(
        lay,
        kernel,
        "first_pieces",
        [scalars],
        [qkv, out, up, down],
        [
            pl.BlockSpec((block, 6 * part), lambda i, s: (s[0], 0)),
            pl.BlockSpec((2 * part, block), lambda i, s: (0, s[0])),
            pl.BlockSpec((block, 2 * wide), lambda i, s: (s[0], 0)),
            pl.BlockSpec((2 * wide, block), lambda i, s: (0, s[0])),
        ],
        [attention_spec, dense_spec] * 2,
        [attention_shape, dense_shape] * 2,
        (1,),
        [],
        16,
    )


def pick_slots(lay, gathered, slot_order):
    rows, columns = gathered.shape[1:]

    def kernel(_, in_ref, out_ref):
        out_ref[0] = in_ref[...]

    return launch(
        lay,
        kernel,
        "pick_slots",
        [slot_order],
        [gathered],
        [pl.BlockSpec((1, rows, columns), lambda k, s: (s[k + 1], 0, 0))],
        [pl.BlockSpec((1, 1, rows, columns), lambda k, s: (0, k, 0, 0))],
        [jax.ShapeDtypeStruct((1, lay.shards - 1, rows, columns), LOW)],
        (lay.shards - 1,),
        [],
        8,
    )[0]


def join(lay, first, second):
    count, rows = first.shape[0], first.shape[1]
    shape = (2 * count,) + first.shape[1:]
    block = (1, rows) + first.shape[2:]

    def kernel(first_ref, second_ref, out_ref):
        step = pl.program_id(0)

        @pl.when(step < count)
        def _():
            out_ref[...] = first_ref[...]

        @pl.when(step >= count)
        def _():
            out_ref[...] = second_ref[...]

    return launch(
        lay,
        kernel,
        "join",
        [],
        [first, second],
        [
            pl.BlockSpec(block, lambda i: (jnp.minimum(i, count - 1), 0, 0, 0)),
            pl.BlockSpec(block, lambda i: (jnp.maximum(i - count, 0), 0, 0, 0)),
        ],
        [pl.BlockSpec(block, lambda i: (i, 0, 0, 0))],
        [jax.ShapeDtypeStruct(shape, LOW)],
        (2 * count,),
        [],
        16,
    )[0]


def copied(lay, value):
    def kernel(in_ref, out_ref):
        out_ref[...] = in_ref[...]

    spec = pl.BlockSpec(value.shape, lambda i: (0, 0))
    shape = jax.ShapeDtypeStruct(value.shape, value.dtype)
    return launch(lay, kernel, "copied", [], [value], [spec], [spec], [shape], (1,), [], 8)[0]


class Gather:
    def __init__(self, lay, slot_order, pieces):
        self.lay, self.pieces, self.slot_order = lay, pieces, slot_order
        self.state = [None] * len(pieces)
        self.done = [0] * len(pieces)

    def start(self, n):
        piece = self.pieces[n] if n == 0 else copied(self.lay, self.pieces[n])
        self.state[n] = lax.all_gather(piece, "shard")

    def step(self, n):
        lay = self.lay
        if self.done[n] == 0:
            near = pick_slots(lay, self.state[n], self.slot_order)
        else:
            near = join(lay, *self.state[n])
        self.state[n] = (near, lay.along_bit(near, self.done[n]))
        self.done[n] += 1

    def settle(self, n):
        near, arrived = self.state[n]
        self.state[n] = (near, *self.lay.hold(arrived))

    def finish(self, n, own):
        lay = self.lay
        while self.done[n] < lay.bits:
            self.step(n)
        near, far = self.state[n]
        (far,) = lay.hold(far)
        return (own, near, far, lay.across_cores(near), lay.across_cores(far))


def fetch_weights(lay, refs, held, sems, slot):
    own, near, far, near_other, far_other = refs
    half = lay.near
    side, k = divmod(slot, lay.shards)

    def start(source, target):
        pltpu.make_async_copy(source, target, sems.at[slot]).start()

    if k == 0:
        start(own.at[side], held.at[slot])
    elif side == 0:
        start(near.at[:, k - 1], held.at[slot, 0:half])
        start(far.at[:, k - 1], held.at[slot, half : 2 * half])
    else:
        for b in range(half):
            start(near_other.at[b, k - 1], held.at[slot, lay.flip[b]])
            start(far_other.at[b, k - 1], held.at[slot, lay.flip[half + b]])


def await_weights(held, sems, slot):
    pltpu.make_async_copy(held.at[slot], held.at[slot], sems.at[slot]).wait()


def flat(block):
    return block.reshape(block.shape[0] * block.shape[1], block.shape[2])


def layer_call(lay, kernel, name, weights, slotted, whole, late, rows, outs, megabytes):
    slots, width, shards = lay.slots, lay.width, lay.shards
    once = dict(pipeline_mode=pl.Buffered(1))

    def own_half(i):
        return (jnp.minimum(i, shards), 0, 0)

    def other_half(i):
        return (jnp.where(i < shards, shards, i - shards), 0, 0)

    def spec(shape, **mode):
        if len(shape) == 3:
            return pl.BlockSpec((1,) + shape[1:], lambda i: (i, 0, 0))
        return pl.BlockSpec(shape, lambda i: (0, 0), **mode)

    out_specs, out_shape = [], []
    for o in outs:
        if len(o.shape) == 3 and o.shape[0] == shards + 1:
            out_specs += [pl.BlockSpec((1,) + o.shape[1:], m) for m in (own_half, other_half)]
            out_shape += [o, o]
        else:
            out_specs.append(spec(o.shape))
            out_shape.append(o)
    outs = out_shape
    anywhere = pl.BlockSpec(memory_space=pltpu.HBM)
    counts = [5 * len(weights), len(slotted), len(whole), len(late), len(rows), len(outs)]

    def body(*refs):
        groups, at = [], 0
        for count in counts + [1, len(weights), len(weights), len(late)]:
            groups.append(refs[at : at + count])
            at += count
        arrays, slot_refs, whole_refs, late_refs, row_refs, out_refs = groups[:6]
        (total,), held, sems, late_held = groups[6:10]
        late_sem = refs[at] if late else None
        step = pl.program_id(0)

        def late_copy(n):
            return pltpu.make_async_copy(late_refs[n], late_held[n], late_sem.at[n])

        @pl.when(step == 0)
        def _():
            for slot in range(slots):
                for n in range(len(weights)):
                    fetch_weights(lay, arrays[5 * n : 5 * n + 5], held[n], sems[n], slot)
            for n in range(len(late)):
                late_copy(n).start()

        def weight(n):
            await_weights(held[n], sems[n], step)
            return flat(held[n][step])

        def late_values():
            for n in range(len(late)):
                late_copy(n).wait()
            return late_held

        kernel(step, weight, slot_refs, whole_refs, late_values, row_refs, out_refs, total)

    arrays = [array for matrix in weights for array in matrix]
    scratch = [pltpu.VMEM((PAD, width), F32)]
    scratch += [pltpu.VMEM((slots,) + matrix[0].shape[1:], LOW) for matrix in weights]
    scratch += [pltpu.SemaphoreType.DMA((slots,)) for _ in weights]
    scratch += [pltpu.VMEM(a.shape, a.dtype) for a in late]
    if late:
        scratch.append(pltpu.SemaphoreType.DMA((len(late),)))
    return launch(
        lay,
        body,
        name,
        [],
        [*arrays, *slotted, *whole, *late, *rows],
        [anywhere] * len(arrays)
        + [spec(a.shape) for a in slotted]
        + [spec(a.shape, **once) for a in whole]
        + [anywhere] * len(late)
        + [spec(a.shape, **once) for a in rows],
        out_specs,
        out_shape,
        (slots,),
        scratch,
        megabytes,
    )


def add_product(lay, step, total, acts, matrix):
    for b in range(lay.replicas):
        columns = slice(b * lay.block, (b + 1) * lay.block)
        term = product(acts, matrix[columns], NT)
        total[:, columns] = jnp.where(step == 0, 0.0, total[:, columns]) + term


def low_shape(*shape):
    return jax.ShapeDtypeStruct(shape, LOW)


def wide_shape(*shape):
    return jax.ShapeDtypeStruct(shape, F32)


def mask_keys(scores, low):
    edge = SEQ // 16 * 16
    valid = lax.broadcasted_iota(jnp.int32, (PAD - edge, 1), 0) < SEQ - edge
    return jnp.concatenate([scores[:edge], jnp.where(valid, scores[edge:], low)], axis=0)


def attend(block, part):
    query, keys, values = block[:, :part], block[:, part : 2 * part], block[:, 2 * part :]
    heads = range(part // HEAD)
    lanes = lax.broadcasted_iota(jnp.int32, (1, part), 1) // HEAD
    query = query * HEAD ** (-0.5)
    turned = values.T
    ones = jnp.ones((16, PAD), LOW)
    scores = [product(keys, jnp.where(lanes == h, query, 0), NT) for h in heads]
    scores = [mask_keys(score, -1e30) for score in scores]
    peaks = [jnp.max(score, axis=0, keepdims=True) for score in scores]
    weights = [jnp.exp(score - peak).astype(LOW) for score, peak in zip(scores, peaks)]
    sums = [
        product(jnp.concatenate([turned[h * HEAD : (h + 1) * HEAD], ones], axis=0), weights[h], NN)
        for h in heads
    ]
    result = jnp.concatenate([s[:HEAD] / s[HEAD : HEAD + 1] for s in sums], axis=0).T
    spot = lax.broadcasted_iota(jnp.int32, (8, 1), 0)
    logs = jnp.zeros((8, PAD), F32)
    for h in heads:
        logs = jnp.where(spot == h, peaks[h] + jnp.log(sums[h][HEAD : HEAD + 1]), logs)
    return result.astype(LOW), logs


def attend_back(block, grads, attended, logs, part):
    query, keys, values = block[:, :part], block[:, part : 2 * part], block[:, 2 * part :]
    heads = range(part // HEAD)
    lanes = lax.broadcasted_iota(jnp.int32, (1, part), 1) // HEAD
    wide = lax.broadcasted_iota(jnp.int32, (1, 128), 1)
    query = query * HEAD ** (-0.5)

    def pick(h, array):
        return jnp.where(lanes == h, array, 0)

    along = grads.astype(F32) * attended.astype(F32)
    inner = jnp.zeros((PAD, 128), F32)
    for h in heads:
        inner = jnp.where(wide == h, jnp.sum(pick(h, along), axis=-1, keepdims=True), inner)
    inner = inner.T
    scores = [product(keys, pick(h, query), NT) for h in heads]
    slopes = [product(values, pick(h, grads), NT) for h in heads]
    chances = [mask_keys(jnp.exp(scores[h] - logs[h : h + 1]), 0.0) for h in heads]
    grad_scores = [(chances[h] * (slopes[h] - inner[h : h + 1])).astype(LOW) for h in heads]
    low = [chance.astype(LOW) for chance in chances]
    value_terms = [product(low[h], grads, NN) for h in heads]
    key_terms = [product(grad_scores[h], query, NN) for h in heads]
    turned = keys.T
    query_terms = [
        product(turned[h * HEAD : (h + 1) * HEAD], grad_scores[h], NN) for h in heads
    ]

    def merge(terms):
        result = terms[0]
        for h in heads:
            result = jnp.where(lanes == h, terms[h], result)
        return result

    return (
        jnp.concatenate(query_terms, axis=0).T * HEAD ** (-0.5),
        merge(key_terms),
        merge(value_terms),
    )


def norm_back(values, grads, gain):
    values, inverse = normalized(values)
    slope = grads * gain
    mean = jnp.mean(slope, axis=-1, keepdims=True)
    along = jnp.mean(slope * values, axis=-1, keepdims=True)
    term = inverse * (slope - mean - values * along)
    return (
        term,
        jnp.sum(grads * values, axis=0, keepdims=True),
        jnp.sum(grads, axis=0, keepdims=True),
    )


def attention_forward(lay, entry, weights, bias, rows):
    slots, width = lay.slots, lay.width
    part = weights[0].shape[3] // 4

    def kernel(step, weight, slotted, whole, late, rows, outs, total):
        normed, mixed, attended, logs, middle, normed_two = outs

        @pl.when(step == 0)
        def _():
            def norm_rows(start, count):
                values, _ = normalized(whole[0][pl.ds(start, count), :].astype(F32))
                normed[pl.ds(start, count), :] = (values * rows[0][...] + rows[1][...]).astype(LOW)

            row_loop(norm_rows)

        matrix = weight(0)
        block = (product(normed[...], matrix[:, : 3 * part], NN) + slotted[0][0]).astype(LOW)
        mixed[0] = block
        result, log_rows = attend(block, part)
        attended[0] = result
        logs[0] = log_rows
        add_product(lay, step, total, result, matrix[:, 3 * part :])

        @pl.when(step == slots - 1)
        def _():
            def finish(start, count):
                at = pl.ds(start, count)
                sums = whole[0][at, :].astype(F32) + total[at, :] + rows[2][...]
                middle[at, :] = sums
                values, _ = normalized(sums)
                normed_two[at, :] = (values * rows[3][...] + rows[4][...]).astype(LOW)

            row_loop(finish)

    return layer_call(
        lay,
        kernel,
        "attention_forward",
        [weights],
        [bias],
        [entry],
        [],
        rows,
        [
            low_shape(PAD, width),
            low_shape(slots, PAD, 3 * part),
            low_shape(slots, PAD, part),
            wide_shape(slots, 8, PAD),
            wide_shape(PAD, width),
            low_shape(PAD, width),
        ],
        40,
    )


def dense_forward(lay, normed_two, middle, weights, bias, b_down):
    slots, width = lay.slots, lay.width
    size = weights[0].shape[3] // 2

    def kernel(step, weight, slotted, whole, late, rows, outs, total):
        active, active_sent, slope, result = outs
        matrix = weight(0)
        hidden = product(whole[0][...], matrix[:, :size], NN) + slotted[0][0]
        chance = 0.5 + 0.5 * lax.erf(hidden * (0.5**0.5))
        density = jnp.exp(-0.5 * hidden * hidden) * 0.3989422804014327
        low = (hidden * chance).astype(LOW)
        active[0] = low
        active_sent[0] = low
        slope[0] = (chance + hidden * density).astype(LOW)
        add_product(lay, step, total, low, matrix[:, size:])

        @pl.when(step == slots - 1)
        def _():
            (middle_ref,) = late()
            result[...] = (middle_ref[...] + total[...] + rows[0][...]).astype(LOW)

    return layer_call(
        lay,
        kernel,
        "dense_forward",
        [weights],
        [bias],
        [normed_two],
        [middle],
        [b_down],
        [
            low_shape(lay.shards + 1, PAD, size),
            low_shape(slots, PAD, size),
            low_shape(PAD, width),
        ],
        46,
    )


def dense_backward(lay, tangent, slope, middle, weights, gain_two):
    slots, width = lay.slots, lay.width
    size = weights[0].shape[3] // 2

    def kernel(step, weight, slotted, whole, late, rows, outs, total):
        grad_hidden, hidden_sent, up_sums, grad_middle, grad_branch = outs[:5]
        down_sums, gains, shifts, out_sums = outs[5:]

        @pl.when(step == 0)
        def _():
            down_sums[...] = jnp.sum(whole[0][...].astype(F32), axis=0, keepdims=True)
            for ref in (gains, shifts, out_sums):
                ref[...] = jnp.zeros_like(ref)

        matrix = weight(0)
        grad = product(whole[0][...], matrix[:, size:], NN).astype(LOW).astype(F32)
        grad = (grad * slotted[0][0].astype(F32)).astype(LOW)
        grad_hidden[0] = grad
        hidden_sent[0] = grad
        up_sums[0] = jnp.sum(grad.astype(F32), axis=0, keepdims=True)
        add_product(lay, step, total, grad, matrix[:, :size])

        @pl.when(step == slots - 1)
        def _():
            (middle,) = late()

            def finish(start, count):
                at = pl.ds(start, count)
                term, gain_part, shift_part = norm_back(middle[at, :], total[at, :], rows[0][...])
                sums = whole[0][at, :].astype(F32) + term
                grad_middle[at, :] = sums
                grad_branch[at, :] = sums.astype(LOW)
                gains[...] += gain_part
                shifts[...] += shift_part
                out_sums[...] += jnp.sum(sums, axis=0, keepdims=True)

            row_loop(finish)

    row = wide_shape(1, width)
    return layer_call(
        lay,
        kernel,
        "dense_backward",
        [weights],
        [slope],
        [tangent],
        [middle],
        [gain_two],
        [
            low_shape(lay.shards + 1, PAD, size),
            wide_shape(slots, 1, size),
            wide_shape(PAD, width),
            low_shape(PAD, width),
            row,
            row,
            row,
            row,
        ],
        48,
    )


def attention_backward(
    lay, grad_branch, mixed, attended, logs, entry, grad_middle, weights, gain_one
):
    slots, width = lay.slots, lay.width
    part = weights[0].shape[3] // 4

    def kernel(step, weight, slotted, whole, late, rows, outs, total):
        grad_mixed, mixed_sent, qkv_sums, grad_entry, gains, shifts = outs

        @pl.when(step == 0)
        def _():
            for ref in (gains, shifts):
                ref[...] = jnp.zeros_like(ref)

        matrix = weight(0)
        upstream = product(whole[0][...], matrix[:, 3 * part :], NN).astype(LOW)
        parts = attend_back(slotted[0][0], upstream, slotted[1][0], slotted[2][0], part)
        for spot, term in enumerate(parts):
            columns = slice(spot * part, (spot + 1) * part)
            rounded = term.astype(LOW)
            grad_mixed[0, :, columns] = rounded
            mixed_sent[0, :, columns] = rounded
            qkv_sums[0, :, columns] = jnp.sum(rounded.astype(F32), axis=0, keepdims=True)
        add_product(lay, step, total, grad_mixed[0], matrix[:, : 3 * part])

        @pl.when(step == slots - 1)
        def _():
            entry, grad_middle = late()

            def finish(start, count):
                at = pl.ds(start, count)
                term, gain_part, shift_part = norm_back(
                    entry[at, :].astype(F32), total[at, :], rows[0][...]
                )
                grad_entry[at, :] = (grad_middle[at, :] + term).astype(LOW)
                gains[...] += gain_part
                shifts[...] += shift_part

            row_loop(finish)

    row = wide_shape(1, width)
    return layer_call(
        lay,
        kernel,
        "attention_backward",
        [weights],
        [mixed, attended, logs],
        [grad_branch],
        [entry, grad_middle],
        [gain_one],
        [
            low_shape(lay.shards + 1, PAD, 3 * part),
            wide_shape(slots, 1, 3 * part),
            low_shape(PAD, width),
            row,
            row,
        ],
        48,
    )


def weight_grads(lay, slot_order, pairs, cost):
    half, block, shards, width = lay.near, lay.block, lay.shards, lay.width
    sizes = [pair[2].shape[2] for pair in pairs]
    total = sum(sizes)
    whole = pl.BlockSpec((PAD, width), lambda k, s: (0, 0), pipeline_mode=pl.Buffered(1))
    specs, operands, scratch = [], [], []
    for x, x_other, feats, feats_other in pairs:
        feature_spec = pl.BlockSpec((1, PAD, feats.shape[2]), lambda k, s: (k, 0, 0))
        specs += [whole, whole, feature_spec, feature_spec]
        operands += [x, x_other, feats, feats_other]

    def kernel(_, *refs):
        far_ref, near_ref = refs[4 * len(pairs) :]
        start = 0
        for n, size in enumerate(sizes):
            x, x_other, feats, feats_other = refs[4 * n : 4 * n + 4]
            for b in range(2 * half):
                mine = slice(b * block, (b + 1) * block)
                other = slice(lay.flip[b] * block, (lay.flip[b] + 1) * block)
                grads = product(x[:, mine], feats[0], TN)
                grads = (grads + product(x_other[:, other], feats_other[0], TN)).astype(LOW)
                ref = near_ref if b < half else far_ref
                ref[b % half, 0, :, start : start + size] = grads
            start += size

    return launch(
        lay,
        kernel,
        "weight_grads",
        [slot_order],
        operands,
        specs,
        [pl.BlockSpec((half, 1, block, total), lambda k, s: (0, s[k], 0, 0))] * 2,
        [low_shape(half, shards, block, total)] * 2,
        (shards,),
        scratch,
        28,
        cost,
    )


def add_blocks(lay, *groups, cost=10**10):
    count = min(array.shape[0] - start for group in groups for array, start in group)
    widths = [group[0][0].shape[3] for group in groups]
    middle = groups[0][0][0].shape[1:3]

    def kernel(*refs):
        at, column = 0, 0
        for group, width in zip(groups, widths):
            total = refs[at][...].astype(F32)
            for ref in refs[at + 1 : at + len(group)]:
                total = total + ref[...].astype(F32)
            refs[-1][..., column : column + width] = total.astype(LOW)
            at, column = at + len(group), column + width

    def spec(start, width):
        return pl.BlockSpec((1,) + middle + (width,), lambda i: (i + start, 0, 0, 0))

    return launch(
        lay,
        kernel,
        "add_blocks",
        [],
        [array for group in groups for array, _ in group],
        [spec(start, width) for group, width in zip(groups, widths) for _, start in group],
        [spec(0, sum(widths))],
        [jax.ShapeDtypeStruct((count,) + middle + (sum(widths),), LOW)],
        (count,),
        [],
        28,
        cost,
    )[0]


def pause(lay, cost=4 * 10**10):
    def kernel(out_ref):
        out_ref[...] = jnp.zeros_like(out_ref)

    spec = pl.BlockSpec((8, 128), lambda i: (0, 0))
    shape = jax.ShapeDtypeStruct((8, 128), F32)
    launch(lay, kernel, "pause", [], [], [], [spec], [shape], (1,), [], 8, cost)


def pack_vectors(lay, sums, blocks, slot_order, core):
    rep, block, shards = lay.replicas, lay.block, lay.shards
    assert rep == shards
    wide = sums[0][1].shape[2]
    operands = [v for layer in (0, 1) for v in (*sums[layer][0], *sums[layer][1:])]

    def kernel(s, *refs):
        keep_ref, send_ref = refs[16:]
        owner = s[rep + shards]
        keep_ref[...] = jnp.zeros_like(keep_ref)
        send_ref[...] = jnp.zeros_like(send_ref)
        here, there = refs[:8], refs[8:16]

        def chosen(n, index, mine):
            first = (owner == 0) if mine else (owner != 0)
            return jnp.where(first, here[n][index], there[n][index])

        for out_ref, mine in ((keep_ref, True), (send_ref, False)):
            for n in range(6):
                for b in range(rep):
                    columns = slice(b * block, (b + 1) * block)
                    value = chosen(n, (slice(None), columns), mine)
                    out_ref[s[b] ^ s[rep], n : n + 1, :block] = value
            for side in range(2):
                half = side ^ owner
                for k in range(shards):
                    slot = side * shards + k
                    ups = chosen(6, slot, mine)
                    parts = chosen(7, slot, mine)
                    out_ref[k, pl.ds(8 + half, 1), :] = ups
                    out_ref[k, pl.ds(6 + half, 1), : parts.shape[1]] = parts

    def spec(array):
        return pl.BlockSpec(array.shape, lambda i, s, n=array.ndim: (0,) * n)

    scalars = jnp.concatenate([blocks, slot_order, core[None]])
    shape = jax.ShapeDtypeStruct((shards, 16, wide), F32)
    keep, send = launch(
        lay,
        kernel,
        "pack_vectors",
        [scalars],
        operands,
        [spec(v) for v in operands],
        [pl.BlockSpec(shape.shape, lambda i, s: (0, 0, 0))] * 2,
        [shape] * 2,
        (1,),
        [],
        8,
    )
    return keep, send


def shards(
    boundary_in,
    counts,
    w_qkv,
    b_qkv,
    w_out,
    b_out,
    w_up,
    b_up,
    w_down,
    b_down,
    norm1_gain,
    norm1_shift,
    norm2_gain,
    norm2_shift,
):
    width = boundary_in.shape[4]
    sizes = {axis: lax.axis_size(axis) for axis in ALL_AXES}
    lay = Layout(sizes, width)
    core = lax.axis_index("section").astype(jnp.int32)
    shard = lax.axis_index("shard").astype(jnp.int32)
    replica = lax.axis_index("replica").astype(jnp.int32)
    on_first = core == 0
    heads_wide = w_qkv.shape[3]
    part = heads_wide // 2
    ff_part = w_up.shape[2] // 2
    positions = jnp.arange(lay.replicas, dtype=jnp.int32)
    flips = jnp.asarray(lay.flip, jnp.int32)
    blocks = jnp.where(on_first, positions, flips) ^ replica
    inverse_blocks = jnp.where(on_first, positions ^ replica, flips[positions ^ replica])
    halves = jnp.arange(2, dtype=jnp.int32) ^ core
    scalars = jnp.concatenate([blocks, halves, core[None]])

    slot_order = jnp.arange(lay.shards, dtype=jnp.int32) ^ shard

    raw_qkv = w_qkv[0].reshape(width, 6 * part)
    raw_out, raw_up, raw_down = w_out[0], w_up[0], w_down[0]
    split_pieces = first_pieces(lay, raw_qkv, raw_out, raw_up, raw_down, scalars)
    first, second = [], []
    for piece, sent in zip(split_pieces[:2], split_pieces[2:]):
        other = lay.across_cores(sent)
        first.append(jnp.where(on_first, piece, other))
        second.append(jnp.where(on_first, other, piece))
    pieces = first + second
    (pictures,) = lay.hold(boundary_in[0, :, 0])
    received = lay.across_cores(pictures)
    live = (shard < counts[replica, core]).astype(F32)[None]
    gather = Gather(lay, slot_order, pieces)
    gather.start(0)
    image, cot = arrange_images(lay, pictures, received, blocks, core, live)

    raws = (raw_qkv, raw_out, raw_up, raw_down)
    raws_other = [lay.across_cores(raw) for raw in raws]
    own_attention = arrange_attention(lay, raws[:2], raws_other[:2], scalars)

    packed = jnp.concatenate(
        [v[0] for v in (b_out, b_down, norm1_gain, norm1_shift, norm2_gain, norm2_shift)]
        + [b_qkv.reshape(-1), b_up.reshape(-1)]
    )
    packed_other = lay.across_cores(packed)
    both = jnp.stack(
        [jnp.where(on_first, packed, packed_other), jnp.where(on_first, packed_other, packed)]
    )
    wide = both[:, : 6 * width].reshape(2, 6, lay.replicas, lay.block)
    wide = jnp.take(wide, blocks, axis=2).reshape(2, 6, 1, width).astype(F32)
    split = both[:, 6 * width :]
    split = jnp.stack([split] + [lay.along_shard(split, k) for k in range(1, lay.shards)])
    split_qkv = split[:, :, : 4 * part].reshape(lay.shards, 2, 2, 2, part)
    split_qkv = jnp.take(split_qkv, halves, axis=3).transpose(1, 3, 0, 2, 4)
    split_qkv = split_qkv.reshape(2, lay.slots, 2, part)
    bias_qkv = jnp.concatenate(
        [split_qkv[:, :, 0], jnp.zeros_like(split_qkv[:, :, 0]), split_qkv[:, :, 1]], axis=-1
    ).reshape(2, lay.slots, 1, 3 * part).astype(F32)
    bias_up = split[:, :, 4 * part :].reshape(lay.shards, 2, 2, ff_part)
    bias_up = jnp.take(bias_up, halves, axis=2).transpose(1, 2, 0, 3)
    bias_up = bias_up.reshape(2, lay.slots, 1, ff_part).astype(F32)

    kept, weights = [], []
    entry = image
    gather.step(0)
    gather.start(1)
    gather.step(0)
    gather.start(2)
    gather.step(1)
    gather.start(3)
    w_attention = gather.finish(0, own_attention[0])
    for layer in range(2):
        vec_out, vec_down, gain_one, shift_one, gain_two, shift_two = wide[layer]
        normed, mixed, attended, logs, middle, normed_two = attention_forward(
            lay,
            entry,
            w_attention,
            bias_qkv[layer],
            (gain_one, shift_one, vec_out, gain_two, shift_two),
        )
        exchanged = [
            lay.across_cores(value) for value in (normed, normed_two, attended[lay.shards :])
        ]
        if layer == 0:
            gather.step(1)
            gather.step(2)
            lay.absorb(*exchanged)
            own_dense = arrange_dense(lay, raws[2:], raws_other[2:], scalars)
            gather.settle(2)
            gather.step(3)
            w_dense = gather.finish(1, own_dense[0])
            gather.step(2)
            gather.step(3)
            pause(lay)
        else:
            w_dense = gather.finish(3, own_dense[1])
            lay.absorb(kept[0][-1][-1])
            pause(lay)
        active, active_sent, slope, result = dense_forward(
            lay,
            normed_two,
            middle,
            w_dense,
            bias_up[layer],
            vec_down,
        )
        weights.append((w_attention, w_dense))
        exchanged.append(lay.across_cores(active_sent))
        if layer == 0:
            w_attention = gather.finish(2, own_attention[1])
            pause(lay)
        kept.append(
            (entry, normed, mixed, attended, logs, middle, normed_two, active, slope, exchanged)
        )
        entry = result

    terms, sums, vector_sums, latest = {}, {}, {}, {}

    def begin(name, *pairs, cost=1000):
        far, near = weight_grads(lay, slot_order, pairs, cost)
        arrived = lay.along_bit(far, lay.bits - 1)
        terms[name] = [(near, 0), (arrived, 0)]

    def halve(name, cost=10**10):
        for bit in range(lay.bits - 2, -1, -1):
            split = 1 << bit
            group = [(array, start + split) for array, start in terms[name]]
            sent = add_blocks(lay, group, cost=cost)
            terms[name] = terms[name] + [(lay.along_bit(sent, bit), 0)]

    def collect(names, direct, cost=10**10, beside=None):
        total = add_blocks(lay, *(terms[name] for name in names), cost=cost)[0]
        if beside is not None:
            total, beside = lax.optimization_barrier((total, beside))
        if direct:
            latest[names] = lax.all_to_all(total, "shard", 0, 0, tiled=True)
        else:
            latest[names] = lax.psum_scatter(total, "shard", scatter_dimension=0)[None]
        return beside

    def settle(*all_names):
        for names, total in zip(all_names, lay.hold(*(latest[names] for names in all_names))):
            spread(names, total)

    def spread(names, total):
        total = jnp.sum(total.astype(F32), axis=0)
        at = 0
        for name in names:
            size = terms[name][0][0].shape[3]
            sums[name] = total[:, at : at + size]
            at += size

    tangent = cot
    for layer in (1, 0):
        w_attention, w_dense = weights[layer]
        vec_out, vec_down, gain_one, shift_one, gain_two, shift_two = wide[layer]
        entry_in, normed, mixed, attended, logs, middle, normed_two, active, slope, other = kept[layer]
        normed_other, normed_two_other, attended_other, active_other = other
        if layer == 1:
            begin((1, "down"), (tangent, lay.across_cores(tangent), active, active_other))
        (
            grad_hidden,
            hidden_sent,
            up_sums,
            grad_middle,
            grad_branch,
            down_sums,
            gain_two_sum,
            shift_two_sum,
            out_sums,
        ) = dense_backward(lay, tangent, slope, middle, w_dense, gain_two)
        branch_other, hidden_other = lay.across_cores(grad_branch), lay.across_cores(hidden_sent)
        out_pair = (grad_branch, branch_other, attended, attended_other)
        if layer == 1:
            halve((1, "down"))
        else:
            settle(((1, "down"),))
            collect(((1, "out"), (1, "up")), False)
            halve((0, "down"))
        begin((layer, "out"), out_pair, cost=4 * 10**10)
        if layer == 0:
            halve((1, "qkv"))
        begin((layer, "up"), (normed_two, normed_two_other, grad_hidden, hidden_other))
        if layer == 0:
            collect(((1, "qkv"), (0, "down")), True)
        grad_mixed, mixed_sent, qkv_sums, grad_entry, gain_one_sum, shift_one_sum = (
            attention_backward(
                lay,
                grad_branch,
                mixed,
                attended,
                logs,
                entry_in,
                grad_middle,
                w_attention,
                gain_one,
            )
        )
        tangent = grad_entry
        if layer == 1:
            mixed_other = lay.across_cores(mixed_sent)
        vector_sums[layer] = (
            [out_sums, down_sums, gain_one_sum, shift_one_sum, gain_two_sum, shift_two_sum],
            up_sums,
            qkv_sums,
        )
        if layer == 1:
            collect(((1, "down"),), False)
        if layer == 0:
            keep, send = pack_vectors(lay, vector_sums, blocks, slot_order, core)
            send = lay.across_cores(send)
        halve((layer, "out"))
        if layer == 0:
            (send,) = lay.hold(send)
            summed = keep + send
        if layer == 0:
            (mixed_sent,) = lay.hold(mixed_sent)
            mixed_other = lay.across_cores(mixed_sent)
        halve((layer, "up"))
        if layer == 1:
            active, active_other = kept[0][7], kept[0][9][3]
            begin((0, "down"), (tangent, lay.across_cores(tangent), active, active_other))
        begin((layer, "qkv"), (normed, normed_other, grad_mixed, mixed_other))
    (summed,) = lay.hold(summed)
    coming = lay.along_bit_plain(summed, 0)
    settle(((1, "out"), (1, "up")))
    back = restore_image(lay, tangent, blocks, jnp.ones((1,), F32))
    ahead = restore_image(lay, entry, blocks, live)
    (coming,) = lay.hold(coming)
    for bit in range(1, lay.bits):
        summed = summed + coming
        coming = lay.along_bit_plain(summed, bit)
    collect(((0, "out"), (0, "up")), False, cost=2 * 10**10)
    halve((0, "qkv"), cost=1000)
    settle(((1, "qkv"), (0, "down")))
    back, ahead, coming = lay.hold(back, ahead, coming)
    summed = summed + coming
    coming = [lay.along_shard(summed[k], k) for k in range(1, lay.shards)]
    coming = collect(((0, "qkv"),), True, cost=1000, beside=coming)
    summed = sum(coming, summed[0])
    last = (((0, "out"), (0, "up")), ((0, "qkv"),))
    for names, total in zip(last, lax.optimization_barrier([latest[names] for names in last])):
        spread(names, total)

    def to_owner(first, second):
        keep = jnp.where(on_first, first, second)
        other = lay.across_cores(jnp.where(on_first, second, first))
        return jnp.where(on_first, keep, other), jnp.where(on_first, other, keep)

    down_halves = to_owner(sums[0, "down"], sums[1, "down"])
    up_halves = to_owner(sums[0, "up"], sums[1, "up"])
    out_halves = to_owner(sums[0, "out"], sums[1, "out"])
    qkv_halves = to_owner(sums[0, "qkv"], sums[1, "qkv"])
    grad_w_down = jnp.concatenate(down_halves, axis=1).T[None]
    grad_w_up = jnp.concatenate(up_halves, axis=1)[None]
    grad_w_qkv = jnp.stack(
        [half.reshape(-1, 3, part) for half in qkv_halves], axis=2
    ).reshape(1, lay.block, 3, heads_wide)
    grad_w_out = jnp.concatenate(out_halves, axis=1).T[None]

    share = lay.block // lay.replicas
    model = lax.dynamic_slice_in_dim(summed[:6, : lay.block], replica * share, share, 1)
    vectors = [model[i : i + 1] for i in range(6)]
    parts = summed[6:8, : 3 * part].reshape(2, 3, part)
    parts = jnp.stack([parts[:, 0], parts[:, 2]]).reshape(2, 2 * part)
    grad_b_qkv = lax.dynamic_slice_in_dim(parts, replica * share, share, 1)[None]
    share_up = 2 * ff_part // lay.replicas
    ups = summed[8:10, :ff_part].reshape(1, 2 * ff_part)
    grad_b_up = lax.dynamic_slice_in_dim(ups, replica * share_up, share_up, 1)

    keep = jnp.where(on_first, back, ahead)
    other = lay.across_cores(jnp.where(on_first, ahead, back))
    boundary_out = jnp.stack([jnp.where(on_first, keep, other), jnp.where(on_first, other, keep)])
    boundary_out = boundary_out[None, :, None]
    return (
        boundary_out,
        grad_w_qkv,
        grad_b_qkv,
        grad_w_out,
        vectors[0],
        grad_w_up,
        grad_b_up,
        grad_w_down,
        vectors[1],
        vectors[2],
        vectors[3],
        vectors[4],
        vectors[5],
    )


def solution(mesh):
    spread = P("section", ("shard", "replica"))
    return jax.shard_map(
        shards,
        mesh=mesh,
        in_specs=(
            P("section", None, ("shard", "replica"), None, None),
            P(),
            P("section", None, None, "shard"),
            P("section", None, "shard"),
            P("section", "shard", None),
            P("section", None),
            P("section", None, "shard"),
            P("section", "shard"),
            P("section", "shard", None),
            P("section", None),
            P("section", None),
            P("section", None),
            P("section", None),
            P("section", None),
        ),
        out_specs=(
            P("section", None, ("shard", "replica"), None, None),
            P("section", "replica", None, "shard"),
            P("section", None, ("shard", "replica")),
            P("section", "shard", "replica"),
            spread,
            P("section", "replica", "shard"),
            spread,
            P("section", "shard", "replica"),
            spread,
            spread,
            spread,
            spread,
            spread,
        ),
        check_vma=False,
    )
```
